32 devices in a mesh: rows: 4 (over y, x), tp: 8 (over z, core).
Axes of the slice: x: 2, y: 2, z: 4, core: 2. Of those that a mesh axis runs over, the one named last changes fastest.
Arguments:
- block_input: bfloat16 [4096, 2048], P(('rows', 'tp')), may hold values from -6 to 6
- norm_gain: bfloat16 [2048], replicated, may hold values from 0.5 to 1.5
- norm_bias: bfloat16 [2048], replicated, may hold values from -1.5 to 1.5
- qkv_weight: bfloat16 [3, 2048, 2048], P(None, 'tp'), may hold values from -0.125 to 0.125
- qkv_bias: bfloat16 [3, 2048], P(None, 'tp'), may hold values from -1 to 1
- out_weight: bfloat16 [2048, 2048], P('tp'), may hold values from -0.75 to 0.75
- gate_weight: bfloat16 [5632, 2048], P('tp'), may hold values from -0.125 to 0.125
- up_weight: bfloat16 [5632, 2048], P('tp'), may hold values from -0.125 to 0.125
- down_weight: bfloat16 [5632, 2048], P('tp'), may hold values from -0.078125 to 0.078125
- cotangent: bfloat16 [4096, 2048], P(('rows', 'tp')), may hold values from -6 to 6
- doc_lengths: int32 [4, 8], P('rows'), may hold values from 1 to 512, 1024 in all within a row
Outputs:
- output: bfloat16 [4096, 2048], P(('rows', 'tp'))
- input_grad: float32 [4096, 2048], P(('rows', 'tp'))
- gain_grad: float32 [2048], replicated
- bias_grad: float32 [2048], replicated
- qkv_grad: float32 [3, 2048, 2048], P(None, 'tp')
- qkv_bias_grad: float32 [3, 2048], P(None, 'tp')
- out_grad: float32 [2048, 2048], P('tp')
- gate_grad: float32 [5632, 2048], P('tp')
- up_grad: float32 [5632, 2048], P('tp')
- down_grad: float32 [5632, 2048], P('tp')
The draws below stay inside these ranges and needn't reach their ends.
Inputs may be any that keep to these rules, and one draw needn't show every extreme that they name: `doc_lengths`: each row holds the lengths of the 8 consecutive pieces of one packed row in order, summing to 1024; the last piece is padding; in every row the longest piece has exactly 512 tokens.
All inputs are finite; a program needn't handle non-finite values.
Results may differ from the reference program's by a relative error of at most 0.0099.
Values may be sent and summed in bfloat16 or wider, within the bound.
No kernel may reach another device: no remote copies, remote signals or barrier semaphores. Data moves between devices by JAX's collectives and lax.ppermute only.
A program may use at most 192 MiB of HBM per device.

```python
import math
import jax
import jax.numpy as jnp
import numpy as np
from jax import lax

D = 2048
HEADS = 32
HEAD = 64
ROT = 16
FF = 5632
DOCS = 8
ROW_LEN = 1024
DOC_MOST = 512
TOKENS = 4096
PACK_ROWS = 4


def levels(stream_key, dims, pieces, smallest, largest):
    loudness, own = 1.0, jax.random.fold_in(stream_key, 6)
    for dim, shards_of in pieces:
        steps = jnp.exp(jax.random.uniform(jax.random.fold_in(own, dim), (shards_of,), jnp.float32, smallest / len(pieces), largest / len(pieces)))
        loudness = loudness * jnp.repeat(steps, dims[dim] // shards_of).reshape([-1 if axis == dim else 1 for axis in range(len(dims))])
    return loudness


def profile(amount, total, most, lean):
    weights = [(1 << 20) // math.isqrt(grade ** lean) + 1 for grade in range(2, amount + 1)]
    spare, given = total - most - (amount - 1), [1] * (amount - 1)
    while spare > 0:
        candidates = [i for i in range(amount - 1) if given[i] < most]
        pool, budget = sum([weights[i] for i in candidates]), spare
        for i in candidates:
            addition = min(most - given[i], max(1, budget * weights[i] // pool), spare)
            given[i] = given[i] + addition
            spare = spare - addition
    return np.array([most] + given)


def ragged_sizes(own_key, count, total, bound, skew):
    if count == 2:
        one = jax.random.randint(own_key, (), max(1, total - bound), min(bound, total - 1) + 1)
        return jnp.stack([one, total - one])
    sizes = jnp.asarray(profile(count, total, bound, skew), jnp.int32)
    pairs = (count - 1) // 2
    donor, sink = sizes[1:1 + 2 * pairs:2], sizes[2:2 + 2 * pairs:2]
    room = jnp.minimum(donor - 1, bound - sink)
    moved = jax.random.randint(jax.random.fold_in(own_key, 1), (pairs,), 0, 1 << 20) % (room + 1)
    sizes = sizes.at[1:1 + 2 * pairs:2].set(donor - moved).at[2:2 + 2 * pairs:2].set(sink + moved)
    return sizes[jax.random.permutation(jax.random.fold_in(own_key, 2), count)]


def bell_draw(stream_key, extent, width, most, pieces=(), kind=jnp.bfloat16):
    drawn = jax.random.normal(stream_key, extent, jnp.float32) * width
    if len(pieces) > 0:
        drawn = levels(stream_key, extent, pieces, -0.22, 0.18) * drawn
    return jnp.clip(drawn, min=-most, max=most).astype(kind)


def setup_inputs(seed: int = 0) -> dict:
    key_list = jax.random.split(jax.random.key(seed), 12)
    block_input = bell_draw(key_list[0], (TOKENS, D), 1.0, 6.0, ((0, 32),))
    norm_gain = jnp.clip(1.0 + 0.1 * jax.random.normal(key_list[1], (D,), jnp.float32), 0.5, 1.5).astype(jnp.bfloat16)
    norm_bias = bell_draw(key_list[2], (D,), 0.3, 1.5)
    qkv_weight = bell_draw(key_list[3], (3, D, D), D ** -0.5, 0.125, ((1, 8),))
    qkv_bias = bell_draw(key_list[4], (3, D), 0.2, 1.0, ((1, 8),))
    out_weight = bell_draw(key_list[5], (D, D), 64 ** -0.5, 0.75, ((0, 8),))
    gate_weight = bell_draw(key_list[6], (FF, D), D ** -0.5, 0.125, ((0, 8),))
    up_weight = bell_draw(key_list[7], (FF, D), D ** -0.5, 0.125, ((0, 8),))
    down_weight = bell_draw(key_list[8], (FF, D), FF ** -0.5, 0.078125, ((0, 8),))
    cotangent = bell_draw(key_list[9], (TOKENS, D), 1.0, 6.0, ((0, 32),))
    doc_lengths = jax.vmap(lambda own: ragged_sizes(own, DOCS, ROW_LEN, DOC_MOST, 2))(jax.random.split(key_list[10], PACK_ROWS)).reshape((PACK_ROWS, DOCS)).astype(jnp.int32)
    return {"block_input": block_input, "norm_gain": norm_gain, "norm_bias": norm_bias, "qkv_weight": qkv_weight, "qkv_bias": qkv_bias, "out_weight": out_weight, "gate_weight": gate_weight, "up_weight": up_weight, "down_weight": down_weight, "cotangent": cotangent, "doc_lengths": doc_lengths}


EPSILON = 1e-05
HIGH = lax.Precision.HIGHEST

@jax.custom_vjp
def low(v):
    return lax.optimization_barrier(v.astype(jnp.bfloat16)).astype(jnp.float32)

@jax.custom_vjp
def low_back(v):
    return v

def low_keep(v):
    return (low(v), None)

def low_pass(kept, grad):
    return (grad,)

def back_keep(v):
    return (v, None)

def back_low(kept, grad):
    return (low(grad),)
low.defvjp(low_keep, low_pass)
low_back.defvjp(back_keep, back_low)

def layout(doc_lengths):
    lengths = doc_lengths.astype(jnp.int32)
    ends = jnp.cumsum(lengths, axis=1).astype(jnp.int32)
    starts = (ends - lengths).astype(jnp.int32)
    places = jnp.arange(ROW_LEN, dtype=jnp.int32)
    segment = lax.optimization_barrier(jnp.sum((places[None, :, None] >= ends[:, None, :]).astype(jnp.int32), axis=2)).astype(jnp.int32)
    chosen = segment[:, :, None] == jnp.arange(DOCS, dtype=jnp.int32)[None, None, :]
    first = lax.optimization_barrier(jnp.sum(jnp.where(chosen, starts[:, None, :], 0), axis=2)).astype(jnp.int32)
    position = (places[None, :] - first).astype(jnp.int32)
    live = segment < DOCS - 1
    return (segment, position, live)

def rotate(values, position):
    half = ROT // 2
    freq = 10000.0 ** (-(jnp.arange(half).astype(jnp.float32) * (2.0 / ROT)))
    angle = position.astype(jnp.float32)[..., None] * freq
    cosine = jnp.cos(angle)[..., None, :]
    sine = jnp.sin(angle)[..., None, :]
    first = values[..., :half]
    second = values[..., half:ROT]
    return jnp.concatenate([first * cosine - second * sine, second * cosine + first * sine, values[..., ROT:]], axis=-1)

def attend_item(item):
    query, key, value, segment = item
    scores = low_back(jnp.dot(query, key.T, precision=HIGH) * HEAD ** (-0.5))
    places = jnp.arange(ROW_LEN)
    allowed = (segment[:, None] == segment[None, :]) & (places[None, :] <= places[:, None])
    weights = jax.nn.softmax(jnp.where(allowed, scores, -1e+30), axis=1)
    return jnp.dot(low(weights), value, precision=HIGH)

def forward(block_input, norm_gain, norm_bias, qkv_weight, qkv_bias, out_weight, gate_weight, up_weight, down_weight, segment, position, live):
    packed = segment.shape[0]
    centre = lax.optimization_barrier(jnp.mean(block_input, axis=1, keepdims=True))
    centred = block_input - centre
    spread = lax.optimization_barrier(jnp.mean(centred * centred, axis=1, keepdims=True))
    normed = centred * lax.rsqrt(spread + EPSILON)
    hidden_in = low(normed * norm_gain + norm_bias)
    lines = jnp.einsum('td,jed->jte', hidden_in, qkv_weight, precision=HIGH) + qkv_bias[:, None, :]
    shape = (packed, ROW_LEN, HEADS, HEAD)
    query = low(rotate(low_back(lines[0]).reshape(shape), position))
    key = low(rotate(low_back(lines[1]).reshape(shape), position))
    value = low(low_back(lines[2])).reshape(shape)

    def heads_first(values):
        return values.transpose(0, 2, 1, 3).reshape(packed * HEADS, ROW_LEN, HEAD)
    segment_items = jnp.repeat(segment, HEADS, axis=0)
    context = lax.map(jax.checkpoint(attend_item), (heads_first(query), heads_first(key), heads_first(value), segment_items))
    context = context.reshape(packed, HEADS, ROW_LEN, HEAD).transpose(0, 2, 1, 3).reshape(packed * ROW_LEN, HEADS * HEAD)
    context = low(low_back(context))
    gate = low_back(jnp.einsum('td,fd->tf', hidden_in, gate_weight, precision=HIGH))
    up = low_back(jnp.einsum('td,fd->tf', hidden_in, up_weight, precision=HIGH))
    mixed = low(jax.nn.silu(gate) * up)
    merged = jnp.dot(context, out_weight, precision=HIGH) + jnp.dot(mixed, down_weight, precision=HIGH)
    return block_input + live.reshape(-1, 1).astype(jnp.float32) * merged

def reference(block_input, norm_gain, norm_bias, qkv_weight, qkv_bias, out_weight, gate_weight, up_weight, down_weight, cotangent, doc_lengths):
    segment, position, live = layout(doc_lengths)
    params = tuple((a.astype(jnp.float32) for a in (block_input, norm_gain, norm_bias, qkv_weight, qkv_bias, out_weight, gate_weight, up_weight, down_weight)))

    def apply(*values):
        return forward(*values, segment, position, live)
    output, pull = jax.vjp(apply, *params)
    grads = pull(cotangent.astype(jnp.float32))
    return (output.astype(jnp.bfloat16), grads[0], grads[1], grads[2], grads[3], grads[4], grads[5], grads[6], grads[7], grads[8])
```

```python
import jax
import jax.numpy as jnp
from jax import lax
from jax.sharding import PartitionSpec as P

HEAD = 64
ROT = 16
DOCS = 8


EPSILON = 1e-05
MASKED = -1e30


def layout(doc_lengths, row_len):
    ends = jnp.cumsum(doc_lengths, axis=1)
    starts = ends - doc_lengths
    places = jnp.arange(row_len, dtype=jnp.int32)
    segment = jnp.sum((places[None, :, None] >= ends[:, None, :]).astype(jnp.int32), axis=2)
    chosen = segment[:, :, None] == jnp.arange(DOCS, dtype=jnp.int32)[None, None, :]
    first = jnp.sum(jnp.where(chosen, starts[:, None, :], 0), axis=2)
    position = places[None, :] - first
    live = segment < DOCS - 1
    return (segment, position, live)


def angles(position):
    half = ROT // 2
    freq = 10000.0 ** (-(jnp.arange(half).astype(jnp.float32) * (2.0 / ROT)))
    angle = position.astype(jnp.float32)[..., None] * freq
    return (jnp.cos(angle)[..., None, :], jnp.sin(angle)[..., None, :])


def rotate(values, position):
    half = ROT // 2
    cosine, sine = angles(position)
    first = values[..., :half]
    second = values[..., half:ROT]
    return jnp.concatenate(
        [first * cosine - second * sine, second * cosine + first * sine, values[..., ROT:]], axis=-1
    )


def unrotate(grads, position):
    half = ROT // 2
    cosine, sine = angles(position)
    first = grads[..., :half]
    second = grads[..., half:ROT]
    return jnp.concatenate(
        [first * cosine + second * sine, second * cosine - first * sine, grads[..., ROT:]], axis=-1
    )


def standardize(values):
    centre = jnp.mean(values, axis=1, keepdims=True)
    centred = values - centre
    spread = jnp.mean(centred * centred, axis=1, keepdims=True)
    inverse = lax.rsqrt(spread + EPSILON)
    return (centred * inverse, inverse)


def project(hidden_in, qkv_weight, qkv_bias, gate_weight, up_weight, position):
    packs = position.shape[0]
    row_len = position.shape[1]
    heads = qkv_weight.shape[1] // HEAD
    lines = jnp.einsum("td,jed->jte", hidden_in, qkv_weight, preferred_element_type=jnp.float32)
    lines = lines + qkv_bias.astype(jnp.float32)[:, None, :]
    shape = (packs, row_len, heads, HEAD)
    query = rotate(lines[0].reshape(shape), position).astype(jnp.bfloat16)
    key = rotate(lines[1].reshape(shape), position).astype(jnp.bfloat16)
    value = lines[2].reshape(shape).astype(jnp.bfloat16)
    gate = jnp.einsum("td,fd->tf", hidden_in, gate_weight, preferred_element_type=jnp.float32)
    up = jnp.einsum("td,fd->tf", hidden_in, up_weight, preferred_element_type=jnp.float32)
    return (query, key, value, gate, up)


def block_allowed(segment, start, size):
    places = jnp.arange(segment.shape[0], dtype=jnp.int32)
    rows_here = start + jnp.arange(size, dtype=jnp.int32)
    segment_rows = lax.dynamic_slice_in_dim(segment, start, size)
    return (segment_rows[:, None] == segment[None, :]) & (places[None, :] <= rows_here[:, None])


def attend_forward(query, key, value, segment):
    length = query.shape[0]
    size = min(512, length)
    scale = HEAD ** (-0.5)

    def one_block(index):
        start = index * size
        block = lax.dynamic_slice_in_dim(query, start, size)
        scores = jnp.einsum("qhd,khd->hqk", block, key, preferred_element_type=jnp.float32) * scale
        scores = jnp.where(block_allowed(segment, start, size)[None], scores, MASKED)
        highest = jnp.max(scores, axis=2, keepdims=True)
        raised = jnp.exp(scores - highest)
        total = jnp.sum(raised, axis=2, keepdims=True)
        weights = (raised / total).astype(jnp.bfloat16)
        context = jnp.einsum("hqk,khd->qhd", weights, value, preferred_element_type=jnp.float32)
        return (context.astype(jnp.bfloat16), (highest + jnp.log(total))[:, :, 0])

    context, logsum = lax.map(one_block, jnp.arange(length // size, dtype=jnp.int32))
    return (context.reshape(length, -1), logsum)


def attend_backward(query, key, value, segment, context_grad, logsum):
    length = query.shape[0]
    size = min(512, length)
    scale = HEAD ** (-0.5)

    def one_block(carry, index):
        key_grad, value_grad = carry
        start = index * size
        block = lax.dynamic_slice_in_dim(query, start, size)
        block_grad = lax.dynamic_slice_in_dim(context_grad, start, size)
        scores = jnp.einsum("qhd,khd->hqk", block, key, preferred_element_type=jnp.float32) * scale
        allowed = block_allowed(segment, start, size)[None]
        probs = jnp.where(allowed, jnp.exp(scores - logsum[index][:, :, None]), 0.0)
        value_grad = value_grad + jnp.einsum(
            "hqk,qhd->khd",
            probs.astype(jnp.bfloat16),
            block_grad,
            preferred_element_type=jnp.float32,
        )
        prob_grad = jnp.einsum(
            "qhd,khd->hqk", block_grad, value, preferred_element_type=jnp.float32
        )
        inner = jnp.sum(probs * prob_grad, axis=2, keepdims=True)
        score_low = (probs * (prob_grad - inner)).astype(jnp.bfloat16)
        query_grad = (
            jnp.einsum("hqk,khd->qhd", score_low, key, preferred_element_type=jnp.float32) * scale
        )
        key_grad = (
            key_grad
            + jnp.einsum("hqk,qhd->khd", score_low, block, preferred_element_type=jnp.float32)
            * scale
        )
        return ((key_grad, value_grad), query_grad)

    zeros = jnp.zeros(key.shape, jnp.float32)
    (key_grad, value_grad), query_grad = lax.scan(
        one_block, (zeros, zeros), jnp.arange(length // size, dtype=jnp.int32)
    )
    return (query_grad.reshape(key.shape), key_grad, value_grad)


def over_rows(partial, earlier=None):
    partial = partial.astype(jnp.bfloat16)
    if earlier is not None:
        partial, _ = lax.optimization_barrier((partial, earlier))
    return lax.psum(partial, "rows")


def per_device(
    block_input,
    norm_gain,
    norm_bias,
    qkv_weight,
    qkv_bias,
    out_weight,
    gate_weight,
    up_weight,
    down_weight,
    cotangent,
    doc_lengths,
):
    shard = block_input.shape[0]
    tokens = shard * lax.axis_size("tp")
    width = qkv_weight.shape[1]
    heads = width // HEAD
    packs = doc_lengths.shape[0]
    row_len = tokens // packs
    segment, position, live = layout(doc_lengths, row_len)
    live_all = live.reshape(tokens)
    live_mine = lax.dynamic_slice_in_dim(live_all, lax.axis_index("tp") * shard, shard).astype(
        jnp.float32
    )
    input_wide = block_input.astype(jnp.float32)
    gain = norm_gain.astype(jnp.float32)
    shift = norm_bias.astype(jnp.float32)
    normed, inverse = standardize(input_wide)
    normed_low = (normed * gain + shift).astype(jnp.bfloat16)
    hidden_in = lax.all_gather(normed_low, "tp", axis=0, tiled=True)
    query, key, value, gate, up = project(
        hidden_in, qkv_weight, qkv_bias, gate_weight, up_weight, position
    )
    mixed = (jax.nn.silu(gate) * up).astype(jnp.bfloat16)
    pack = 0
    grad_all = lax.all_gather(cotangent, "tp", axis=0, tiled=True)
    grad_low = grad_all * live_all.astype(jnp.bfloat16)[:, None]
    down_sum = over_rows(jnp.dot(mixed.T, grad_low, preferred_element_type=jnp.float32))
    context_part, logsum = attend_forward(query[pack], key[pack], value[pack], segment[pack])
    out_sum = over_rows(
        jnp.dot(context_part.T, grad_low, preferred_element_type=jnp.float32), down_sum
    )
    merged = lax.psum_scatter(
        (
            jnp.dot(context_part, out_weight, preferred_element_type=jnp.float32)
            + jnp.dot(mixed, down_weight, preferred_element_type=jnp.float32)
        ).astype(jnp.bfloat16),
        "tp",
        scatter_dimension=0,
        tiled=True,
    ).astype(jnp.float32)
    output = (input_wide + live_mine[:, None] * merged).astype(jnp.bfloat16)
    mixed_grad = jnp.dot(grad_low, down_weight.T, preferred_element_type=jnp.float32)
    sigmoid = jax.nn.sigmoid(gate)
    gate_low = (mixed_grad * up * sigmoid * (1.0 + gate * (1.0 - sigmoid))).astype(jnp.bfloat16)
    up_low = (mixed_grad * gate * sigmoid).astype(jnp.bfloat16)
    gate_sum = over_rows(
        jnp.einsum("tf,td->fd", gate_low, hidden_in, preferred_element_type=jnp.float32), out_sum
    )
    up_sum = over_rows(
        jnp.einsum("tf,td->fd", up_low, hidden_in, preferred_element_type=jnp.float32), gate_sum
    )
    context_grad = jnp.dot(grad_low, out_weight.T, preferred_element_type=jnp.float32).astype(
        jnp.bfloat16
    )
    context_grad = context_grad.reshape(packs, row_len, heads, HEAD)
    query_part, key_part, value_part = attend_backward(
        query[pack], key[pack], value[pack], segment[pack], context_grad[pack], logsum
    )
    query_grad = unrotate(query_part[None], position).reshape(tokens, width)
    key_grad = unrotate(key_part[None], position).reshape(tokens, width)
    value_grad = value_part.reshape(tokens, width)
    lines_low = jnp.stack([query_grad, key_grad, value_grad]).astype(jnp.bfloat16)
    qkv_sum = over_rows(
        jnp.einsum("jte,td->jed", lines_low, hidden_in, preferred_element_type=jnp.float32), up_sum
    )
    qkv_bias_grad = lax.psum(jnp.sum(lines_low, axis=1, dtype=jnp.float32), "rows")
    term = jnp.einsum("jte,jed->td", lines_low, qkv_weight, preferred_element_type=jnp.float32)
    term = term + jnp.dot(gate_low, gate_weight, preferred_element_type=jnp.float32)
    normed_grad = lax.psum_scatter(
        (term + jnp.dot(up_low, up_weight, preferred_element_type=jnp.float32)).astype(
            jnp.bfloat16
        ),
        "tp",
        scatter_dimension=0,
        tiled=True,
    ).astype(jnp.float32)
    scaled = normed_grad * gain
    input_grad = inverse * (
        scaled
        - jnp.mean(scaled, axis=1, keepdims=True)
        - normed * jnp.mean(scaled * normed, axis=1, keepdims=True)
    )
    input_grad = input_grad + cotangent.astype(jnp.float32)
    gain_grad, bias_grad = lax.psum(
        (jnp.sum(normed_grad * normed, axis=0), jnp.sum(normed_grad, axis=0)), ("rows", "tp")
    )
    return (
        output,
        input_grad,
        gain_grad,
        bias_grad,
        qkv_sum.astype(jnp.float32),
        qkv_bias_grad,
        out_sum.astype(jnp.float32),
        gate_sum.astype(jnp.float32),
        up_sum.astype(jnp.float32),
        down_sum.astype(jnp.float32),
    )


def solution(mesh):
    placed = (
        P(("rows", "tp"), None),
        P(),
        P(),
        P(None, "tp", None),
        P(None, "tp"),
        P("tp", None),
        P("tp", None),
        P("tp", None),
        P("tp", None),
        P(("rows", "tp"), None),
        P("rows", None),
    )
    return jax.shard_map(
        per_device,
        mesh=mesh,
        in_specs=placed,
        out_specs=(
            P(("rows", "tp"), None),
            P(("rows", "tp"), None),
            P(),
            P(),
            P(None, "tp", None),
            P(None, "tp"),
            P("tp", None),
            P("tp", None),
            P("tp", None),
            P("tp", None),
        ),
        check_vma=False,
    )
```

```python
import functools
import jax
import jax.numpy as jnp
from jax import lax
from jax.experimental import pallas as pl
from jax.experimental.pallas import tpu as pltpu
from jax.sharding import PartitionSpec as P

HEAD = 64
ROT = 16
MASKED = -1e30
EPSILON = 1e-05
VMEM = 60 * 1024 * 1024


def dot_rows(a, b):
    return lax.dot_general(a, b, (((1,), (0,)), ((), ())), preferred_element_type=jnp.float32)


def dot_lanes(a, b):
    return lax.dot_general(a, b, (((1,), (1,)), ((), ())), preferred_element_type=jnp.float32)


def dot_tall(a, b):
    return lax.dot_general(a, b, (((0,), (0,)), ((), ())), preferred_element_type=jnp.float32)


def turn(values, tables, sign):
    half = ROT // 2
    width = values.shape[1]
    up = pltpu.roll(values, width - half, 1)
    down = pltpu.roll(values, half, 1)
    return values * tables[0] + sign * (up * tables[1] + down * tables[2])


def of_head(head, shape):
    return lax.broadcasted_iota(jnp.int32, shape, 1) // HEAD == head


def over_blocks(row_len, block, body):
    longest = row_len // 2
    blocks = row_len // block
    if blocks <= 8:
        for index in range(blocks):
            first = index * block
            start = max(0, first + block - (longest + block))
            body(first, start, first + block - start)
    else:
        size = longest + block

        def step(index, carry):
            first = pl.multiple_of(index * block, block)
            start = pl.multiple_of(jnp.maximum(first - longest, 0), block)
            body(first, start, size)
            return carry

        lax.fori_loop(0, blocks, step, 0)


def mask_of(seg_col, seg_row, first, start, block, size):
    rows = first + lax.broadcasted_iota(jnp.int32, (block, size), 0)
    keys = start + lax.broadcasted_iota(jnp.int32, (block, size), 1)
    same = seg_col[pl.ds(first, block), 0:1] == seg_row[0:1, pl.ds(start, size)]
    return jnp.where(same & (keys <= rows), 0.0, MASKED)


def forward_kernel(
    heads, lines, tables, seg_col, seg_row, query, key, value, context, context_t, logsum
):
    row_len, width = query.shape
    block = 256
    scale = HEAD ** (-0.5)
    query[...] = (turn(lines[:, 0:width], tables, 1.0).astype(jnp.bfloat16)) * jnp.bfloat16(scale)
    key[...] = turn(lines[:, width : 2 * width], tables, 1.0).astype(jnp.bfloat16)
    value[...] = lines[:, 2 * width : 3 * width].astype(jnp.bfloat16)

    def one_block(first, start, size):
        bias = mask_of(seg_col, seg_row, first, start, block, size)
        here = query[pl.ds(first, block), :]
        keys = key[pl.ds(start, size), :]
        values = value[pl.ds(start, size), :]
        total = jnp.zeros((block, width), jnp.float32)
        lane = lax.broadcasted_iota(jnp.int32, (block, 128), 1)
        sums = jnp.zeros((block, 128), jnp.float32)
        for head in range(heads):
            mine = of_head(head, (block, width))
            scores = dot_lanes(jnp.where(mine, here, jnp.bfloat16(0)), keys) + bias
            highest = jnp.max(scores, axis=1, keepdims=True)
            raised = jnp.exp(scores - highest)
            amount = jnp.sum(raised, axis=1, keepdims=True)
            weights = (raised * (1.0 / amount)).astype(jnp.bfloat16)
            total = jnp.where(mine, dot_rows(weights, values), total)
            sums = jnp.where(lane == head, highest + jnp.log(amount), sums)
        context[pl.ds(first, block), :] = total.astype(jnp.bfloat16)
        context_t[:, pl.ds(first, block)] = total.T.astype(jnp.bfloat16)
        logsum[pl.ds(first, block), :] = sums

    over_blocks(row_len, block, one_block)


def attend_forward(lines, tables, seg_col, seg_row, heads):
    row_len, width = lines.shape[0], lines.shape[1] // 3
    low = jax.ShapeDtypeStruct((row_len, width), jnp.bfloat16)
    return pl.pallas_call(
        functools.partial(forward_kernel, heads),
        out_shape=(
            low,
            low,
            low,
            low,
            jax.ShapeDtypeStruct((width, row_len), jnp.bfloat16),
            jax.ShapeDtypeStruct((row_len, 128), jnp.float32),
        ),
        compiler_params=pltpu.CompilerParams(vmem_limit_bytes=VMEM),
        cost_estimate=cost(
            heads * row_len * row_len * 256 * 2, 30 * row_len * width, heads * row_len * row_len // 2
        ),
        name="attend_forward",
    )(lines, tables, seg_col, seg_row)


def backward_kernel(
    heads,
    query,
    key,
    value,
    context_grad,
    logsum,
    tables,
    seg_col,
    seg_row,
    lines_low,
    lines_low_t,
    bias_grad,
    key_grad,
    value_grad,
):
    row_len, width = query.shape
    block = 256
    scale = HEAD ** (-0.5)
    key_grad[...] = jnp.zeros_like(key_grad)
    value_grad[...] = jnp.zeros_like(value_grad)
    bias_grad[...] = jnp.zeros_like(bias_grad)

    def put(part, first, grads):
        low = grads.astype(jnp.bfloat16)
        wide = low.astype(jnp.float32)
        columns = slice(part * width, (part + 1) * width)
        lines_low[pl.ds(first, block), columns] = low
        lines_low_t[columns, pl.ds(first, block)] = wide.T.astype(jnp.bfloat16)
        bias_grad[0:1, columns] += jnp.sum(wide, axis=0, keepdims=True)

    def one_block(first, start, size):
        bias = mask_of(seg_col, seg_row, first, start, block, size)
        here = query[pl.ds(first, block), :]
        grad_here = context_grad[pl.ds(first, block), :]
        keys = key[pl.ds(start, size), :]
        values = value[pl.ds(start, size), :]
        sums = logsum[pl.ds(first, block), :]
        total = jnp.zeros((block, width), jnp.float32)
        for head in range(heads):
            mine = of_head(head, (block, width))
            asked = jnp.where(mine, here, jnp.bfloat16(0))
            pulled = jnp.where(mine, grad_here, jnp.bfloat16(0))
            scores = dot_lanes(asked, keys) + bias
            probs = jnp.exp(scores - sums[:, head : head + 1])
            prob_grad = dot_lanes(pulled, values)
            value_grad[pl.ds(start, size), :] += dot_tall(probs.astype(jnp.bfloat16), pulled)
            inner = jnp.sum(probs * prob_grad, axis=1, keepdims=True)
            score_low = (probs * (prob_grad - inner)).astype(jnp.bfloat16)
            total = jnp.where(mine, dot_rows(score_low, keys), total)
            key_grad[pl.ds(start, size), :] += dot_tall(score_low, asked)
        here_tables = [tables[part, pl.ds(first, block), :] for part in range(3)]
        put(0, first, turn(total * scale, here_tables, -1.0))

    over_blocks(row_len, block, one_block)
    for index in range(row_len // block):
        first = index * block
        here_tables = [tables[part, pl.ds(first, block), :] for part in range(3)]
        put(1, first, turn(key_grad[pl.ds(first, block), :], here_tables, -1.0))
        put(2, first, value_grad[pl.ds(first, block), :])


def attend_backward(query, key, value, context_grad, logsum, tables, seg_col, seg_row, heads):
    row_len, width = query.shape
    return pl.pallas_call(
        functools.partial(backward_kernel, heads),
        out_shape=(
            jax.ShapeDtypeStruct((row_len, 3 * width), jnp.bfloat16),
            jax.ShapeDtypeStruct((3 * width, row_len), jnp.bfloat16),
            jax.ShapeDtypeStruct((8, 3 * width), jnp.float32),
        ),
        scratch_shapes=[
            pltpu.VMEM((row_len, width), jnp.float32),
            pltpu.VMEM((row_len, width), jnp.float32),
        ],
        compiler_params=pltpu.CompilerParams(vmem_limit_bytes=VMEM),
        cost_estimate=cost(
            5 * heads * row_len * row_len * 256, 30 * row_len * width, heads * row_len * row_len // 2
        ),
        name="attend_backward",
    )(query, key, value, context_grad, logsum, tables, seg_col, seg_row)


def layout(doc_lengths, row_len):
    ends = jnp.cumsum(doc_lengths[0])
    starts = ends - doc_lengths[0]
    places = jnp.arange(row_len, dtype=jnp.int32)
    segment = jnp.sum((places[:, None] >= ends[None, :]).astype(jnp.int32), axis=1)
    chosen = segment[:, None] == jnp.arange(ends.shape[0], dtype=jnp.int32)[None, :]
    first = jnp.sum(jnp.where(chosen, starts[None, :], 0), axis=1)
    return segment, places - first, segment < ends.shape[0] - 1


def turns(position, width):
    half = ROT // 2
    freq = 10000.0 ** (-(jnp.arange(half).astype(jnp.float32) * (2.0 / ROT)))
    angle = position.astype(jnp.float32)[:, None] * freq
    cosine, sine = jnp.cos(angle), jnp.sin(angle)
    rest = jnp.zeros((position.shape[0], HEAD - ROT), jnp.float32)
    none = jnp.zeros_like(sine)
    parts = (
        jnp.concatenate([cosine, cosine, rest + 1.0], axis=1),
        jnp.concatenate([-sine, none, rest], axis=1),
        jnp.concatenate([none, sine, rest], axis=1),
    )
    return jnp.stack([jnp.tile(part, (1, width // HEAD)) for part in parts])


def cost(flops, moved, transcendentals=0):
    return pl.CostEstimate(
        flops=int(flops), bytes_accessed=int(moved), transcendentals=int(transcendentals)
    )


def weight_kernel(count, order, *refs):
    lhs, rhs, (send, keep) = refs[:count], refs[count], refs[count + 1 :]
    step = pl.program_id(0)
    first = 0
    for part in lhs:
        rows = part.shape[0]
        term = dot_rows(part[...], rhs[...]).astype(jnp.bfloat16)

        @pl.when(step < 2)
        def _(first=first, rows=rows, term=term):
            send[first : first + rows, :] = term

        @pl.when(step >= 2)
        def _(first=first, rows=rows, term=term):
            keep[first : first + rows, :] = term

        first += rows


def weight_terms(lhs, rhs, base, bit, narrow):
    rows = sum(part.shape[0] for part in lhs)
    tokens = rhs.shape[0]
    order = base + jnp.stack([2 * (1 - bit), 2 * (1 - bit) + 1, 2 * bit, 2 * bit + 1])
    half = jax.ShapeDtypeStruct((rows, 2 * narrow), jnp.bfloat16)
    return pl.pallas_call(
        functools.partial(weight_kernel, len(lhs)),
        grid_spec=pltpu.PrefetchScalarGridSpec(
            num_scalar_prefetch=1,
            grid=(4,),
            in_specs=[
                *(pl.BlockSpec(part.shape, lambda step, order: (0, 0)) for part in lhs),
                pl.BlockSpec((tokens, narrow), lambda step, order: (0, order[step])),
            ],
            out_specs=[
                pl.BlockSpec((rows, narrow), lambda step, order: (0, jnp.minimum(step, 1))),
                pl.BlockSpec((rows, narrow), lambda step, order: (0, jnp.maximum(step - 2, 0))),
            ],
        ),
        out_shape=(half, half),
        compiler_params=pltpu.CompilerParams(vmem_limit_bytes=VMEM),
        cost_estimate=cost(
            2 * rows * tokens * 4 * narrow,
            2 * (rows * tokens + tokens * 4 * narrow + rows * 4 * narrow),
        ),
        name="weight_terms",
    )(order.astype(jnp.int32), *lhs, rhs)


def join_kernel(order, keep, came, send, mine):
    total = keep[...] + came[...]

    @pl.when(pl.program_id(1) == 0)
    def _():
        send[...] = total

    @pl.when(pl.program_id(1) == 1)
    def _():
        mine[...] = total


def join_terms(keep, came, bit):
    rows, narrow = keep.shape[0], keep.shape[1] // 2
    tall = rows // 4 if rows % 64 == 0 else rows
    order = jnp.stack([1 - bit, bit]).astype(jnp.int32)
    part = jax.ShapeDtypeStruct((rows, narrow), jnp.bfloat16)
    return pl.pallas_call(
        join_kernel,
        grid_spec=pltpu.PrefetchScalarGridSpec(
            num_scalar_prefetch=1,
            grid=(rows // tall, 2),
            in_specs=[
                pl.BlockSpec((tall, narrow), lambda block, step, order: (block, order[step])),
                pl.BlockSpec((tall, narrow), lambda block, step, order: (block, order[step])),
            ],
            out_specs=[
                pl.BlockSpec((tall, narrow), lambda block, step, order: (block, 0)),
                pl.BlockSpec((tall, narrow), lambda block, step, order: (block, 0)),
            ],
        ),
        out_shape=(part, part),
        compiler_params=pltpu.CompilerParams(vmem_limit_bytes=VMEM),
        cost_estimate=cost(rows * narrow, 12 * rows * narrow),
        name="join_terms",
    )(order, keep, came)


def place_kernel(count, order, *refs):
    pieces, outs = refs[:count], refs[count:]
    step = pl.program_id(0)
    for index, piece in enumerate(pieces):

        @pl.when(step == index)
        def _(piece=piece):
            first = 0
            for out in outs:
                rows = out.shape[0]
                out[...] = piece[first : first + rows, :].astype(jnp.float32)
                first += rows


def place_pieces(pieces, order, sizes):
    count = len(pieces)
    rows, narrow = pieces[0].shape
    return pl.pallas_call(
        functools.partial(place_kernel, count),
        grid_spec=pltpu.PrefetchScalarGridSpec(
            num_scalar_prefetch=1,
            grid=(count,),
            in_specs=[pl.BlockSpec((rows, narrow), lambda step, order: (0, 0))] * count,
            out_specs=[
                pl.BlockSpec((size, narrow), lambda step, order: (0, order[step]))
                for size in sizes
            ],
        ),
        out_shape=[jax.ShapeDtypeStruct((size, count * narrow), jnp.float32) for size in sizes],
        compiler_params=pltpu.CompilerParams(vmem_limit_bytes=VMEM),
        cost_estimate=cost(rows * narrow * count, 6 * rows * narrow * count),
        name="place_pieces",
    )(order.astype(jnp.int32), *pieces)


NEAR = [(0, 1), (1, 0), (2, 3), (3, 2)]
FAR = [(0, 2), (2, 0), (1, 3), (3, 1)]


def sum_half(lhs, rhs, base, pairs, bits, narrow):
    (first, second), (bit, other) = pairs, bits
    send, keep = weight_terms(lhs, rhs, base, bit, narrow)
    came = lax.ppermute(send, "rows", first)
    send, mine = join_terms(keep, came, other)
    mine = mine + lax.ppermute(send, "rows", second)
    across = lax.ppermute(mine, "rows", second)
    return [
        mine,
        across,
        lax.ppermute(mine, "rows", first),
        lax.ppermute(across, "rows", first),
    ]


def sum_over_rows(lhs, halves, bases, narrow):
    row = lax.axis_index("rows")
    near, far = row % 2, row // 2
    left = sum_half(lhs, halves[0], bases[0], (NEAR, FAR), (near, far), narrow)
    right = sum_half(lhs, halves[1], bases[1], (FAR, NEAR), (far, near), narrow)
    order = []
    for base, bit, other in ((0, near, far), (4, far, near)):
        for a, b in ((bit, other), (bit, 1 - other), (1 - bit, other), (1 - bit, 1 - other)):
            order.append(base + 2 * a + b)
    return place_pieces(left + right, jnp.stack(order), [part.shape[0] for part in lhs])


def standardize(values):
    centre = jnp.mean(values, axis=1, keepdims=True)
    centred = values - centre
    spread = jnp.mean(centred * centred, axis=1, keepdims=True)
    inverse = lax.rsqrt(spread + EPSILON)
    return (centred * inverse, inverse)


def product(a, b):
    return jnp.dot(a, b, preferred_element_type=jnp.float32)


def widen(values, heads_width, width):
    if heads_width == width:
        return values
    groups = values.shape[-1] // heads_width
    split = values.reshape(*values.shape[:-1], groups, heads_width)
    spare = [(0, 0)] * (split.ndim - 1) + [(0, width - heads_width)]
    return jnp.pad(split, spare).reshape(*values.shape[:-1], groups * width)


def per_device(
    block_input,
    norm_gain,
    norm_bias,
    qkv_weight,
    qkv_bias,
    out_weight,
    gate_weight,
    up_weight,
    down_weight,
    cotangent,
    doc_lengths,
):
    shard, features = block_input.shape
    group = lax.axis_size("tp")
    tokens = shard * group
    width = qkv_weight.shape[1]
    heads = width // HEAD
    padded = max(width, 128)
    half = features // 2
    me = lax.axis_index("tp")
    segment, position, live = layout(doc_lengths, tokens)
    live_mine = lax.dynamic_slice_in_dim(live, me * shard, shard)[:, None]
    input_wide = block_input.astype(jnp.float32)
    gain = norm_gain.astype(jnp.float32)
    shift = norm_bias.astype(jnp.float32)
    normed, inverse = standardize(input_wide)
    normed_low = (normed * gain + shift).astype(jnp.bfloat16)
    hidden_in = lax.all_gather(normed_low, "tp", axis=0, tiled=True)
    grad_mine = jnp.where(live_mine, cotangent, jnp.zeros_like(cotangent))
    grad_mine, _ = lax.optimization_barrier((grad_mine, hidden_in))
    grad_left = lax.all_gather(grad_mine[:, :half], "tp", axis=0, tiled=True)
    grad_right_mine, _ = lax.optimization_barrier((grad_mine[:, half:], grad_left))
    grad_right = lax.all_gather(grad_right_mine, "tp", axis=0, tiled=True)
    tables = turns(position, padded)
    seg_col = jnp.broadcast_to(segment[:, None], (tokens, 128))
    seg_row = jnp.broadcast_to(segment[None, :], (8, tokens))

    gate = jnp.einsum("td,fd->tf", hidden_in, gate_weight, preferred_element_type=jnp.float32)
    up = jnp.einsum("td,fd->tf", hidden_in, up_weight, preferred_element_type=jnp.float32)
    sigmoid = jax.nn.sigmoid(gate)
    mixed = (gate * sigmoid * up).astype(jnp.bfloat16)
    projection = qkv_weight.reshape(3 * width, features)
    lines = jnp.einsum("td,ed->te", hidden_in, projection, preferred_element_type=jnp.float32)
    lines = lines + qkv_bias.astype(jnp.float32).reshape(1, 3 * width)
    query, key, value, context, context_t, logsum = attend_forward(
        widen(lines, width, padded), tables, seg_col, seg_row, heads
    )
    context, context_t = context[:, :width], context_t[:width]
    down_grad, out_grad = sum_over_rows(
        [mixed.T, context_t], [grad_left, grad_right], [0, 0], features // 8
    )
    merged = product(context, out_weight) + product(mixed, down_weight)
    merged = lax.psum_scatter(
        merged.astype(jnp.bfloat16), "tp", scatter_dimension=0, tiled=True
    ).astype(jnp.float32)
    output = (input_wide + jnp.where(live_mine, merged, 0.0)).astype(jnp.bfloat16)

    def pulled(weight):
        return product(grad_left, weight[:, :half].T) + product(grad_right, weight[:, half:].T)

    mixed_grad = pulled(down_weight)
    gate_low = (mixed_grad * up * sigmoid * (1.0 + gate * (1.0 - sigmoid))).astype(jnp.bfloat16)
    up_low = (mixed_grad * gate * sigmoid).astype(jnp.bfloat16)
    gate_grad, up_grad = sum_over_rows(
        [gate_low.T, up_low.T], [hidden_in, hidden_in], [0, 4], features // 8
    )
    context_grad = pulled(out_weight).astype(jnp.bfloat16)
    lines_low, lines_low_t, bias_grad = attend_backward(
        query,
        key,
        value,
        widen(context_grad, width, padded),
        logsum,
        tables,
        seg_col,
        seg_row,
        heads,
    )
    lines_low = lines_low.reshape(tokens, 3, padded)[:, :, :width].reshape(tokens, 3 * width)
    lines_low_t = lines_low_t.reshape(3, padded, tokens)[:, :width].reshape(3 * width, tokens)
    bias_grad = bias_grad[0].reshape(3, padded)[:, :width]
    (qkv_grad,) = sum_over_rows([lines_low_t], [hidden_in, hidden_in], [0, 4], features // 8)
    term = product(lines_low, projection) + product(gate_low, gate_weight)
    term = term + product(up_low, up_weight)
    normed_grad = lax.psum_scatter(
        term.astype(jnp.bfloat16), "tp", scatter_dimension=0, tiled=True
    ).astype(jnp.float32)
    scaled = normed_grad * gain
    input_grad = inverse * (
        scaled
        - jnp.mean(scaled, axis=1, keepdims=True)
        - normed * jnp.mean(scaled * normed, axis=1, keepdims=True)
    )
    input_grad = input_grad + cotangent.astype(jnp.float32)
    bias_slots = lax.dynamic_update_slice(
        jnp.zeros((3, group * width), jnp.float32), bias_grad, (0, me * width)
    )
    small = jnp.concatenate(
        [
            jnp.sum(normed_grad * normed, axis=0),
            jnp.sum(normed_grad, axis=0),
            bias_slots.reshape(-1),
        ]
    )
    small = lax.psum(small, ("rows", "tp"))
    bias_slots = small[2 * features :].reshape(3, group * width)
    return (
        output,
        input_grad,
        small[:features],
        small[features : 2 * features],
        qkv_grad.reshape(3, width, features),
        lax.dynamic_slice(bias_slots, (0, me * width), (3, width)),
        out_grad,
        gate_grad,
        up_grad,
        down_grad,
    )


def solution(mesh):
    placed = (
        P(("rows", "tp"), None),
        P(),
        P(),
        P(None, "tp", None),
        P(None, "tp"),
        P("tp", None),
        P("tp", None),
        P("tp", None),
        P("tp", None),
        P(("rows", "tp"), None),
        P("rows", None),
    )
    return jax.shard_map(
        per_device,
        mesh=mesh,
        in_specs=placed,
        out_specs=(
            P(("rows", "tp"), None),
            P(("rows", "tp"), None),
            P(),
            P(),
            P(None, "tp", None),
            P(None, "tp"),
            P("tp", None),
            P("tp", None),
            P("tp", None),
            P("tp", None),
        ),
        check_vma=False,
    )
```

```python
import functools
import jax
import jax.numpy as jnp
from jax import lax
from jax.experimental import pallas as pl
from jax.experimental.pallas import tpu as pltpu
from jax.sharding import PartitionSpec as P

HEAD = 64
ROT = 16
MASKED = -1e30
LONG = 1000
EPSILON = 1e-05
ROOM = 16 * 2**20
IN_VMEM = pl.BlockSpec(memory_space=pltpu.VMEM)
IN_SMEM = pl.BlockSpec(memory_space=pltpu.SMEM)


def dot_rows(a, b):
    return lax.dot_general(a, b, (((1,), (0,)), ((), ())), preferred_element_type=jnp.float32)


def dot_lanes(a, b):
    return lax.dot_general(a, b, (((1,), (1,)), ((), ())), preferred_element_type=jnp.float32)


def dot_tall(a, b):
    return lax.dot_general(a, b, (((0,), (0,)), ((), ())), preferred_element_type=jnp.float32)


def turn(values, tables, sign):
    half = ROT // 2
    width = values.shape[1]
    tables = [jnp.concatenate([part] * (width // 128), axis=1) for part in tables]
    up = pltpu.roll(values, width - half, 1)
    down = pltpu.roll(values, half, 1)
    return values * tables[0] + sign * (up * tables[1] + down * tables[2])


def of_head(head, shape):
    return lax.broadcasted_iota(jnp.int32, shape, 1) // HEAD == head


def over_blocks(row_len, block, body):
    longest = row_len // 2
    blocks = row_len // block
    if blocks <= 8:
        for index in range(blocks):
            first = index * block
            start = max(0, first + block - (longest + block))
            body(first, start, first + block - start)
    else:
        size = longest + block

        def step(index, carry):
            first = pl.multiple_of(index * block, block)
            start = pl.multiple_of(jnp.maximum(first - longest, 0), block)
            body(first, start, size)
            return carry

        lax.fori_loop(0, blocks, step, 0)


def mask_of(seg_col, seg_row, first, start, block, size):
    rows = first + lax.broadcasted_iota(jnp.int32, (block, size), 0)
    keys = start + lax.broadcasted_iota(jnp.int32, (block, size), 1)
    same = seg_col[pl.ds(first, block), 0:1] == seg_row[0:1, pl.ds(start, size)]
    return jnp.where(same & (keys <= rows), 0.0, MASKED)


def forward_kernel(
    heads,
    hidden_in,
    projection,
    shift,
    tables,
    seg_col,
    seg_row,
    query,
    key,
    value,
    context,
    context_t,
    logsum,
):
    row_len, width = query.shape
    block = 256
    scale = HEAD ** (-0.5)
    for first in range(0, row_len, block):
        here = slice(first, first + block)
        lines = dot_lanes(hidden_in[here, :], projection[...]) + shift[...]
        turning = [tables[part, here, :] for part in range(3)]
        asked = turn(lines[:, 0:width], turning, 1.0).astype(jnp.bfloat16)
        query[here, :] = asked * jnp.bfloat16(scale)
        key[here, :] = turn(lines[:, width : 2 * width], turning, 1.0).astype(jnp.bfloat16)
        value[here, :] = lines[:, 2 * width : 3 * width].astype(jnp.bfloat16)

    def one_block(first, start, size):
        bias = mask_of(seg_col, seg_row, first, start, block, size)
        here = query[pl.ds(first, block), :]
        keys = key[pl.ds(start, size), :]
        values = value[pl.ds(start, size), :]
        total = jnp.zeros((block, width), jnp.float32)
        lane = lax.broadcasted_iota(jnp.int32, (block, 128), 1)
        sums = jnp.zeros((block, 128), jnp.float32)
        for head in range(heads):
            mine = of_head(head, (block, width))
            scores = dot_lanes(jnp.where(mine, here, jnp.bfloat16(0)), keys) + bias
            highest = jnp.max(scores, axis=1, keepdims=True)
            raised = jnp.exp(scores - highest)
            amount = jnp.sum(raised, axis=1, keepdims=True)
            weights = (raised * (1.0 / amount)).astype(jnp.bfloat16)
            total = jnp.where(mine, dot_rows(weights, values), total)
            sums = jnp.where(lane == head, highest + jnp.log(amount), sums)
        context[pl.ds(first, block), :] = total.astype(jnp.bfloat16)
        context_t[:, pl.ds(first, block)] = total.T.astype(jnp.bfloat16)
        logsum[pl.ds(first, block), :] = sums

    over_blocks(row_len, block, one_block)


def attend_forward(hidden_in, projection, shift, tables, seg_col, seg_row, heads):
    row_len, width = hidden_in.shape[0], projection.shape[0] // 3
    low = jax.ShapeDtypeStruct((row_len, width), jnp.bfloat16)
    return pl.pallas_call(
        functools.partial(forward_kernel, heads),
        in_specs=[IN_VMEM] * 6,
        out_shape=(
            low,
            low,
            low,
            low,
            jax.ShapeDtypeStruct((width, row_len), jnp.bfloat16),
            jax.ShapeDtypeStruct((row_len, 128), jnp.float32),
        ),
        compiler_params=pltpu.CompilerParams(vmem_limit_bytes=ROOM + 4096 * row_len),
        cost_estimate=busy(8.5),
        name="attend_forward",
    )(hidden_in, projection, shift, tables, seg_col, seg_row)


def backward_kernel(
    heads,
    query,
    key,
    value,
    grad_all,
    out_weight,
    logsum,
    tables,
    seg_col,
    seg_row,
    lines_low,
    lines_low_t,
    bias_grad,
    key_grad,
    value_grad,
):
    row_len, width = query.shape
    block = 256
    scale = HEAD ** (-0.5)
    key_grad[...] = jnp.zeros_like(key_grad)
    value_grad[...] = jnp.zeros_like(value_grad)
    bias_grad[...] = jnp.zeros_like(bias_grad)

    def put(part, first, grads):
        low = grads.astype(jnp.bfloat16)
        wide = low.astype(jnp.float32)
        columns = slice(part * width, (part + 1) * width)
        lines_low[pl.ds(first, block), columns] = low
        lines_low_t[columns, pl.ds(first, block)] = wide.T.astype(jnp.bfloat16)
        bias_grad[0:1, columns] += jnp.sum(wide, axis=0, keepdims=True)

    def one_block(first, start, size):
        bias = mask_of(seg_col, seg_row, first, start, block, size)
        here = query[pl.ds(first, block), :]
        grad_here = dot_lanes(grad_all[pl.ds(first, block), :], out_weight[...])
        grad_here = grad_here.astype(jnp.bfloat16)
        keys = key[pl.ds(start, size), :]
        values = value[pl.ds(start, size), :]
        sums = logsum[pl.ds(first, block), :]
        total = jnp.zeros((block, width), jnp.float32)
        for head in range(heads):
            mine = of_head(head, (block, width))
            asked = jnp.where(mine, here, jnp.bfloat16(0))
            pulled = jnp.where(mine, grad_here, jnp.bfloat16(0))
            scores = dot_lanes(asked, keys) + bias
            probs = jnp.exp(scores - sums[:, head : head + 1])
            prob_grad = dot_lanes(pulled, values)
            value_grad[pl.ds(start, size), :] += dot_tall(probs.astype(jnp.bfloat16), pulled)
            inner = jnp.sum(probs * prob_grad, axis=1, keepdims=True)
            score_low = (probs * (prob_grad - inner)).astype(jnp.bfloat16)
            total = jnp.where(mine, dot_rows(score_low, keys), total)
            key_grad[pl.ds(start, size), :] += dot_tall(score_low, asked)
        here_tables = [tables[part, pl.ds(first, block), :] for part in range(3)]
        put(0, first, turn(total * scale, here_tables, -1.0))

    over_blocks(row_len, block, one_block)
    for index in range(row_len // block):
        first = index * block
        here_tables = [tables[part, pl.ds(first, block), :] for part in range(3)]
        put(1, first, turn(key_grad[pl.ds(first, block), :], here_tables, -1.0))
        put(2, first, value_grad[pl.ds(first, block), :])


def attend_backward(
    query, key, value, grad_all, out_weight, logsum, tables, seg_col, seg_row, heads
):
    row_len, width = query.shape
    return pl.pallas_call(
        functools.partial(backward_kernel, heads),
        in_specs=[IN_VMEM] * 9,
        out_shape=(
            jax.ShapeDtypeStruct((row_len, 3 * width), jnp.bfloat16),
            jax.ShapeDtypeStruct((3 * width, row_len), jnp.bfloat16),
            jax.ShapeDtypeStruct((8, 3 * width), jnp.float32),
        ),
        scratch_shapes=[
            pltpu.VMEM((row_len, width), jnp.float32),
            pltpu.VMEM((row_len, width), jnp.float32),
        ],
        compiler_params=pltpu.CompilerParams(vmem_limit_bytes=ROOM + 4096 * row_len),
        cost_estimate=busy(13.3),
        name="attend_backward",
    )(query, key, value, grad_all, out_weight, logsum, tables, seg_col, seg_row)


def layout(doc_lengths, row_len):
    ends = jnp.cumsum(doc_lengths[0])
    starts = ends - doc_lengths[0]
    places = jnp.arange(row_len, dtype=jnp.int32)
    segment = jnp.sum((places[:, None] >= ends[None, :]).astype(jnp.int32), axis=1)
    chosen = segment[:, None] == jnp.arange(ends.shape[0], dtype=jnp.int32)[None, :]
    first = jnp.sum(jnp.where(chosen, starts[None, :], 0), axis=1)
    return segment, places - first, segment < ends.shape[0] - 1


def turns(position):
    half = ROT // 2
    lane = lax.broadcasted_iota(jnp.int32, (position.shape[0], 128), 1) % HEAD
    freq = 10000.0 ** (-((lane % half).astype(jnp.float32) * (2.0 / ROT)))
    angle = position.astype(jnp.float32)[:, None] * freq
    cosine, sine = jnp.cos(angle), jnp.sin(angle)
    return jnp.stack(
        [
            jnp.where(lane < ROT, cosine, 1.0),
            jnp.where(lane < half, -sine, 0.0),
            jnp.where((lane >= half) & (lane < ROT), sine, 0.0),
        ]
    )


def busy(time):
    return pl.CostEstimate(flops=int(time * 1.0 * 10**9), bytes_accessed=0, transcendentals=0)


def blocks_of(tokens):
    return min(512, tokens)


def gated_kernel(hidden_in, gate_weight, up_weight, gate, up, mixed, mixed_t):
    gate_here = dot_lanes(gate_weight[...], hidden_in[...])
    up_here = dot_lanes(up_weight[...], hidden_in[...])
    gate[...] = gate_here
    up[...] = up_here
    total = gate_here * jax.nn.sigmoid(gate_here) * up_here
    mixed_t[...] = total.astype(jnp.bfloat16)
    mixed[...] = total.T.astype(jnp.bfloat16)


def gated_forward(hidden_in, gate_weight, up_weight):
    (tokens, features), units = hidden_in.shape, gate_weight.shape[0]
    block = blocks_of(tokens)
    tall = pl.BlockSpec((units, block), lambda step: (0, step))
    flat = pl.BlockSpec((block, units), lambda step: (step, 0))
    return pl.pallas_call(
        gated_kernel,
        grid=(tokens // block,),
        in_specs=[pl.BlockSpec((block, features), lambda step: (step, 0)), IN_VMEM, IN_VMEM],
        out_specs=[tall, tall, flat, tall],
        out_shape=[
            jax.ShapeDtypeStruct((units, tokens), jnp.float32),
            jax.ShapeDtypeStruct((units, tokens), jnp.float32),
            jax.ShapeDtypeStruct((tokens, units), jnp.bfloat16),
            jax.ShapeDtypeStruct((units, tokens), jnp.bfloat16),
        ],
        compiler_params=pltpu.CompilerParams(vmem_limit_bytes=ROOM),
        cost_estimate=busy(7.5),
        name="gated_forward",
    )(hidden_in, gate_weight, up_weight)


def gated_back_kernel(
    grad_all, down_weight, gate, up, gate_low, gate_low_t, up_low, up_low_t
):
    mixed_grad = dot_lanes(down_weight[...], grad_all[...])
    gate_here = gate[...]
    sigmoid = jax.nn.sigmoid(gate_here)
    pulled = mixed_grad * sigmoid
    gate_grad = pulled * up[...] * (1.0 + gate_here * (1.0 - sigmoid))
    up_grad = pulled * gate_here
    gate_low_t[...] = gate_grad.astype(jnp.bfloat16)
    up_low_t[...] = up_grad.astype(jnp.bfloat16)
    gate_low[...] = gate_grad.T.astype(jnp.bfloat16)
    up_low[...] = up_grad.T.astype(jnp.bfloat16)


def gated_backward(grad_all, down_weight, gate, up):
    (tokens, features), units = grad_all.shape, down_weight.shape[0]
    block = blocks_of(tokens)
    tall = pl.BlockSpec((units, block), lambda step: (0, step))
    flat = pl.BlockSpec((block, units), lambda step: (step, 0))
    wide = jax.ShapeDtypeStruct((tokens, units), jnp.bfloat16)
    long = jax.ShapeDtypeStruct((units, tokens), jnp.bfloat16)
    return pl.pallas_call(
        gated_back_kernel,
        grid=(tokens // block,),
        in_specs=[pl.BlockSpec((block, features), lambda step: (step, 0)), IN_VMEM, tall, tall],
        out_specs=[flat, tall, flat, tall],
        out_shape=[wide, long, wide, long],
        compiler_params=pltpu.CompilerParams(vmem_limit_bytes=ROOM),
        cost_estimate=busy(5.4),
        name="gated_backward",
    )(grad_all, down_weight, gate, up)


def merge_kernel(count, *refs):
    total = dot_rows(refs[0][...], refs[count][...])
    for index in range(1, count):
        total = total + dot_rows(refs[index][...], refs[count + index][...])
    refs[2 * count][...] = total.astype(jnp.bfloat16)


def merge(lhs, weights):
    tokens, features, count = lhs[0].shape[0], weights[0].shape[1], len(lhs)
    block = min(256, tokens)
    return pl.pallas_call(
        functools.partial(merge_kernel, count),
        grid=(tokens // block,),
        in_specs=[
            *(pl.BlockSpec((block, part.shape[1]), lambda step: (step, 0)) for part in lhs),
            *([IN_VMEM] * count),
        ],
        out_specs=pl.BlockSpec((block, features), lambda step: (step, 0)),
        out_shape=jax.ShapeDtypeStruct((tokens, features), jnp.bfloat16),
        compiler_params=pltpu.CompilerParams(vmem_limit_bytes=ROOM),
        cost_estimate=busy(8),
        name="merge",
    )(*lhs, *weights)


def stacked(lhs, which, rhs, first, wide, keep):
    row = 0
    blocks = [part[:, pl.ds(pl.multiple_of(at, 128), wide)] for part, at in zip(rhs, first)]
    for part, index in zip(lhs, which):
        keep(row, part.shape[0], dot_rows(part[...], blocks[index]))
        row += part.shape[0]


def send_kernel(which, wide, order, *refs):
    count = len(which)
    lhs, rhs, outs = refs[:count], refs[count:-2], refs[-2:]
    for half, out in enumerate(outs):

        def keep(row, rows, term, out=out):
            out[row : row + rows, :] = term.astype(jnp.bfloat16)

        first = [order[half, index] for index in range(len(rhs))]
        stacked(lhs, which, rhs, first, wide, keep)


def join_kernel(which, wide, order, *refs):
    count = len(which)
    lhs, rhs, came = refs[:count], refs[count:-7], refs[-7:-5]
    outs, total = refs[-5:-1], refs[-1]
    narrow = wide // 2
    for half in range(2):

        def keep(row, rows, term, half=half):
            there = came[half][row : row + rows, :].astype(jnp.float32)
            total[row : row + rows, :] = (term + there).astype(jnp.bfloat16)

        first = [order[half, index] for index in range(len(rhs))]
        stacked(lhs, which, rhs, first, wide, keep)
        bit = order[2, half]
        outs[2 * half][...] = total[:, pl.ds(pl.multiple_of((1 - bit) * narrow, narrow), narrow)]
        outs[2 * half + 1][...] = total[:, pl.ds(pl.multiple_of(bit * narrow, narrow), narrow)]


def place_kernel(order, *refs):
    pieces, outs = refs[:6], refs[6:]
    rows = pieces[0].shape[0]
    step = pl.program_id(0)
    for index in range(8):
        piece, start = pieces[min(index, 4 + index % 2)], rows * (index // 6)

        @pl.when(step == index)
        def _(piece=piece, start=start):
            first = start
            for out in outs:
                size = out.shape[0]
                out[...] = piece[first : first + size, :].astype(jnp.float32)
                first += size


def place(pieces, order, sizes, features):
    rows, narrow = pieces[0].shape
    return pl.pallas_call(
        place_kernel,
        grid_spec=pltpu.PrefetchScalarGridSpec(
            num_scalar_prefetch=1,
            grid=(8,),
            in_specs=[IN_VMEM] * len(pieces),
            out_specs=[
                pl.BlockSpec((size, narrow), lambda step, order: (0, order[step]))
                for size in sizes
            ],
        ),
        out_shape=[jax.ShapeDtypeStruct((size, features), jnp.float32) for size in sizes],
        compiler_params=pltpu.CompilerParams(vmem_limit_bytes=ROOM),
        cost_estimate=busy(6.5),
        name="place",
    )(jnp.stack(order).astype(jnp.int32), *pieces)


NEAR = [(0, 1), (1, 0), (2, 3), (3, 2)]
FAR = [(0, 2), (2, 0), (1, 3), (3, 1)]
PATHS = ((NEAR, FAR), (FAR, NEAR))


def after(value, *others):
    return lax.optimization_barrier((value, others))[0]


class Sum:
    def __init__(self, lhs, which, rhs, starts, columns, time=0):
        row = lax.axis_index("rows")
        near, far = row % 2, row // 2
        self.bits = ((near, far), (far, near))
        self.lhs, self.which, self.rhs, self.starts = lhs, which, rhs, starts
        self.narrow = columns // 8
        self.time = time
        self.rows = sum(part.shape[0] for part in lhs)

    def first(self, half, bit):
        return [start + self.narrow * (4 * half + 2 * bit) for start in self.starts]

    def piece(self, wide):
        return jax.ShapeDtypeStruct((self.rows, wide), jnp.bfloat16)

    def send(self, *earlier):
        order = jnp.array([self.first(half, 1 - self.bits[half][0]) for half in range(2)])
        wide = 2 * self.narrow
        head = after(self.lhs[0], *earlier)
        sent = pl.pallas_call(
            functools.partial(send_kernel, self.which, wide),
            in_specs=[IN_SMEM] + [IN_VMEM] * (len(self.lhs) + len(self.rhs)),
            out_shape=[self.piece(wide)] * 2,
            compiler_params=pltpu.CompilerParams(vmem_limit_bytes=ROOM + 2048 * self.lhs[0].shape[1]),
            cost_estimate=busy(self.rows / 256),
            name="send_terms",
        )(order.astype(jnp.int32), head, *self.lhs[1:], *self.rhs)
        self.came = [lax.ppermute(sent[half], "rows", PATHS[half][0]) for half in range(2)]
        return sent[0]

    def join(self, *earlier):
        wide = 2 * self.narrow
        order = [[*self.first(half, self.bits[half][0]), 0][:2] for half in range(2)]
        order.append([self.bits[0][1], self.bits[1][1]])
        head = after(self.lhs[0], *earlier)
        outs = pl.pallas_call(
            functools.partial(join_kernel, self.which, wide),
            in_specs=[IN_SMEM] + [IN_VMEM] * (len(self.lhs) + len(self.rhs) + 2),
            out_shape=[self.piece(self.narrow)] * 4,
            scratch_shapes=[pltpu.VMEM((self.rows, wide), jnp.bfloat16)],
            compiler_params=pltpu.CompilerParams(vmem_limit_bytes=ROOM + 2048 * self.lhs[0].shape[1]),
            cost_estimate=busy(self.time if self.time else self.rows / 256),
            name="join_terms",
        )(jnp.array(order).astype(jnp.int32), head, *self.lhs[1:], *self.rhs, *self.came)
        self.mine = [outs[1], outs[3]]
        self.came = [lax.ppermute(outs[2 * half], "rows", PATHS[half][1]) for half in range(2)]
        return outs[0]

    def total(self, *earlier):
        mine = lax.optimization_barrier((*self.mine, *earlier))[:2]
        self.mine = [mine[half] + self.came[half] for half in range(2)]
        self.across = [lax.ppermute(self.mine[half], "rows", PATHS[half][1]) for half in range(2)]
        return self.mine

    def share(self, *earlier):
        mine = lax.optimization_barrier((*self.mine, *earlier))[:2]
        both = [jnp.concatenate([mine[half], self.across[half]]) for half in range(2)]
        self.last = [lax.ppermute(both[half], "rows", PATHS[half][0]) for half in range(2)]
        return both

    def place(self, features, *earlier):
        order = []
        for first, second in ((0, 0), (0, 1), (1, 0), (1, 1)):
            for half in range(2):
                a, b = self.bits[half]
                order.append(4 * half + 2 * jnp.abs(a - first) + jnp.abs(b - second))
        mine = lax.optimization_barrier((*self.mine, *earlier))[:2]
        sizes = [part.shape[0] for part in self.lhs]
        return place([*mine, *self.across, *self.last], order, sizes, features)


def sum_everywhere(values, axis):
    size, step = lax.axis_size(axis), 1
    while step < size:
        values = values + lax.ppermute(values, axis, [(i, i ^ step) for i in range(size)])
        step *= 2
    return values


def standardize(values):
    centre = jnp.mean(values, axis=1, keepdims=True)
    centred = values - centre
    spread = jnp.mean(centred * centred, axis=1, keepdims=True)
    inverse = lax.rsqrt(spread + EPSILON)
    return (centred * inverse, inverse)


def widen(weight, width):
    return jnp.pad(weight, ((0, 0), (0, width - weight.shape[1]), (0, 0)))


def per_device(
    block_input,
    norm_gain,
    norm_bias,
    qkv_weight,
    qkv_bias,
    out_weight,
    gate_weight,
    up_weight,
    down_weight,
    cotangent,
    doc_lengths,
):
    shard, features = block_input.shape
    group = lax.axis_size("tp")
    tokens = shard * group
    width = qkv_weight.shape[1]
    heads = width // HEAD
    padded = max(width, 128)
    me = lax.axis_index("tp")
    segment, position, live = layout(doc_lengths, tokens)
    live_mine = lax.dynamic_slice_in_dim(live, me * shard, shard)[:, None]
    input_wide = block_input.astype(jnp.float32)
    gain = norm_gain.astype(jnp.float32)
    shift = norm_bias.astype(jnp.float32)
    normed, inverse = standardize(input_wide)
    normed_low = (normed * gain + shift).astype(jnp.bfloat16)
    hidden_in = lax.all_gather(normed_low, "tp", axis=0, tiled=True)
    grad_mine = jnp.where(live_mine, cotangent, jnp.zeros_like(cotangent))
    grad_all = lax.all_gather(after(grad_mine, hidden_in), "tp", axis=0, tiled=True)
    tables = turns(position)
    seg_col = jnp.broadcast_to(segment[:, None], (tokens, 128))
    seg_row = jnp.broadcast_to(segment[None, :], (8, tokens))

    projection = widen(qkv_weight, padded).reshape(3 * padded, features)
    shift_lines = widen(qkv_bias[..., None], padded).reshape(1, 3 * padded).astype(jnp.float32)
    out_wide = widen(out_weight[None], padded)[0]
    gate, up, mixed, mixed_t = gated_forward(hidden_in, gate_weight, up_weight)
    query, key, value, context, context_t, logsum = attend_forward(
        after(hidden_in, mixed), projection, shift_lines, tables, seg_col, seg_row, heads
    )
    merged = merge([context, mixed], [out_wide, down_weight])
    down_sum = Sum([mixed_t], [0], [grad_all], [0], features)
    order = down_sum.send(merged)
    gate_low, gate_low_t, up_low, up_low_t = gated_backward(
        after(grad_all, order), down_weight, gate, up
    )
    inner_sum = Sum([gate_low_t, up_low_t], [0, 0], [hidden_in], [0], features, LONG)
    order = inner_sum.send()
    order = down_sum.join(order)
    lines_low, lines_low_t, bias_grad = attend_backward(
        query,
        key,
        value,
        after(grad_all, order),
        out_wide,
        logsum,
        tables,
        seg_col,
        seg_row,
        heads,
    )
    bias_grad = bias_grad[0].reshape(3, padded)[:, :width]
    outer_sum = Sum([lines_low_t, context_t], [0, 1], [hidden_in, grad_all], [0, 0], features, LONG)
    term = merge([gate_low, up_low, lines_low], [gate_weight, up_weight, projection])
    order = down_sum.total(term)
    order = inner_sum.join(order)
    order = down_sum.share(order)
    order = outer_sum.send(order)
    (down_grad,) = down_sum.place(features, order)
    order = inner_sum.total(down_grad)
    order = outer_sum.join(order)
    normed_grad = lax.psum_scatter(term, "tp", scatter_dimension=0, tiled=True)
    normed_grad = after(normed_grad, order).astype(jnp.float32)
    sums = jnp.concatenate([jnp.sum(normed_grad * normed, axis=0), jnp.sum(normed_grad, axis=0)])
    sums = sum_everywhere(sums, "tp")
    order = inner_sum.share(sums)
    order = outer_sum.total(order)
    sums = after(jnp.concatenate([sums, bias_grad.reshape(-1)]), order)
    sums = sum_everywhere(sums, "rows")
    order = outer_sum.share(sums)
    merged = lax.psum_scatter(merged, "tp", scatter_dimension=0, tiled=True)
    merged = merged.astype(jnp.float32)
    output = (input_wide + jnp.where(live_mine, merged, 0.0)).astype(jnp.bfloat16)
    scaled = normed_grad * gain
    input_grad = inverse * (
        scaled
        - jnp.mean(scaled, axis=1, keepdims=True)
        - normed * jnp.mean(scaled * normed, axis=1, keepdims=True)
    )
    input_grad = input_grad + cotangent.astype(jnp.float32)
    gate_grad, up_grad = inner_sum.place(features, order)
    qkv_grad, out_grad = outer_sum.place(features, gate_grad)
    return (
        output,
        input_grad,
        sums[:features],
        sums[features : 2 * features],
        qkv_grad.reshape(3, padded, features)[:, :width],
        sums[2 * features :].reshape(3, width),
        out_grad[:width],
        gate_grad,
        up_grad,
        down_grad,
    )


def solution(mesh):
    placed = (
        P(("rows", "tp"), None),
        P(),
        P(),
        P(None, "tp", None),
        P(None, "tp"),
        P("tp", None),
        P("tp", None),
        P("tp", None),
        P("tp", None),
        P(("rows", "tp"), None),
        P("rows", None),
    )
    return jax.shard_map(
        per_device,
        mesh=mesh,
        in_specs=placed,
        out_specs=(
            P(("rows", "tp"), None),
            P(("rows", "tp"), None),
            P(),
            P(),
            P(None, "tp", None),
            P(None, "tp"),
            P("tp", None),
            P("tp", None),
            P("tp", None),
            P("tp", None),
        ),
        check_vma=False,
    )
```

```python
import functools
import jax
import jax.numpy as jnp
from jax import lax
from jax.experimental import pallas as pl
from jax.experimental.pallas import tpu as pltpu
from jax.sharding import PartitionSpec as P

HEAD = 64
ROT = 16
MASKED = -1e30
LONG = 1000
EPSILON = 1e-05
ROOM = 16 * 2**20
IN_VMEM = pl.BlockSpec(memory_space=pltpu.VMEM)
IN_SMEM = pl.BlockSpec(memory_space=pltpu.SMEM)


def dot_rows(a, b):
    return lax.dot_general(a, b, (((1,), (0,)), ((), ())), preferred_element_type=jnp.float32)


def dot_lanes(a, b):
    return lax.dot_general(a, b, (((1,), (1,)), ((), ())), preferred_element_type=jnp.float32)


def dot_tall(a, b):
    return lax.dot_general(a, b, (((0,), (0,)), ((), ())), preferred_element_type=jnp.float32)


def turn(values, tables, sign):
    half = ROT // 2
    width = values.shape[1]
    tables = [jnp.concatenate([part] * (width // 128), axis=1) for part in tables]
    up = pltpu.roll(values, width - half, 1)
    down = pltpu.roll(values, half, 1)
    return values * tables[0] + sign * (up * tables[1] + down * tables[2])


def of_head(head, shape):
    return lax.broadcasted_iota(jnp.int32, shape, 1) // HEAD == head


def over_blocks(row_len, block, body):
    longest = row_len // 2
    blocks = row_len // block
    if blocks <= 8:
        for index in range(blocks):
            first = index * block
            start = max(0, first + block - (longest + block))
            body(first, start, first + block - start)
    else:
        size = longest + block

        def step(index, carry):
            first = pl.multiple_of(index * block, block)
            start = pl.multiple_of(jnp.maximum(first - longest, 0), block)
            body(first, start, size)
            return carry

        lax.fori_loop(0, blocks, step, 0)


def mask_of(seg_col, seg_row, first, start, block, size):
    rows = first + lax.broadcasted_iota(jnp.int32, (block, size), 0)
    keys = start + lax.broadcasted_iota(jnp.int32, (block, size), 1)
    same = seg_col[pl.ds(first, block), 0:1] == seg_row[0:1, pl.ds(start, size)]
    return jnp.where(same & (keys <= rows), 0.0, MASKED)


def forward_kernel(
    heads,
    hidden_in,
    projection,
    shift,
    tables,
    seg_col,
    seg_row,
    query,
    key,
    value,
    context,
    context_t,
    logsum,
):
    row_len, width = query.shape
    block = 256
    scale = HEAD ** (-0.5)
    for first in range(0, row_len, block):
        here = slice(first, first + block)
        lines = dot_lanes(hidden_in[here, :], projection[...]) + shift[...]
        turning = [tables[part, here, :] for part in range(3)]
        asked = turn(lines[:, 0:width], turning, 1.0).astype(jnp.bfloat16)
        query[here, :] = asked * jnp.bfloat16(scale)
        key[here, :] = turn(lines[:, width : 2 * width], turning, 1.0).astype(jnp.bfloat16)
        value[here, :] = lines[:, 2 * width : 3 * width].astype(jnp.bfloat16)

    def one_block(first, start, size):
        bias = mask_of(seg_col, seg_row, first, start, block, size)
        here = query[pl.ds(first, block), :]
        keys = key[pl.ds(start, size), :]
        values = value[pl.ds(start, size), :]
        total = jnp.zeros((block, width), jnp.float32)
        lane = lax.broadcasted_iota(jnp.int32, (block, 128), 1)
        sums = jnp.zeros((block, 128), jnp.float32)
        for head in range(heads):
            mine = of_head(head, (block, width))
            scores = dot_lanes(jnp.where(mine, here, jnp.bfloat16(0)), keys) + bias
            highest = jnp.max(scores, axis=1, keepdims=True)
            raised = jnp.exp(scores - highest)
            amount = jnp.sum(raised, axis=1, keepdims=True)
            weights = (raised * (1.0 / amount)).astype(jnp.bfloat16)
            total = jnp.where(mine, dot_rows(weights, values), total)
            sums = jnp.where(lane == head, highest + jnp.log(amount), sums)
        context[pl.ds(first, block), :] = total.astype(jnp.bfloat16)
        context_t[:, pl.ds(first, block)] = total.T.astype(jnp.bfloat16)
        logsum[pl.ds(first, block), :] = sums

    over_blocks(row_len, block, one_block)


def attend_forward(hidden_in, projection, shift, tables, seg_col, seg_row, heads):
    row_len, width = hidden_in.shape[0], projection.shape[0] // 3
    low = jax.ShapeDtypeStruct((row_len, width), jnp.bfloat16)
    return pl.pallas_call(
        functools.partial(forward_kernel, heads),
        in_specs=[IN_VMEM] * 6,
        out_shape=(
            low,
            low,
            low,
            low,
            jax.ShapeDtypeStruct((width, row_len), jnp.bfloat16),
            jax.ShapeDtypeStruct((row_len, 128), jnp.float32),
        ),
        compiler_params=pltpu.CompilerParams(vmem_limit_bytes=ROOM + 4096 * row_len),
        cost_estimate=busy(8.5),
        name="attend_forward",
    )(hidden_in, projection, shift, tables, seg_col, seg_row)


def backward_kernel(
    heads,
    query,
    key,
    value,
    grad_left,
    grad_right,
    out_weight,
    logsum,
    tables,
    seg_col,
    seg_row,
    lines_low,
    lines_low_t,
    bias_grad,
    key_grad,
    value_grad,
):
    row_len, width = query.shape
    block = 256
    scale = HEAD ** (-0.5)
    half = grad_left.shape[1]
    key_grad[...] = jnp.zeros_like(key_grad)
    value_grad[...] = jnp.zeros_like(value_grad)
    bias_grad[...] = jnp.zeros_like(bias_grad)

    def put(part, first, grads):
        low = grads.astype(jnp.bfloat16)
        wide = low.astype(jnp.float32)
        columns = slice(part * width, (part + 1) * width)
        lines_low[pl.ds(first, block), columns] = low
        lines_low_t[columns, pl.ds(first, block)] = wide.T.astype(jnp.bfloat16)
        bias_grad[0:1, columns] += jnp.sum(wide, axis=0, keepdims=True)

    def one_block(first, start, size):
        bias = mask_of(seg_col, seg_row, first, start, block, size)
        here = query[pl.ds(first, block), :]
        here_rows = pl.ds(first, block)
        grad_here = dot_lanes(grad_left[here_rows, :], out_weight[:, 0:half])
        grad_here = grad_here + dot_lanes(grad_right[here_rows, :], out_weight[:, half:])
        grad_here = grad_here.astype(jnp.bfloat16)
        keys = key[pl.ds(start, size), :]
        values = value[pl.ds(start, size), :]
        sums = logsum[pl.ds(first, block), :]
        total = jnp.zeros((block, width), jnp.float32)
        for head in range(heads):
            mine = of_head(head, (block, width))
            asked = jnp.where(mine, here, jnp.bfloat16(0))
            pulled = jnp.where(mine, grad_here, jnp.bfloat16(0))
            scores = dot_lanes(asked, keys) + bias
            probs = jnp.exp(scores - sums[:, head : head + 1])
            prob_grad = dot_lanes(pulled, values)
            value_grad[pl.ds(start, size), :] += dot_tall(probs.astype(jnp.bfloat16), pulled)
            inner = jnp.sum(probs * prob_grad, axis=1, keepdims=True)
            score_low = (probs * (prob_grad - inner)).astype(jnp.bfloat16)
            total = jnp.where(mine, dot_rows(score_low, keys), total)
            key_grad[pl.ds(start, size), :] += dot_tall(score_low, asked)
        here_tables = [tables[part, pl.ds(first, block), :] for part in range(3)]
        put(0, first, turn(total * scale, here_tables, -1.0))

    over_blocks(row_len, block, one_block)
    for index in range(row_len // block):
        first = index * block
        here_tables = [tables[part, pl.ds(first, block), :] for part in range(3)]
        put(1, first, turn(key_grad[pl.ds(first, block), :], here_tables, -1.0))
        put(2, first, value_grad[pl.ds(first, block), :])


def attend_backward(
    query, key, value, grads, out_weight, logsum, tables, seg_col, seg_row, heads
):
    row_len, width = query.shape
    return pl.pallas_call(
        functools.partial(backward_kernel, heads),
        in_specs=[IN_VMEM] * 10,
        out_shape=(
            jax.ShapeDtypeStruct((row_len, 3 * width), jnp.bfloat16),
            jax.ShapeDtypeStruct((3 * width, row_len), jnp.bfloat16),
            jax.ShapeDtypeStruct((8, 3 * width), jnp.float32),
        ),
        scratch_shapes=[
            pltpu.VMEM((row_len, width), jnp.float32),
            pltpu.VMEM((row_len, width), jnp.float32),
        ],
        compiler_params=pltpu.CompilerParams(vmem_limit_bytes=ROOM + 4096 * row_len),
        cost_estimate=busy(13.3),
        name="attend_backward",
    )(query, key, value, *grads, out_weight, logsum, tables, seg_col, seg_row)


def layout(doc_lengths, row_len):
    ends = jnp.cumsum(doc_lengths[0])
    starts = ends - doc_lengths[0]
    places = jnp.arange(row_len, dtype=jnp.int32)
    segment = jnp.sum((places[:, None] >= ends[None, :]).astype(jnp.int32), axis=1)
    chosen = segment[:, None] == jnp.arange(ends.shape[0], dtype=jnp.int32)[None, :]
    first = jnp.sum(jnp.where(chosen, starts[None, :], 0), axis=1)
    return segment, places - first, segment < ends.shape[0] - 1


def turns(position):
    half = ROT // 2
    lane = lax.broadcasted_iota(jnp.int32, (position.shape[0], 128), 1) % HEAD
    freq = 10000.0 ** (-((lane % half).astype(jnp.float32) * (2.0 / ROT)))
    angle = position.astype(jnp.float32)[:, None] * freq
    cosine, sine = jnp.cos(angle), jnp.sin(angle)
    return jnp.stack(
        [
            jnp.where(lane < ROT, cosine, 1.0),
            jnp.where(lane < half, -sine, 0.0),
            jnp.where((lane >= half) & (lane < ROT), sine, 0.0),
        ]
    )


def busy(time):
    return pl.CostEstimate(flops=int(time * 1.5 * 10**9), bytes_accessed=0, transcendentals=0)


def blocks_of(tokens):
    return min(512, tokens)


def gated_kernel(hidden_in, gate_weight, up_weight, gate, up, mixed, mixed_t):
    gate_here = dot_lanes(gate_weight[...], hidden_in[...])
    up_here = dot_lanes(up_weight[...], hidden_in[...])
    gate[...] = gate_here
    up[...] = up_here
    total = gate_here * jax.nn.sigmoid(gate_here) * up_here
    mixed_t[...] = total.astype(jnp.bfloat16)
    mixed[...] = total.T.astype(jnp.bfloat16)


def gated_forward(hidden_in, gate_weight, up_weight):
    (tokens, features), units = hidden_in.shape, gate_weight.shape[0]
    block = blocks_of(tokens)
    tall = pl.BlockSpec((units, block), lambda step: (0, step))
    flat = pl.BlockSpec((block, units), lambda step: (step, 0))
    return pl.pallas_call(
        gated_kernel,
        grid=(tokens // block,),
        in_specs=[pl.BlockSpec((block, features), lambda step: (step, 0)), IN_VMEM, IN_VMEM],
        out_specs=[tall, tall, flat, tall],
        out_shape=[
            jax.ShapeDtypeStruct((units, tokens), jnp.float32),
            jax.ShapeDtypeStruct((units, tokens), jnp.float32),
            jax.ShapeDtypeStruct((tokens, units), jnp.bfloat16),
            jax.ShapeDtypeStruct((units, tokens), jnp.bfloat16),
        ],
        compiler_params=pltpu.CompilerParams(vmem_limit_bytes=ROOM),
        cost_estimate=busy(7.5),
        name="gated_forward",
    )(hidden_in, gate_weight, up_weight)


def gated_back_kernel(
    grad_left, grad_right, down_weight, gate, up, gate_low, gate_low_t, up_low, up_low_t
):
    half = grad_left.shape[1]
    mixed_grad = dot_lanes(down_weight[:, 0:half], grad_left[...])
    mixed_grad = mixed_grad + dot_lanes(down_weight[:, half:], grad_right[...])
    gate_here = gate[...]
    sigmoid = jax.nn.sigmoid(gate_here)
    pulled = mixed_grad * sigmoid
    gate_grad = pulled * up[...] * (1.0 + gate_here * (1.0 - sigmoid))
    up_grad = pulled * gate_here
    gate_low_t[...] = gate_grad.astype(jnp.bfloat16)
    up_low_t[...] = up_grad.astype(jnp.bfloat16)
    gate_low[...] = gate_grad.T.astype(jnp.bfloat16)
    up_low[...] = up_grad.T.astype(jnp.bfloat16)


def gated_backward(grads, down_weight, gate, up):
    (tokens, half), units = grads[0].shape, down_weight.shape[0]
    block = blocks_of(tokens)
    tall = pl.BlockSpec((units, block), lambda step: (0, step))
    flat = pl.BlockSpec((block, units), lambda step: (step, 0))
    wide = jax.ShapeDtypeStruct((tokens, units), jnp.bfloat16)
    long = jax.ShapeDtypeStruct((units, tokens), jnp.bfloat16)
    return pl.pallas_call(
        gated_back_kernel,
        grid=(tokens // block,),
        in_specs=[pl.BlockSpec((block, half), lambda step: (step, 0))] * 2 + [IN_VMEM, tall, tall],
        out_specs=[flat, tall, flat, tall],
        out_shape=[wide, long, wide, long],
        compiler_params=pltpu.CompilerParams(vmem_limit_bytes=ROOM),
        cost_estimate=busy(5.4),
        name="gated_backward",
    )(*grads, down_weight, gate, up)


def merge_kernel(count, *refs):
    total = dot_rows(refs[0][...], refs[count][...])
    for index in range(1, count):
        total = total + dot_rows(refs[index][...], refs[count + index][...])
    refs[2 * count][...] = total.astype(jnp.bfloat16)


def merge(lhs, weights):
    tokens, features, count = lhs[0].shape[0], weights[0].shape[1], len(lhs)
    block = min(256, tokens)
    return pl.pallas_call(
        functools.partial(merge_kernel, count),
        grid=(tokens // block,),
        in_specs=[
            *(pl.BlockSpec((block, part.shape[1]), lambda step: (step, 0)) for part in lhs),
            *([IN_VMEM] * count),
        ],
        out_specs=pl.BlockSpec((block, features), lambda step: (step, 0)),
        out_shape=jax.ShapeDtypeStruct((tokens, features), jnp.bfloat16),
        compiler_params=pltpu.CompilerParams(vmem_limit_bytes=ROOM),
        cost_estimate=busy(8),
        name="merge",
    )(*lhs, *weights)


def stacked(lhs, rhs, first, wide, keep):
    row = 0
    block = rhs[:, pl.ds(pl.multiple_of(first, 128), wide)]
    for part in lhs:
        keep(row, part.shape[0], dot_rows(part[...], block))
        row += part.shape[0]


def send_kernel(count, wide, order, *refs):
    lhs, rhs, outs = refs[:count], refs[count], refs[-2:]
    for half, out in enumerate(outs):

        def keep(row, rows, term, out=out):
            out[row : row + rows, :] = term.astype(jnp.bfloat16)

        stacked(lhs, rhs, order[half], wide, keep)


def join_kernel(count, parts, order, *refs):
    lhs, rhs, came = refs[:count], refs[count : count + parts], refs[count + parts : -5]
    outs, total = refs[-5:-1], refs[-1]
    for half in range(2):
        at, bit = 0, order[parts, half]
        for part in range(parts):
            here = came[2 * part + half]
            wide = here.shape[1]
            narrow = wide // 2

            def keep(row, rows, term, here=here, wide=wide):
                there = here[row : row + rows, :].astype(jnp.float32)
                total[row : row + rows, 0:wide] = (term + there).astype(jnp.bfloat16)

            stacked(lhs, rhs[part], order[part, half], wide, keep)
            for out, which in ((outs[2 * half], 1 - bit), (outs[2 * half + 1], bit)):
                columns = pl.ds(pl.multiple_of(which * narrow, narrow), narrow)
                out[:, at : at + narrow] = total[:, columns]
            at += narrow


def place_kernel(takes, olds, order, *refs):
    count = 1 + max(take[0] for take in takes)
    pieces, outs = refs[:count], refs[count + olds :]
    step = pl.program_id(0)
    for index, (which, row, column) in enumerate(takes):
        piece = pieces[which]

        @pl.when(step == index)
        def _(piece=piece, first=row, column=column):
            for out in outs:
                size, narrow = out.shape
                block = piece[first : first + size, column : column + narrow]
                out[...] = block.astype(jnp.float32)
                first += size


def place(pieces, takes, order, sizes, narrow, features, old):
    return pl.pallas_call(
        functools.partial(place_kernel, takes, len(old)),
        grid_spec=pltpu.PrefetchScalarGridSpec(
            num_scalar_prefetch=1,
            grid=(len(takes),),
            in_specs=[IN_VMEM] * len(pieces) + [pl.BlockSpec(memory_space=pl.ANY)] * len(old),
            out_specs=[
                pl.BlockSpec((size, narrow), lambda step, order: (0, order[step]))
                for size in sizes
            ],
        ),
        out_shape=[jax.ShapeDtypeStruct((size, features), jnp.float32) for size in sizes],
        input_output_aliases={1 + len(pieces) + index: index for index in range(len(old))},
        compiler_params=pltpu.CompilerParams(vmem_limit_bytes=ROOM),
        cost_estimate=busy(sum(sizes) * len(takes) * narrow / 300_000),
        name="place",
    )(jnp.stack(order).astype(jnp.int32), *pieces, *old)


def lay_kernel(where, *refs):
    mine, theirs, out, sems = refs[0:6], refs[6:12], refs[12], refs[13]
    for inner in (0, 1):

        @pl.when(where[5] == inner)
        def _(inner=inner):
            taken = (0, 1, 3 - inner, 5 - inner)
            copies = []
            for place, index in enumerate(taken):
                for side, pieces in enumerate((mine, theirs)):
                    core = where[4] if side == 0 else 1 - where[4]
                    target = out.at[where[place], core]
                    copies.append(
                        pltpu.make_async_copy(pieces[index], target, sems.at[place, side])
                    )
            for copy in copies:
                copy.start()
            for copy in copies:
                copy.wait()


def gather(values):
    line = [(2 * i + c, 2 * (i ^ 1) + c) for i in range(4) for c in range(2)]
    middle = [(2 * i + c, 2 * j + c) for i, j in ((0, 0), (1, 2), (2, 1), (3, 3)) for c in range(2)]
    core = [(i, i ^ 1) for i in range(8)]
    me = lax.axis_index("tp")
    chip = me // 2

    def move(pieces, pairs):
        return lax.ppermute(pieces, "tp", pairs)

    near = move(values, line)
    across = move(values, middle)
    far = move(across, line)
    beyond = move(near, middle)
    last = move(beyond, line)
    mine = [values, near, across, far, beyond, last]
    theirs = [move(pieces, core) for pieces in mine]
    low, inner = chip < 2, (chip == 1) | (chip == 2)
    where = [chip, chip ^ 1, 1 + low, 3 * low, me % 2, inner]
    where = jnp.stack([jnp.asarray(entry, jnp.int32) for entry in where])
    shard, features = values.shape
    out = pl.pallas_call(
        lay_kernel,
        in_specs=[IN_SMEM] + [pl.BlockSpec(memory_space=pl.ANY)] * 12,
        out_specs=pl.BlockSpec(memory_space=pl.ANY),
        out_shape=jax.ShapeDtypeStruct((4, 2, shard, features), values.dtype),
        scratch_shapes=[pltpu.SemaphoreType.DMA((4, 2))],
        compiler_params=pltpu.CompilerParams(vmem_limit_bytes=4 * 2**20),
        cost_estimate=busy(2),
        name="lay",
    )(where, *mine, *theirs)
    return out.reshape(8 * shard, features)


NEAR = [(0, 1), (1, 0), (2, 3), (3, 2)]
FAR = [(0, 2), (2, 0), (1, 3), (3, 1)]
PATHS = ((NEAR, FAR), (FAR, NEAR))


def after(value, *others):
    return lax.optimization_barrier((value, others))[0]


class Sum:
    def __init__(self, lhs, parts, time=0):
        row = lax.axis_index("rows")
        near, far = row % 2, row // 2
        self.bits = ((near, far), (far, near))
        self.lhs, self.parts, self.time = lhs, parts, time
        self.rows, self.sizes = sum(part.shape[0] for part in lhs), [part.shape[0] for part in lhs]
        self.came = []

    def first(self, part, half, bit):
        return part.shape[1] // 8 * (4 * half + 2 * bit)

    def piece(self, wide):
        return jax.ShapeDtypeStruct((self.rows, wide), jnp.bfloat16)

    def room(self):
        return pltpu.CompilerParams(vmem_limit_bytes=ROOM + 2048 * self.lhs[0].shape[1])

    def send(self, part, *earlier):
        rhs = self.parts[part]
        order = jnp.stack([self.first(rhs, half, 1 - self.bits[half][0]) for half in range(2)])
        wide = rhs.shape[1] // 4
        head = after(self.lhs[0], *earlier)
        sent = pl.pallas_call(
            functools.partial(send_kernel, len(self.lhs), wide),
            in_specs=[IN_SMEM] + [IN_VMEM] * (len(self.lhs) + 1),
            out_shape=[self.piece(wide)] * 2,
            compiler_params=self.room(),
            cost_estimate=busy(self.rows * wide / 131072),
            name="send_terms",
        )(order.astype(jnp.int32), head, *self.lhs[1:], rhs)
        self.came += [lax.ppermute(sent[half], "rows", PATHS[half][0]) for half in range(2)]
        return sent

    def join(self, *earlier):
        order = [[self.first(part, half, self.bits[half][0]) for half in range(2)] for part in self.parts]
        order.append([self.bits[0][1], self.bits[1][1]])
        wide = sum(part.shape[1] // 8 for part in self.parts)
        head = after(self.lhs[0], *earlier)
        outs = pl.pallas_call(
            functools.partial(join_kernel, len(self.lhs), len(self.parts)),
            in_specs=[IN_SMEM] + [IN_VMEM] * (len(self.lhs) + 3 * len(self.parts)),
            out_shape=[self.piece(wide)] * 4,
            scratch_shapes=[pltpu.VMEM((self.rows, 2 * wide), jnp.bfloat16)],
            compiler_params=self.room(),
            cost_estimate=busy(self.time if self.time else self.rows / 256),
            name="join_terms",
        )(jnp.array(order).astype(jnp.int32), head, *self.lhs[1:], *self.parts, *self.came)
        self.mine = [outs[1], outs[3]]
        self.came = [lax.ppermute(outs[2 * half], "rows", PATHS[half][1]) for half in range(2)]
        return outs

    def total(self, *earlier):
        mine = lax.optimization_barrier((*self.mine, *earlier))[:2]
        self.mine = [mine[half] + self.came[half] for half in range(2)]
        self.across = [lax.ppermute(self.mine[half], "rows", PATHS[half][1]) for half in range(2)]
        return self.mine

    def share(self, *earlier):
        mine = lax.optimization_barrier((*self.mine, *earlier))[:2]
        both = [jnp.concatenate([mine[half], self.across[half]]) for half in range(2)]
        self.last = [lax.ppermute(both[half], "rows", PATHS[half][0]) for half in range(2)]
        return both

    def place(self, pieces, kinds, old, *earlier):
        features = sum(part.shape[1] for part in self.parts)
        narrow = min(part.shape[1] // 8 for part in self.parts)
        takes, order = [], []
        for pair, places in enumerate(kinds):
            for half in range(2):
                a, b = self.bits[half]
                for index, (first, second) in enumerate(places):
                    block = 4 * half + 2 * jnp.abs(a - first) + jnp.abs(b - second)
                    for part in range(len(self.parts)):
                        takes.append((2 * pair + half, index * self.rows, part * narrow))
                        order.append(8 * part + block)
        pieces = lax.optimization_barrier((*pieces, *earlier))[: len(pieces)]
        return place(pieces, takes, order, self.sizes, narrow, features, old)

    def place_early(self, *earlier):
        pieces = [*self.mine, *self.across]
        return self.place(pieces, [[(0, 0)], [(0, 1)]], (), *earlier)

    def place_last(self, old, *earlier):
        return self.place(self.last, [[(1, 0), (1, 1)]], old, *earlier)


def sum_everywhere(values, axis):
    size, step = lax.axis_size(axis), 1
    while step < size:
        values = values + lax.ppermute(values, axis, [(i, i ^ step) for i in range(size)])
        step *= 2
    return values


def standardize(values):
    centre = jnp.mean(values, axis=1, keepdims=True)
    centred = values - centre
    spread = jnp.mean(centred * centred, axis=1, keepdims=True)
    inverse = lax.rsqrt(spread + EPSILON)
    return (centred * inverse, inverse)


def widen(weight, width):
    return jnp.pad(weight, ((0, 0), (0, width - weight.shape[1]), (0, 0)))


def per_device(
    block_input,
    norm_gain,
    norm_bias,
    qkv_weight,
    qkv_bias,
    out_weight,
    gate_weight,
    up_weight,
    down_weight,
    cotangent,
    doc_lengths,
):
    shard, features = block_input.shape
    group = lax.axis_size("tp")
    tokens = shard * group
    width = qkv_weight.shape[1]
    heads = width // HEAD
    padded = max(width, 128)
    me = lax.axis_index("tp")
    segment, position, live = layout(doc_lengths, tokens)
    live_mine = lax.dynamic_slice_in_dim(live, me * shard, shard)[:, None]
    input_wide = block_input.astype(jnp.float32)
    gain = norm_gain.astype(jnp.float32)
    shift = norm_bias.astype(jnp.float32)
    normed, inverse = standardize(input_wide)
    normed_low = (normed * gain + shift).astype(jnp.bfloat16)
    hidden_in = lax.all_gather(normed_low, "tp", axis=0, tiled=True)
    grad_mine = jnp.where(live_mine, cotangent, jnp.zeros_like(cotangent))
    half = features // 2
    if group == 8:
        grad_left = gather(grad_mine[:, :half])
        hidden_in = after(hidden_in, grad_left)
    else:
        grad_left = lax.all_gather(after(grad_mine[:, :half], hidden_in), "tp", axis=0, tiled=True)
    grad_right = lax.all_gather(after(grad_mine[:, half:], hidden_in), "tp", axis=0, tiled=True)
    tables = turns(position)
    seg_col = jnp.broadcast_to(segment[:, None], (tokens, 128))
    seg_row = jnp.broadcast_to(segment[None, :], (8, tokens))

    projection = widen(qkv_weight, padded).reshape(3 * padded, features)
    shift_lines = widen(qkv_bias[..., None], padded).reshape(1, 3 * padded).astype(jnp.float32)
    out_wide = widen(out_weight[None], padded)[0]
    gate, up, mixed, mixed_t = gated_forward(hidden_in, gate_weight, up_weight)
    query, key, value, context, context_t, logsum = attend_forward(
        after(hidden_in, mixed), projection, shift_lines, tables, seg_col, seg_row, heads
    )
    merged = merge([context, mixed], [out_wide, down_weight])
    wide_sum = Sum([mixed_t, context_t], [grad_left, grad_right])
    order = wide_sum.send(0)
    order = wide_sum.send(1, order)
    gate_low, gate_low_t, up_low, up_low_t = gated_backward(
        [grad_left, after(grad_right, order)], down_weight, gate, up
    )
    inner_sum = Sum([gate_low_t, up_low_t], [hidden_in], LONG)
    order = inner_sum.send(0)
    order = wide_sum.join(order)
    lines_low, lines_low_t, bias_grad = attend_backward(
        query,
        key,
        value,
        [grad_left, after(grad_right, order)],
        out_wide,
        logsum,
        tables,
        seg_col,
        seg_row,
        heads,
    )
    bias_grad = bias_grad[0].reshape(3, padded)[:, :width]
    outer_sum = Sum([lines_low_t], [hidden_in], LONG)
    term = merge([gate_low, up_low, lines_low], [gate_weight, up_weight, projection])
    order = wide_sum.total(term)
    order = inner_sum.join(order)
    order = wide_sum.share(order)
    order = outer_sum.send(0, order)
    old = wide_sum.place_early(order)
    down_grad, out_grad = wide_sum.place_last(old)
    order = inner_sum.total(down_grad)
    order = outer_sum.join(order)
    order = inner_sum.share(order)
    order = outer_sum.total(order)
    order = outer_sum.share(order)
    normed_grad = lax.psum_scatter(term, "tp", scatter_dimension=0, tiled=True).astype(jnp.float32)
    sums = jnp.concatenate([jnp.sum(normed_grad * normed, axis=0), jnp.sum(normed_grad, axis=0)])
    merged = lax.psum_scatter(merged, "tp", scatter_dimension=0, tiled=True)
    merged = merged.astype(jnp.float32)
    output = (input_wide + jnp.where(live_mine, merged, 0.0)).astype(jnp.bfloat16)
    scaled = normed_grad * gain
    input_grad = inverse * (
        scaled
        - jnp.mean(scaled, axis=1, keepdims=True)
        - normed * jnp.mean(scaled * normed, axis=1, keepdims=True)
    )
    input_grad = input_grad + cotangent.astype(jnp.float32)
    inner_old = inner_sum.place_early(order, output, input_grad)
    outer_old = outer_sum.place_early(inner_old)
    sums = sum_everywhere(after(sums, outer_old), "tp")
    gate_grad, up_grad = inner_sum.place_last(inner_old, sums)
    sums = sum_everywhere(jnp.concatenate([sums, bias_grad.reshape(-1)]), "rows")
    (qkv_grad,) = outer_sum.place_last(outer_old, gate_grad)
    return (
        output,
        input_grad,
        sums[:features],
        sums[features : 2 * features],
        qkv_grad.reshape(3, padded, features)[:, :width],
        sums[2 * features :].reshape(3, width),
        out_grad[:width],
        gate_grad,
        up_grad,
        down_grad,
    )


def solution(mesh):
    placed = (
        P(("rows", "tp"), None),
        P(),
        P(),
        P(None, "tp", None),
        P(None, "tp"),
        P("tp", None),
        P("tp", None),
        P("tp", None),
        P("tp", None),
        P(("rows", "tp"), None),
        P("rows", None),
    )
    return jax.shard_map(
        per_device,
        mesh=mesh,
        in_specs=placed,
        out_specs=(
            P(("rows", "tp"), None),
            P(("rows", "tp"), None),
            P(),
            P(),
            P(None, "tp", None),
            P(None, "tp"),
            P("tp", None),
            P("tp", None),
            P("tp", None),
            P("tp", None),
        ),
        check_vma=False,
    )
```

```python
import functools
import jax
import jax.numpy as jnp
from jax import lax
from jax.experimental import pallas as pl
from jax.experimental.pallas import tpu as pltpu
from jax.sharding import PartitionSpec as P

HEAD = 64
ROT = 16
MASKED = -1e30
LONG = 1000
EPSILON = 1e-05
ROOM = 16 * 2**20
IN_VMEM = pl.BlockSpec(memory_space=pltpu.VMEM)
IN_SMEM = pl.BlockSpec(memory_space=pltpu.SMEM)


def dot_rows(a, b):
    return lax.dot_general(a, b, (((1,), (0,)), ((), ())), preferred_element_type=jnp.float32)


def dot_lanes(a, b):
    return lax.dot_general(a, b, (((1,), (1,)), ((), ())), preferred_element_type=jnp.float32)


def dot_tall(a, b):
    return lax.dot_general(a, b, (((0,), (0,)), ((), ())), preferred_element_type=jnp.float32)


def turn(values, tables, sign):
    half = ROT // 2
    width = values.shape[1]
    tables = [jnp.concatenate([part] * (width // 128), axis=1) for part in tables]
    up = pltpu.roll(values, width - half, 1)
    down = pltpu.roll(values, half, 1)
    return values * tables[0] + sign * (up * tables[1] + down * tables[2])


def of_head(head, shape):
    return lax.broadcasted_iota(jnp.int32, shape, 1) // HEAD == head


def over_blocks(row_len, block, body):
    longest = row_len // 2
    blocks = row_len // block
    if blocks <= 8:
        for index in range(blocks):
            first = index * block
            start = max(0, first + block - (longest + block))
            body(first, start, first + block - start)
    else:
        size = longest + block

        def step(index, carry):
            first = pl.multiple_of(index * block, block)
            start = pl.multiple_of(jnp.maximum(first - longest, 0), block)
            body(first, start, size)
            return carry

        lax.fori_loop(0, blocks, step, 0)


def mask_of(seg_col, seg_row, first, start, block, size):
    rows = first + lax.broadcasted_iota(jnp.int32, (block, size), 0)
    keys = start + lax.broadcasted_iota(jnp.int32, (block, size), 1)
    same = seg_col[pl.ds(first, block), 0:1] == seg_row[0:1, pl.ds(start, size)]
    return jnp.where(same & (keys <= rows), 0.0, MASKED)


def forward_kernel(
    heads,
    hidden_in,
    projection,
    shift,
    tables,
    seg_col,
    seg_row,
    query,
    key,
    value,
    context,
    context_t,
    logsum,
):
    row_len, width = query.shape
    block = 256
    scale = HEAD ** (-0.5)
    for first in range(0, row_len, block):
        here = slice(first, first + block)
        lines = dot_lanes(hidden_in[here, :], projection[...]) + shift[...]
        turning = [tables[part, here, :] for part in range(3)]
        asked = turn(lines[:, 0:width], turning, 1.0).astype(jnp.bfloat16)
        query[here, :] = asked * jnp.bfloat16(scale)
        key[here, :] = turn(lines[:, width : 2 * width], turning, 1.0).astype(jnp.bfloat16)
        value[here, :] = lines[:, 2 * width : 3 * width].astype(jnp.bfloat16)

    def one_block(first, start, size):
        bias = mask_of(seg_col, seg_row, first, start, block, size)
        here = query[pl.ds(first, block), :]
        keys = key[pl.ds(start, size), :]
        values = value[pl.ds(start, size), :]
        total = jnp.zeros((block, width), jnp.float32)
        lane = lax.broadcasted_iota(jnp.int32, (block, 128), 1)
        sums = jnp.zeros((block, 128), jnp.float32)
        for head in range(heads):
            mine = of_head(head, (block, width))
            scores = dot_lanes(jnp.where(mine, here, jnp.bfloat16(0)), keys) + bias
            highest = jnp.max(scores, axis=1, keepdims=True)
            raised = jnp.exp(scores - highest)
            amount = jnp.sum(raised, axis=1, keepdims=True)
            weights = (raised * (1.0 / amount)).astype(jnp.bfloat16)
            total = jnp.where(mine, dot_rows(weights, values), total)
            sums = jnp.where(lane == head, highest + jnp.log(amount), sums)
        context[pl.ds(first, block), :] = total.astype(jnp.bfloat16)
        context_t[:, pl.ds(first, block)] = total.T.astype(jnp.bfloat16)
        logsum[pl.ds(first, block), :] = sums

    over_blocks(row_len, block, one_block)


def attend_forward(hidden_in, projection, shift, tables, seg_col, seg_row, heads):
    row_len, width = hidden_in.shape[0], projection.shape[0] // 3
    low = jax.ShapeDtypeStruct((row_len, width), jnp.bfloat16)
    return pl.pallas_call(
        functools.partial(forward_kernel, heads),
        in_specs=[IN_VMEM] * 6,
        out_shape=(
            low,
            low,
            low,
            low,
            jax.ShapeDtypeStruct((width, row_len), jnp.bfloat16),
            jax.ShapeDtypeStruct((row_len, 128), jnp.float32),
        ),
        compiler_params=pltpu.CompilerParams(vmem_limit_bytes=ROOM + 4096 * row_len),
        cost_estimate=busy(8.5),
        name="attend_forward",
    )(hidden_in, projection, shift, tables, seg_col, seg_row)


def backward_kernel(
    heads,
    query,
    key,
    value,
    grad_left,
    grad_right,
    out_weight,
    logsum,
    tables,
    seg_col,
    seg_row,
    lines_low,
    lines_low_t,
    bias_grad,
    key_grad,
    value_grad,
):
    row_len, width = query.shape
    block = 256
    scale = HEAD ** (-0.5)
    half = grad_left.shape[1]
    key_grad[...] = jnp.zeros_like(key_grad)
    value_grad[...] = jnp.zeros_like(value_grad)
    bias_grad[...] = jnp.zeros_like(bias_grad)

    def put(part, first, grads):
        low = grads.astype(jnp.bfloat16)
        wide = low.astype(jnp.float32)
        columns = slice(part * width, (part + 1) * width)
        lines_low[pl.ds(first, block), columns] = low
        lines_low_t[columns, pl.ds(first, block)] = wide.T.astype(jnp.bfloat16)
        bias_grad[0:1, columns] += jnp.sum(wide, axis=0, keepdims=True)

    def one_block(first, start, size):
        bias = mask_of(seg_col, seg_row, first, start, block, size)
        here = query[pl.ds(first, block), :]
        here_rows = pl.ds(first, block)
        grad_here = dot_lanes(grad_left[here_rows, :], out_weight[:, 0:half])
        grad_here = grad_here + dot_lanes(grad_right[here_rows, :], out_weight[:, half:])
        grad_here = grad_here.astype(jnp.bfloat16)
        keys = key[pl.ds(start, size), :]
        values = value[pl.ds(start, size), :]
        sums = logsum[pl.ds(first, block), :]
        total = jnp.zeros((block, width), jnp.float32)
        for head in range(heads):
            mine = of_head(head, (block, width))
            asked = jnp.where(mine, here, jnp.bfloat16(0))
            pulled = jnp.where(mine, grad_here, jnp.bfloat16(0))
            scores = dot_lanes(asked, keys) + bias
            probs = jnp.exp(scores - sums[:, head : head + 1])
            prob_grad = dot_lanes(pulled, values)
            value_grad[pl.ds(start, size), :] += dot_tall(probs.astype(jnp.bfloat16), pulled)
            inner = jnp.sum(probs * prob_grad, axis=1, keepdims=True)
            score_low = (probs * (prob_grad - inner)).astype(jnp.bfloat16)
            total = jnp.where(mine, dot_rows(score_low, keys), total)
            key_grad[pl.ds(start, size), :] += dot_tall(score_low, asked)
        here_tables = [tables[part, pl.ds(first, block), :] for part in range(3)]
        put(0, first, turn(total * scale, here_tables, -1.0))

    over_blocks(row_len, block, one_block)
    for index in range(row_len // block):
        first = index * block
        here_tables = [tables[part, pl.ds(first, block), :] for part in range(3)]
        put(1, first, turn(key_grad[pl.ds(first, block), :], here_tables, -1.0))
        put(2, first, value_grad[pl.ds(first, block), :])


def attend_backward(
    query, key, value, grads, out_weight, logsum, tables, seg_col, seg_row, heads
):
    row_len, width = query.shape
    return pl.pallas_call(
        functools.partial(backward_kernel, heads),
        in_specs=[IN_VMEM] * 10,
        out_shape=(
            jax.ShapeDtypeStruct((row_len, 3 * width), jnp.bfloat16),
            jax.ShapeDtypeStruct((3 * width, row_len), jnp.bfloat16),
            jax.ShapeDtypeStruct((8, 3 * width), jnp.float32),
        ),
        scratch_shapes=[
            pltpu.VMEM((row_len, width), jnp.float32),
            pltpu.VMEM((row_len, width), jnp.float32),
        ],
        compiler_params=pltpu.CompilerParams(vmem_limit_bytes=ROOM + 4096 * row_len),
        cost_estimate=busy(13.3),
        name="attend_backward",
    )(query, key, value, *grads, out_weight, logsum, tables, seg_col, seg_row)


def layout(doc_lengths, row_len):
    ends = jnp.cumsum(doc_lengths[0])
    starts = ends - doc_lengths[0]
    places = jnp.arange(row_len, dtype=jnp.int32)
    segment = jnp.sum((places[:, None] >= ends[None, :]).astype(jnp.int32), axis=1)
    chosen = segment[:, None] == jnp.arange(ends.shape[0], dtype=jnp.int32)[None, :]
    first = jnp.sum(jnp.where(chosen, starts[None, :], 0), axis=1)
    return segment, places - first, segment < ends.shape[0] - 1


def turns(position):
    half = ROT // 2
    lane = lax.broadcasted_iota(jnp.int32, (position.shape[0], 128), 1) % HEAD
    freq = 10000.0 ** (-((lane % half).astype(jnp.float32) * (2.0 / ROT)))
    angle = position.astype(jnp.float32)[:, None] * freq
    cosine, sine = jnp.cos(angle), jnp.sin(angle)
    return jnp.stack(
        [
            jnp.where(lane < ROT, cosine, 1.0),
            jnp.where(lane < half, -sine, 0.0),
            jnp.where((lane >= half) & (lane < ROT), sine, 0.0),
        ]
    )


def busy(time):
    return pl.CostEstimate(flops=int(time * 1.5 * 10**9), bytes_accessed=0, transcendentals=0)


def blocks_of(tokens):
    return min(512, tokens)


def gated_kernel(hidden_in, gate_weight, up_weight, gate, up, mixed, mixed_t):
    gate_here = dot_lanes(gate_weight[...], hidden_in[...])
    up_here = dot_lanes(up_weight[...], hidden_in[...])
    gate[...] = gate_here
    up[...] = up_here
    total = gate_here * jax.nn.sigmoid(gate_here) * up_here
    mixed_t[...] = total.astype(jnp.bfloat16)
    mixed[...] = total.T.astype(jnp.bfloat16)


def gated_forward(hidden_in, gate_weight, up_weight):
    (tokens, features), units = hidden_in.shape, gate_weight.shape[0]
    block = blocks_of(tokens)
    tall = pl.BlockSpec((units, block), lambda step: (0, step))
    flat = pl.BlockSpec((block, units), lambda step: (step, 0))
    return pl.pallas_call(
        gated_kernel,
        grid=(tokens // block,),
        in_specs=[pl.BlockSpec((block, features), lambda step: (step, 0)), IN_VMEM, IN_VMEM],
        out_specs=[tall, tall, flat, tall],
        out_shape=[
            jax.ShapeDtypeStruct((units, tokens), jnp.float32),
            jax.ShapeDtypeStruct((units, tokens), jnp.float32),
            jax.ShapeDtypeStruct((tokens, units), jnp.bfloat16),
            jax.ShapeDtypeStruct((units, tokens), jnp.bfloat16),
        ],
        compiler_params=pltpu.CompilerParams(vmem_limit_bytes=ROOM),
        cost_estimate=busy(7.5),
        name="gated_forward",
    )(hidden_in, gate_weight, up_weight)


def gated_back_kernel(
    grad_left, grad_right, down_weight, gate, up, gate_low, gate_low_t, up_low, up_low_t
):
    half = grad_left.shape[1]
    mixed_grad = dot_lanes(down_weight[:, 0:half], grad_left[...])
    mixed_grad = mixed_grad + dot_lanes(down_weight[:, half:], grad_right[...])
    gate_here = gate[...]
    sigmoid = jax.nn.sigmoid(gate_here)
    pulled = mixed_grad * sigmoid
    gate_grad = pulled * up[...] * (1.0 + gate_here * (1.0 - sigmoid))
    up_grad = pulled * gate_here
    gate_low_t[...] = gate_grad.astype(jnp.bfloat16)
    up_low_t[...] = up_grad.astype(jnp.bfloat16)
    gate_low[...] = gate_grad.T.astype(jnp.bfloat16)
    up_low[...] = up_grad.T.astype(jnp.bfloat16)


def gated_backward(grads, down_weight, gate, up):
    (tokens, half), units = grads[0].shape, down_weight.shape[0]
    block = blocks_of(tokens)
    tall = pl.BlockSpec((units, block), lambda step: (0, step))
    flat = pl.BlockSpec((block, units), lambda step: (step, 0))
    wide = jax.ShapeDtypeStruct((tokens, units), jnp.bfloat16)
    long = jax.ShapeDtypeStruct((units, tokens), jnp.bfloat16)
    return pl.pallas_call(
        gated_back_kernel,
        grid=(tokens // block,),
        in_specs=[pl.BlockSpec((block, half), lambda step: (step, 0))] * 2 + [IN_VMEM, tall, tall],
        out_specs=[flat, tall, flat, tall],
        out_shape=[wide, long, wide, long],
        compiler_params=pltpu.CompilerParams(vmem_limit_bytes=ROOM),
        cost_estimate=busy(5.4),
        name="gated_backward",
    )(*grads, down_weight, gate, up)


def merge_kernel(count, *refs):
    total = dot_rows(refs[0][...], refs[count][...])
    for index in range(1, count):
        total = total + dot_rows(refs[index][...], refs[count + index][...])
    refs[2 * count][...] = total.astype(jnp.bfloat16)


def merge(lhs, weights):
    tokens, features, count = lhs[0].shape[0], weights[0].shape[1], len(lhs)
    block = min(256, tokens)
    return pl.pallas_call(
        functools.partial(merge_kernel, count),
        grid=(tokens // block,),
        in_specs=[
            *(pl.BlockSpec((block, part.shape[1]), lambda step: (step, 0)) for part in lhs),
            *([IN_VMEM] * count),
        ],
        out_specs=pl.BlockSpec((block, features), lambda step: (step, 0)),
        out_shape=jax.ShapeDtypeStruct((tokens, features), jnp.bfloat16),
        compiler_params=pltpu.CompilerParams(vmem_limit_bytes=ROOM),
        cost_estimate=busy(8),
        name="merge",
    )(*lhs, *weights)


def stacked(lhs, rhs, first, wide, keep):
    row = 0
    block = rhs[:, pl.ds(pl.multiple_of(first, 128), wide)]
    for part in lhs:
        keep(row, part.shape[0], dot_rows(part[...], block))
        row += part.shape[0]


def send_kernel(count, wide, order, *refs):
    lhs, rhs, outs = refs[:count], refs[count], refs[-2:]
    for half, out in enumerate(outs):

        def keep(row, rows, term, out=out):
            out[row : row + rows, :] = term.astype(jnp.bfloat16)

        stacked(lhs, rhs, order[half], wide, keep)


def join_kernel(count, parts, order, *refs):
    lhs, rhs, came = refs[:count], refs[count : count + parts], refs[count + parts : -5]
    outs, total = refs[-5:-1], refs[-1]
    for half in range(2):
        at, bit = 0, order[parts, half]
        for part in range(parts):
            here = came[2 * part + half]
            wide = here.shape[1]
            narrow = wide // 2

            def keep(row, rows, term, here=here, wide=wide):
                there = here[row : row + rows, :].astype(jnp.float32)
                total[row : row + rows, 0:wide] = (term + there).astype(jnp.bfloat16)

            stacked(lhs, rhs[part], order[part, half], wide, keep)
            for out, which in ((outs[2 * half], 1 - bit), (outs[2 * half + 1], bit)):
                columns = pl.ds(pl.multiple_of(which * narrow, narrow), narrow)
                out[:, at : at + narrow] = total[:, columns]
            at += narrow


def place_kernel(takes, olds, order, *refs):
    count = 1 + max(take[0] for take in takes)
    pieces, outs = refs[:count], refs[count + olds :]
    step = pl.program_id(0)
    for index, (which, row, column) in enumerate(takes):
        piece = pieces[which]

        @pl.when(step == index)
        def _(piece=piece, first=row, column=column):
            for out in outs:
                size, narrow = out.shape
                block = piece[first : first + size, column : column + narrow]
                out[...] = block.astype(jnp.float32)
                first += size


def place(pieces, takes, order, sizes, narrow, features, old):
    return pl.pallas_call(
        functools.partial(place_kernel, takes, len(old)),
        grid_spec=pltpu.PrefetchScalarGridSpec(
            num_scalar_prefetch=1,
            grid=(len(takes),),
            in_specs=[IN_VMEM] * len(pieces) + [pl.BlockSpec(memory_space=pl.ANY)] * len(old),
            out_specs=[
                pl.BlockSpec((size, narrow), lambda step, order: (0, order[step]))
                for size in sizes
            ],
        ),
        out_shape=[jax.ShapeDtypeStruct((size, features), jnp.float32) for size in sizes],
        input_output_aliases={1 + len(pieces) + index: index for index in range(len(old))},
        compiler_params=pltpu.CompilerParams(vmem_limit_bytes=ROOM),
        cost_estimate=busy(sum(sizes) * len(takes) * narrow / 300_000),
        name="place",
    )(jnp.stack(order).astype(jnp.int32), *pieces, *old)


def lay_kernel(where, *refs):
    mine, theirs, out, sems = refs[0:6], refs[6:12], refs[12], refs[13]
    for inner in (0, 1):

        @pl.when(where[5] == inner)
        def _(inner=inner):
            taken = (0, 1, 3 - inner, 5 - inner)
            copies = []
            for place, index in enumerate(taken):
                for side, pieces in enumerate((mine, theirs)):
                    core = where[4] if side == 0 else 1 - where[4]
                    target = out.at[where[place], core]
                    copies.append(
                        pltpu.make_async_copy(pieces[index], target, sems.at[place, side])
                    )
            for copy in copies:
                copy.start()
            for copy in copies:
                copy.wait()


def gather(values):
    line = [(2 * i + c, 2 * (i ^ 1) + c) for i in range(4) for c in range(2)]
    middle = [(2 * i + c, 2 * j + c) for i, j in ((0, 0), (1, 2), (2, 1), (3, 3)) for c in range(2)]
    core = [(i, i ^ 1) for i in range(8)]
    me = lax.axis_index("tp")
    chip = me // 2

    def move(pieces, pairs):
        return lax.ppermute(pieces, "tp", pairs)

    near = move(values, line)
    across = move(values, middle)
    far = move(across, line)
    beyond = move(near, middle)
    last = move(beyond, line)
    mine = [values, near, across, far, beyond, last]
    theirs = [move(pieces, core) for pieces in mine]
    low, inner = chip < 2, (chip == 1) | (chip == 2)
    where = [chip, chip ^ 1, 1 + low, 3 * low, me % 2, inner]
    where = jnp.stack([jnp.asarray(entry, jnp.int32) for entry in where])
    shard, features = values.shape
    out = pl.pallas_call(
        lay_kernel,
        in_specs=[IN_SMEM] + [pl.BlockSpec(memory_space=pl.ANY)] * 12,
        out_specs=pl.BlockSpec(memory_space=pl.ANY),
        out_shape=jax.ShapeDtypeStruct((4, 2, shard, features), values.dtype),
        scratch_shapes=[pltpu.SemaphoreType.DMA((4, 2))],
        compiler_params=pltpu.CompilerParams(vmem_limit_bytes=4 * 2**20),
        cost_estimate=busy(2),
        name="lay",
    )(where, *mine, *theirs)
    return out.reshape(8 * shard, features)


NEAR = [(0, 1), (1, 0), (2, 3), (3, 2)]
FAR = [(0, 2), (2, 0), (1, 3), (3, 1)]
PATHS = ((NEAR, FAR), (FAR, NEAR))


def after(value, *others):
    return lax.optimization_barrier((value, others))[0]


class Sum:
    def __init__(self, lhs, parts, time=0):
        row = lax.axis_index("rows")
        near, far = row % 2, row // 2
        self.bits = ((near, far), (far, near))
        self.lhs, self.parts, self.time = lhs, parts, time
        self.rows, self.sizes = sum(part.shape[0] for part in lhs), [part.shape[0] for part in lhs]
        self.came = []

    def first(self, part, half, bit):
        return part.shape[1] // 8 * (4 * half + 2 * bit)

    def piece(self, wide):
        return jax.ShapeDtypeStruct((self.rows, wide), jnp.bfloat16)

    def room(self):
        return pltpu.CompilerParams(vmem_limit_bytes=ROOM + 2048 * self.lhs[0].shape[1])

    def send(self, part, *earlier):
        rhs = self.parts[part]
        order = jnp.stack([self.first(rhs, half, 1 - self.bits[half][0]) for half in range(2)])
        wide = rhs.shape[1] // 4
        head = after(self.lhs[0], *earlier)
        sent = pl.pallas_call(
            functools.partial(send_kernel, len(self.lhs), wide),
            in_specs=[IN_SMEM] + [IN_VMEM] * (len(self.lhs) + 1),
            out_shape=[self.piece(wide)] * 2,
            compiler_params=self.room(),
            cost_estimate=busy(self.rows * wide / 131072),
            name="send_terms",
        )(order.astype(jnp.int32), head, *self.lhs[1:], rhs)
        self.came += [lax.ppermute(sent[half], "rows", PATHS[half][0]) for half in range(2)]
        return sent

    def join(self, *earlier):
        order = [[self.first(part, half, self.bits[half][0]) for half in range(2)] for part in self.parts]
        order.append([self.bits[0][1], self.bits[1][1]])
        wide = sum(part.shape[1] // 8 for part in self.parts)
        head = after(self.lhs[0], *earlier)
        outs = pl.pallas_call(
            functools.partial(join_kernel, len(self.lhs), len(self.parts)),
            in_specs=[IN_SMEM] + [IN_VMEM] * (len(self.lhs) + 3 * len(self.parts)),
            out_shape=[self.piece(wide)] * 4,
            scratch_shapes=[pltpu.VMEM((self.rows, 2 * wide), jnp.bfloat16)],
            compiler_params=self.room(),
            cost_estimate=busy(self.time if self.time else self.rows / 256),
            name="join_terms",
        )(jnp.array(order).astype(jnp.int32), head, *self.lhs[1:], *self.parts, *self.came)
        self.mine = [outs[1], outs[3]]
        self.came = [lax.ppermute(outs[2 * half], "rows", PATHS[half][1]) for half in range(2)]
        return outs

    def total(self, *earlier):
        mine = lax.optimization_barrier((*self.mine, *earlier))[:2]
        self.mine = [mine[half] + self.came[half] for half in range(2)]
        self.across = [lax.ppermute(self.mine[half], "rows", PATHS[half][1]) for half in range(2)]
        return self.mine

    def share(self, *earlier):
        mine = lax.optimization_barrier((*self.mine, *earlier))[:2]
        both = [jnp.concatenate([mine[half], self.across[half]]) for half in range(2)]
        self.last = [lax.ppermute(both[half], "rows", PATHS[half][0]) for half in range(2)]
        return both

    def place(self, pieces, kinds, old, *earlier):
        features = sum(part.shape[1] for part in self.parts)
        narrow = min(part.shape[1] // 8 for part in self.parts)
        takes, order = [], []
        for pair, places in enumerate(kinds):
            for half in range(2):
                a, b = self.bits[half]
                for index, (first, second) in enumerate(places):
                    block = 4 * half + 2 * jnp.abs(a - first) + jnp.abs(b - second)
                    for part in range(len(self.parts)):
                        takes.append((2 * pair + half, index * self.rows, part * narrow))
                        order.append(8 * part + block)
        pieces = lax.optimization_barrier((*pieces, *earlier))[: len(pieces)]
        return place(pieces, takes, order, self.sizes, narrow, features, old)

    def place_early(self, *earlier):
        pieces = [*self.mine, *self.across]
        return self.place(pieces, [[(0, 0)], [(0, 1)]], (), *earlier)

    def place_last(self, old, *earlier):
        return self.place(self.last, [[(1, 0), (1, 1)]], old, *earlier)


def sum_everywhere(values, axis):
    size, step = lax.axis_size(axis), 1
    while step < size:
        values = values + lax.ppermute(values, axis, [(i, i ^ step) for i in range(size)])
        step *= 2
    return values


def norm_kernel(
    place, lengths, values, gain, shift, cotangent, normed, inverse, hidden, left, right
):
    wide = values[...].astype(jnp.float32)
    centred = wide - jnp.mean(wide, axis=1, keepdims=True)
    spread = jnp.mean(centred * centred, axis=1, keepdims=True)
    scale = lax.rsqrt(spread + EPSILON)
    units = centred * scale
    normed[...] = units
    inverse[...] = jnp.broadcast_to(scale, inverse.shape)
    low = units * gain[...].astype(jnp.float32) + shift[...].astype(jnp.float32)
    hidden[...] = low.astype(jnp.bfloat16)
    alive = -place[0]
    for piece in range(lengths.shape[1] - 1):
        alive = alive + lengths[0, piece]
    rows = lax.broadcasted_iota(jnp.int32, wide.shape, 0)
    grads = jnp.where(rows < alive, cotangent[...].astype(jnp.float32), 0.0).astype(jnp.bfloat16)
    half = wide.shape[1] // 2
    left[...] = grads[:, 0:half]
    right[...] = grads[:, half:]


def norm(place, lengths, values, gain, shift, cotangent):
    shard, features = values.shape
    part = jax.ShapeDtypeStruct((shard, features // 2), jnp.bfloat16)
    return pl.pallas_call(
        norm_kernel,
        in_specs=[IN_SMEM] * 2 + [pl.BlockSpec()] * 4,
        out_shape=[
            jax.ShapeDtypeStruct((shard, features), jnp.float32),
            jax.ShapeDtypeStruct((shard, 128), jnp.float32),
            jax.ShapeDtypeStruct((shard, features), jnp.bfloat16),
            part,
            part,
        ],
        compiler_params=pltpu.CompilerParams(vmem_limit_bytes=ROOM),
        cost_estimate=busy(2),
        name="norm",
    )(place, lengths, values, gain[None], shift[None], cotangent)


def widen(weight, width):
    return jnp.pad(weight, ((0, 0), (0, width - weight.shape[1]), (0, 0)))


def per_device(
    block_input,
    norm_gain,
    norm_bias,
    qkv_weight,
    qkv_bias,
    out_weight,
    gate_weight,
    up_weight,
    down_weight,
    cotangent,
    doc_lengths,
):
    shard, features = block_input.shape
    group = lax.axis_size("tp")
    tokens = shard * group
    width = qkv_weight.shape[1]
    heads = width // HEAD
    padded = max(width, 128)
    me = lax.axis_index("tp")
    segment, position, live = layout(doc_lengths, tokens)
    first = me * shard
    normed, inverse, normed_low, left_mine, right_mine = norm(
        first[None].astype(jnp.int32), doc_lengths, block_input, norm_gain, norm_bias, cotangent
    )
    hidden_in = lax.all_gather(normed_low, "tp", axis=0, tiled=True)
    if group == 8:
        grad_left = gather(left_mine)
        hidden_in = after(hidden_in, grad_left)
    else:
        grad_left = lax.all_gather(after(left_mine, hidden_in), "tp", axis=0, tiled=True)
    grad_right = lax.all_gather(after(right_mine, hidden_in), "tp", axis=0, tiled=True)
    inverse = inverse[:, 0:1]
    live_mine = lax.dynamic_slice_in_dim(live, first, shard)[:, None]
    input_wide = block_input.astype(jnp.float32)
    gain = norm_gain.astype(jnp.float32)
    tables = turns(position)
    seg_col = jnp.broadcast_to(segment[:, None], (tokens, 128))
    seg_row = jnp.broadcast_to(segment[None, :], (8, tokens))

    projection = widen(qkv_weight, padded).reshape(3 * padded, features)
    shift_lines = widen(qkv_bias[..., None], padded).reshape(1, 3 * padded).astype(jnp.float32)
    out_wide = widen(out_weight[None], padded)[0]
    gate, up, mixed, mixed_t = gated_forward(hidden_in, gate_weight, up_weight)
    query, key, value, context, context_t, logsum = attend_forward(
        after(hidden_in, mixed), projection, shift_lines, tables, seg_col, seg_row, heads
    )
    wide_sum = Sum([mixed_t, context_t], [grad_left, grad_right])
    order = wide_sum.send(0)
    order = wide_sum.send(1, order)
    gate_low, gate_low_t, up_low, up_low_t = gated_backward(
        [grad_left, after(grad_right, order)], down_weight, gate, up
    )
    inner_sum = Sum([gate_low_t, up_low_t], [hidden_in], LONG)
    order = inner_sum.send(0)
    order = wide_sum.join(order)
    lines_low, lines_low_t, bias_grad = attend_backward(
        query,
        key,
        value,
        [grad_left, after(grad_right, order)],
        out_wide,
        logsum,
        tables,
        seg_col,
        seg_row,
        heads,
    )
    bias_grad = bias_grad[0].reshape(3, padded)[:, :width]
    outer_sum = Sum([lines_low_t], [hidden_in], LONG)
    term = merge([gate_low, up_low, lines_low], [gate_weight, up_weight, projection])
    order = wide_sum.total(term)
    order = inner_sum.join(order)
    order = wide_sum.share(order)
    order = outer_sum.send(0, order)
    merged = merge([after(context, order), mixed], [out_wide, down_weight])
    old = wide_sum.place_early(merged)
    down_grad, out_grad = wide_sum.place_last(old)
    order = inner_sum.total(down_grad)
    order = outer_sum.join(order)
    order = inner_sum.share(order)
    order = outer_sum.total(order)
    order = outer_sum.share(order)
    normed_grad = lax.psum_scatter(term, "tp", scatter_dimension=0, tiled=True).astype(jnp.float32)
    sums = jnp.concatenate([jnp.sum(normed_grad * normed, axis=0), jnp.sum(normed_grad, axis=0)])
    merged = lax.psum_scatter(merged, "tp", scatter_dimension=0, tiled=True)
    merged = merged.astype(jnp.float32)
    output = (input_wide + jnp.where(live_mine, merged, 0.0)).astype(jnp.bfloat16)
    scaled = normed_grad * gain
    input_grad = inverse * (
        scaled
        - jnp.mean(scaled, axis=1, keepdims=True)
        - normed * jnp.mean(scaled * normed, axis=1, keepdims=True)
    )
    input_grad = input_grad + cotangent.astype(jnp.float32)
    inner_old = inner_sum.place_early(order, output, input_grad)
    outer_old = outer_sum.place_early(inner_old)
    sums = sum_everywhere(after(sums, outer_old), "tp")
    gate_grad, up_grad = inner_sum.place_last(inner_old, sums)
    sums = sum_everywhere(jnp.concatenate([sums, bias_grad.reshape(-1)]), "rows")
    (qkv_grad,) = outer_sum.place_last(outer_old, gate_grad)
    return (
        output,
        input_grad,
        sums[:features],
        sums[features : 2 * features],
        qkv_grad.reshape(3, padded, features)[:, :width],
        sums[2 * features :].reshape(3, width),
        out_grad[:width],
        gate_grad,
        up_grad,
        down_grad,
    )


def solution(mesh):
    placed = (
        P(("rows", "tp"), None),
        P(),
        P(),
        P(None, "tp", None),
        P(None, "tp"),
        P("tp", None),
        P("tp", None),
        P("tp", None),
        P("tp", None),
        P(("rows", "tp"), None),
        P("rows", None),
    )
    return jax.shard_map(
        per_device,
        mesh=mesh,
        in_specs=placed,
        out_specs=(
            P(("rows", "tp"), None),
            P(("rows", "tp"), None),
            P(),
            P(),
            P(None, "tp", None),
            P(None, "tp"),
            P("tp", None),
            P("tp", None),
            P("tp", None),
            P("tp", None),
        ),
        check_vma=False,
    )
```

```python
import functools
import jax
import jax.numpy as jnp
from jax import lax
from jax.experimental import pallas as pl
from jax.experimental.pallas import tpu as pltpu
from jax.sharding import PartitionSpec as P

HEAD = 64
ROT = 16
MASKED = -1e30
LONG = 1000
EPSILON = 1e-05
ROOM = 16 * 2**20
SMALL = 10 * 2**20
IN_VMEM = pl.BlockSpec(memory_space=pltpu.VMEM)
IN_SMEM = pl.BlockSpec(memory_space=pltpu.SMEM)


def dot_rows(a, b):
    return lax.dot_general(a, b, (((1,), (0,)), ((), ())), preferred_element_type=jnp.float32)


def dot_lanes(a, b):
    return lax.dot_general(a, b, (((1,), (1,)), ((), ())), preferred_element_type=jnp.float32)


def dot_tall(a, b):
    return lax.dot_general(a, b, (((0,), (0,)), ((), ())), preferred_element_type=jnp.float32)


def turn(values, tables, sign):
    half = ROT // 2
    width = values.shape[1]
    tables = [jnp.concatenate([part] * (width // 128), axis=1) for part in tables]
    up = pltpu.roll(values, width - half, 1)
    down = pltpu.roll(values, half, 1)
    return values * tables[0] + sign * (up * tables[1] + down * tables[2])


def of_head(head, shape):
    return lax.broadcasted_iota(jnp.int32, shape, 1) // HEAD == head


def over_blocks(row_len, block, body):
    longest = row_len // 2
    blocks = row_len // block
    if blocks <= 8:
        for index in range(blocks):
            first = index * block
            start = max(0, first + block - (longest + block))
            body(first, start, first + block - start)
    else:
        size = longest + block

        def step(index, carry):
            first = pl.multiple_of(index * block, block)
            start = pl.multiple_of(jnp.maximum(first - longest, 0), block)
            body(first, start, size)
            return carry

        lax.fori_loop(0, blocks, step, 0)


def mask_of(seg_col, seg_row, first, start, block, size):
    rows = first + lax.broadcasted_iota(jnp.int32, (block, size), 0)
    keys = start + lax.broadcasted_iota(jnp.int32, (block, size), 1)
    same = seg_col[pl.ds(first, block), 0:1] == seg_row[0:1, pl.ds(start, size)]
    return jnp.where(same & (keys <= rows), 0.0, MASKED)


def forward_kernel(
    heads,
    hidden_in,
    projection,
    shift,
    tables,
    seg_col,
    seg_row,
    query,
    key,
    value,
    context,
    context_t,
    logsum,
):
    row_len, width = query.shape
    block = 256
    scale = HEAD ** (-0.5)
    for first in range(0, row_len, block):
        here = slice(first, first + block)
        lines = dot_lanes(hidden_in[here, :], projection[...]) + shift[...]
        turning = [tables[part, here, :] for part in range(3)]
        asked = turn(lines[:, 0:width], turning, 1.0).astype(jnp.bfloat16)
        query[here, :] = asked * jnp.bfloat16(scale)
        key[here, :] = turn(lines[:, width : 2 * width], turning, 1.0).astype(jnp.bfloat16)
        value[here, :] = lines[:, 2 * width : 3 * width].astype(jnp.bfloat16)

    def one_block(first, start, size):
        bias = mask_of(seg_col, seg_row, first, start, block, size)
        here = query[pl.ds(first, block), :]
        keys = key[pl.ds(start, size), :]
        values = value[pl.ds(start, size), :]
        total = jnp.zeros((block, width), jnp.float32)
        lane = lax.broadcasted_iota(jnp.int32, (block, 128), 1)
        sums = jnp.zeros((block, 128), jnp.float32)
        for head in range(heads):
            mine = of_head(head, (block, width))
            scores = dot_lanes(jnp.where(mine, here, jnp.bfloat16(0)), keys) + bias
            highest = jnp.max(scores, axis=1, keepdims=True)
            raised = jnp.exp(scores - highest)
            amount = jnp.sum(raised, axis=1, keepdims=True)
            weights = (raised * (1.0 / amount)).astype(jnp.bfloat16)
            total = jnp.where(mine, dot_rows(weights, values), total)
            sums = jnp.where(lane == head, highest + jnp.log(amount), sums)
        context[pl.ds(first, block), :] = total.astype(jnp.bfloat16)
        context_t[:, pl.ds(first, block)] = total.T.astype(jnp.bfloat16)
        logsum[pl.ds(first, block), :] = sums

    over_blocks(row_len, block, one_block)


def attend_forward(hidden_in, projection, shift, tables, seg_col, seg_row, heads):
    row_len, width = hidden_in.shape[0], projection.shape[0] // 3
    low = jax.ShapeDtypeStruct((row_len, width), jnp.bfloat16)
    return pl.pallas_call(
        functools.partial(forward_kernel, heads),
        in_specs=[IN_VMEM] * 6,
        out_shape=(
            low,
            low,
            low,
            low,
            jax.ShapeDtypeStruct((width, row_len), jnp.bfloat16),
            jax.ShapeDtypeStruct((row_len, 128), jnp.float32),
        ),
        compiler_params=pltpu.CompilerParams(vmem_limit_bytes=ROOM + 4096 * row_len),
        cost_estimate=busy(8.5),
        name="attend_forward",
    )(hidden_in, projection, shift, tables, seg_col, seg_row)


def backward_kernel(
    heads,
    query,
    key,
    value,
    grad_left,
    grad_right,
    out_weight,
    logsum,
    tables,
    seg_col,
    seg_row,
    lines_low,
    lines_low_t,
    bias_grad,
    key_grad,
    value_grad,
):
    row_len, width = query.shape
    block = 256
    scale = HEAD ** (-0.5)
    half = grad_left.shape[1]
    key_grad[...] = jnp.zeros_like(key_grad)
    value_grad[...] = jnp.zeros_like(value_grad)
    bias_grad[...] = jnp.zeros_like(bias_grad)

    def put(part, first, grads):
        low = grads.astype(jnp.bfloat16)
        wide = low.astype(jnp.float32)
        columns = slice(part * width, (part + 1) * width)
        lines_low[pl.ds(first, block), columns] = low
        lines_low_t[columns, pl.ds(first, block)] = wide.T.astype(jnp.bfloat16)
        bias_grad[0:1, columns] += jnp.sum(wide, axis=0, keepdims=True)

    def one_block(first, start, size):
        bias = mask_of(seg_col, seg_row, first, start, block, size)
        here = query[pl.ds(first, block), :]
        here_rows = pl.ds(first, block)
        grad_here = dot_lanes(grad_left[here_rows, :], out_weight[:, 0:half])
        grad_here = grad_here + dot_lanes(grad_right[here_rows, :], out_weight[:, half:])
        grad_here = grad_here.astype(jnp.bfloat16)
        keys = key[pl.ds(start, size), :]
        values = value[pl.ds(start, size), :]
        sums = logsum[pl.ds(first, block), :]
        total = jnp.zeros((block, width), jnp.float32)
        for head in range(heads):
            mine = of_head(head, (block, width))
            asked = jnp.where(mine, here, jnp.bfloat16(0))
            pulled = jnp.where(mine, grad_here, jnp.bfloat16(0))
            scores = dot_lanes(asked, keys) + bias
            probs = jnp.exp(scores - sums[:, head : head + 1])
            prob_grad = dot_lanes(pulled, values)
            value_grad[pl.ds(start, size), :] += dot_tall(probs.astype(jnp.bfloat16), pulled)
            inner = jnp.sum(probs * prob_grad, axis=1, keepdims=True)
            score_low = (probs * (prob_grad - inner)).astype(jnp.bfloat16)
            total = jnp.where(mine, dot_rows(score_low, keys), total)
            key_grad[pl.ds(start, size), :] += dot_tall(score_low, asked)
        here_tables = [tables[part, pl.ds(first, block), :] for part in range(3)]
        put(0, first, turn(total * scale, here_tables, -1.0))

    over_blocks(row_len, block, one_block)
    for index in range(row_len // block):
        first = index * block
        here_tables = [tables[part, pl.ds(first, block), :] for part in range(3)]
        put(1, first, turn(key_grad[pl.ds(first, block), :], here_tables, -1.0))
        put(2, first, value_grad[pl.ds(first, block), :])


def attend_backward(
    query, key, value, grads, out_weight, logsum, tables, seg_col, seg_row, heads
):
    row_len, width = query.shape
    return pl.pallas_call(
        functools.partial(backward_kernel, heads),
        in_specs=[IN_VMEM] * 10,
        out_shape=(
            jax.ShapeDtypeStruct((row_len, 3 * width), jnp.bfloat16),
            jax.ShapeDtypeStruct((3 * width, row_len), jnp.bfloat16),
            jax.ShapeDtypeStruct((8, 3 * width), jnp.float32),
        ),
        scratch_shapes=[
            pltpu.VMEM((row_len, width), jnp.float32),
            pltpu.VMEM((row_len, width), jnp.float32),
        ],
        compiler_params=pltpu.CompilerParams(vmem_limit_bytes=ROOM + 4096 * row_len),
        cost_estimate=busy(13.3),
        name="attend_backward",
    )(query, key, value, *grads, out_weight, logsum, tables, seg_col, seg_row)


def layout(doc_lengths, row_len):
    ends = jnp.cumsum(doc_lengths[0])
    starts = ends - doc_lengths[0]
    places = jnp.arange(row_len, dtype=jnp.int32)
    segment = jnp.sum((places[:, None] >= ends[None, :]).astype(jnp.int32), axis=1)
    chosen = segment[:, None] == jnp.arange(ends.shape[0], dtype=jnp.int32)[None, :]
    first = jnp.sum(jnp.where(chosen, starts[None, :], 0), axis=1)
    return segment, places - first, segment < ends.shape[0] - 1


def turns(position):
    half = ROT // 2
    lane = lax.broadcasted_iota(jnp.int32, (position.shape[0], 128), 1) % HEAD
    freq = 10000.0 ** (-((lane % half).astype(jnp.float32) * (2.0 / ROT)))
    angle = position.astype(jnp.float32)[:, None] * freq
    cosine, sine = jnp.cos(angle), jnp.sin(angle)
    return jnp.stack(
        [
            jnp.where(lane < ROT, cosine, 1.0),
            jnp.where(lane < half, -sine, 0.0),
            jnp.where((lane >= half) & (lane < ROT), sine, 0.0),
        ]
    )


def busy(time):
    return pl.CostEstimate(flops=int(time * 1.5 * 10**9), bytes_accessed=0, transcendentals=0)


def blocks_of(tokens):
    return min(512, tokens)


def gated_kernel(hidden_in, gate_weight, up_weight, gate, up, mixed, mixed_t):
    gate_here = dot_lanes(gate_weight[...], hidden_in[...])
    up_here = dot_lanes(up_weight[...], hidden_in[...])
    gate[...] = gate_here
    up[...] = up_here
    total = gate_here * jax.nn.sigmoid(gate_here) * up_here
    mixed_t[...] = total.astype(jnp.bfloat16)
    mixed[...] = total.T.astype(jnp.bfloat16)


def gated_forward(hidden_in, gate_weight, up_weight):
    (tokens, features), units = hidden_in.shape, gate_weight.shape[0]
    block = blocks_of(tokens)
    tall = pl.BlockSpec((units, block), lambda step: (0, step))
    flat = pl.BlockSpec((block, units), lambda step: (step, 0))
    return pl.pallas_call(
        gated_kernel,
        grid=(tokens // block,),
        in_specs=[pl.BlockSpec((block, features), lambda step: (step, 0)), IN_VMEM, IN_VMEM],
        out_specs=[tall, tall, flat, tall],
        out_shape=[
            jax.ShapeDtypeStruct((units, tokens), jnp.float32),
            jax.ShapeDtypeStruct((units, tokens), jnp.float32),
            jax.ShapeDtypeStruct((tokens, units), jnp.bfloat16),
            jax.ShapeDtypeStruct((units, tokens), jnp.bfloat16),
        ],
        compiler_params=pltpu.CompilerParams(vmem_limit_bytes=ROOM),
        cost_estimate=busy(7.5),
        name="gated_forward",
    )(hidden_in, gate_weight, up_weight)


def gated_back_kernel(
    grad_left, grad_right, down_weight, gate, up, gate_low, gate_low_t, up_low, up_low_t
):
    half = grad_left.shape[1]
    mixed_grad = dot_lanes(down_weight[:, 0:half], grad_left[...])
    mixed_grad = mixed_grad + dot_lanes(down_weight[:, half:], grad_right[...])
    gate_here = gate[...]
    sigmoid = jax.nn.sigmoid(gate_here)
    pulled = mixed_grad * sigmoid
    gate_grad = pulled * up[...] * (1.0 + gate_here * (1.0 - sigmoid))
    up_grad = pulled * gate_here
    gate_low_t[...] = gate_grad.astype(jnp.bfloat16)
    up_low_t[...] = up_grad.astype(jnp.bfloat16)
    gate_low[...] = gate_grad.T.astype(jnp.bfloat16)
    up_low[...] = up_grad.T.astype(jnp.bfloat16)


def gated_backward(grads, down_weight, gate, up):
    (tokens, half), units = grads[0].shape, down_weight.shape[0]
    block = blocks_of(tokens)
    tall = pl.BlockSpec((units, block), lambda step: (0, step))
    flat = pl.BlockSpec((block, units), lambda step: (step, 0))
    wide = jax.ShapeDtypeStruct((tokens, units), jnp.bfloat16)
    long = jax.ShapeDtypeStruct((units, tokens), jnp.bfloat16)
    return pl.pallas_call(
        gated_back_kernel,
        grid=(tokens // block,),
        in_specs=[pl.BlockSpec((block, half), lambda step: (step, 0))] * 2 + [IN_VMEM, tall, tall],
        out_specs=[flat, tall, flat, tall],
        out_shape=[wide, long, wide, long],
        compiler_params=pltpu.CompilerParams(vmem_limit_bytes=ROOM),
        cost_estimate=busy(5.4),
        name="gated_backward",
    )(*grads, down_weight, gate, up)


def merge_kernel(count, *refs):
    total = dot_rows(refs[0][...], refs[count][...])
    for index in range(1, count):
        total = total + dot_rows(refs[index][...], refs[count + index][...])
    refs[2 * count][...] = total.astype(jnp.bfloat16)


def merge(lhs, weights):
    tokens, features, count = lhs[0].shape[0], weights[0].shape[1], len(lhs)
    block = min(256, tokens)
    return pl.pallas_call(
        functools.partial(merge_kernel, count),
        grid=(tokens // block,),
        in_specs=[
            *(pl.BlockSpec((block, part.shape[1]), lambda step: (step, 0)) for part in lhs),
            *([IN_VMEM] * count),
        ],
        out_specs=pl.BlockSpec((block, features), lambda step: (step, 0)),
        out_shape=jax.ShapeDtypeStruct((tokens, features), jnp.bfloat16),
        compiler_params=pltpu.CompilerParams(vmem_limit_bytes=SMALL),
        cost_estimate=busy(8),
        name="merge",
    )(*lhs, *weights)


def stacked(lhs, rhs, first, wide, keep):
    row = 0
    block = rhs[:, pl.ds(pl.multiple_of(first, 128), wide)]
    for part in lhs:
        keep(row, part.shape[0], dot_rows(part[...], block))
        row += part.shape[0]


def send_kernel(count, wide, order, *refs):
    lhs, rhs, outs = refs[:count], refs[count], refs[-2:]
    for half, out in enumerate(outs):

        def keep(row, rows, term, out=out):
            out[row : row + rows, :] = term.astype(jnp.bfloat16)

        stacked(lhs, rhs, order[half], wide, keep)


def join_kernel(count, parts, order, *refs):
    lhs, rhs, came = refs[:count], refs[count : count + parts], refs[count + parts : -5]
    outs, total = refs[-5:-1], refs[-1]
    for half in range(2):
        at, bit = 0, order[parts, half]
        for part in range(parts):
            here = came[2 * part + half]
            wide = here.shape[1]
            narrow = wide // 2

            def keep(row, rows, term, here=here, wide=wide):
                there = here[row : row + rows, :].astype(jnp.float32)
                total[row : row + rows, 0:wide] = (term + there).astype(jnp.bfloat16)

            stacked(lhs, rhs[part], order[part, half], wide, keep)
            for out, which in ((outs[2 * half], 1 - bit), (outs[2 * half + 1], bit)):
                columns = pl.ds(pl.multiple_of(which * narrow, narrow), narrow)
                out[:, at : at + narrow] = total[:, columns]
            at += narrow


def place_kernel(takes, olds, order, *refs):
    count = 1 + max(take[0] for take in takes)
    pieces, outs = refs[:count], refs[count + olds :]
    step = pl.program_id(0)
    for index, (which, row, column) in enumerate(takes):
        piece = pieces[which]

        @pl.when(step == index)
        def _(piece=piece, first=row, column=column):
            for out in outs:
                size, narrow = out.shape
                block = piece[first : first + size, column : column + narrow]
                out[...] = block.astype(jnp.float32)
                first += size


def place(pieces, takes, order, sizes, narrow, features, old):
    return pl.pallas_call(
        functools.partial(place_kernel, takes, len(old)),
        grid_spec=pltpu.PrefetchScalarGridSpec(
            num_scalar_prefetch=1,
            grid=(len(takes),),
            in_specs=[IN_VMEM] * len(pieces) + [pl.BlockSpec(memory_space=pl.ANY)] * len(old),
            out_specs=[
                pl.BlockSpec((size, narrow), lambda step, order: (0, order[step]))
                for size in sizes
            ],
        ),
        out_shape=[jax.ShapeDtypeStruct((size, features), jnp.float32) for size in sizes],
        input_output_aliases={1 + len(pieces) + index: index for index in range(len(old))},
        compiler_params=pltpu.CompilerParams(vmem_limit_bytes=SMALL),
        cost_estimate=busy(sum(sizes) * len(takes) * narrow / 300_000),
        name="place",
    )(jnp.stack(order).astype(jnp.int32), *pieces, *old)


def lay_kernel(where, *refs):
    mine, theirs, out, sems = refs[0:6], refs[6:12], refs[12], refs[13]
    for inner in (0, 1):

        @pl.when(where[5] == inner)
        def _(inner=inner):
            taken = (0, 1, 3 - inner, 5 - inner)
            copies = []
            for place, index in enumerate(taken):
                for side, pieces in enumerate((mine, theirs)):
                    core = where[4] if side == 0 else 1 - where[4]
                    target = out.at[where[place], core]
                    copies.append(
                        pltpu.make_async_copy(pieces[index], target, sems.at[place, side])
                    )
            for copy in copies:
                copy.start()
            for copy in copies:
                copy.wait()


def gather(values):
    line = [(2 * i + c, 2 * (i ^ 1) + c) for i in range(4) for c in range(2)]
    middle = [(2 * i + c, 2 * j + c) for i, j in ((0, 0), (1, 2), (2, 1), (3, 3)) for c in range(2)]
    core = [(i, i ^ 1) for i in range(8)]
    me = lax.axis_index("tp")
    chip = me // 2

    def move(pieces, pairs):
        return lax.ppermute(pieces, "tp", pairs)

    near = move(values, line)
    across = move(values, middle)
    far = move(across, line)
    beyond = move(near, middle)
    last = move(beyond, line)
    mine = [values, near, across, far, beyond, last]
    theirs = [move(pieces, core) for pieces in mine]
    low, inner = chip < 2, (chip == 1) | (chip == 2)
    where = [chip, chip ^ 1, 1 + low, 3 * low, me % 2, inner]
    where = jnp.stack([jnp.asarray(entry, jnp.int32) for entry in where])
    shard, features = values.shape
    out = pl.pallas_call(
        lay_kernel,
        in_specs=[IN_SMEM] + [pl.BlockSpec(memory_space=pl.ANY)] * 12,
        out_specs=pl.BlockSpec(memory_space=pl.ANY),
        out_shape=jax.ShapeDtypeStruct((4, 2, shard, features), values.dtype),
        scratch_shapes=[pltpu.SemaphoreType.DMA((4, 2))],
        compiler_params=pltpu.CompilerParams(vmem_limit_bytes=4 * 2**20),
        cost_estimate=busy(2),
        name="lay",
    )(where, *mine, *theirs)
    return out.reshape(8 * shard, features)


NEAR = [(0, 1), (1, 0), (2, 3), (3, 2)]
FAR = [(0, 2), (2, 0), (1, 3), (3, 1)]
PATHS = ((NEAR, FAR), (FAR, NEAR))


def after(value, *others):
    return lax.optimization_barrier((value, others))[0]


class Sum:
    def __init__(self, lhs, parts, time=0):
        row = lax.axis_index("rows")
        near, far = row % 2, row // 2
        self.bits = ((near, far), (far, near))
        self.lhs, self.parts, self.time = lhs, parts, time
        self.rows, self.sizes = sum(part.shape[0] for part in lhs), [part.shape[0] for part in lhs]
        self.came = []

    def first(self, part, half, bit):
        return part.shape[1] // 8 * (4 * half + 2 * bit)

    def piece(self, wide):
        return jax.ShapeDtypeStruct((self.rows, wide), jnp.bfloat16)

    def room(self):
        return pltpu.CompilerParams(vmem_limit_bytes=SMALL + 4096 * self.lhs[0].shape[1])

    def send(self, part, *earlier):
        rhs = self.parts[part]
        order = jnp.stack([self.first(rhs, half, 1 - self.bits[half][0]) for half in range(2)])
        wide = rhs.shape[1] // 4
        head = after(self.lhs[0], *earlier)
        sent = pl.pallas_call(
            functools.partial(send_kernel, len(self.lhs), wide),
            in_specs=[IN_SMEM] + [IN_VMEM] * (len(self.lhs) + 1),
            out_shape=[self.piece(wide)] * 2,
            compiler_params=self.room(),
            cost_estimate=busy(self.rows * wide / 131072),
            name="send_terms",
        )(order.astype(jnp.int32), head, *self.lhs[1:], rhs)
        self.came += [lax.ppermute(sent[half], "rows", PATHS[half][0]) for half in range(2)]
        return sent

    def join(self, *earlier):
        order = [[self.first(part, half, self.bits[half][0]) for half in range(2)] for part in self.parts]
        order.append([self.bits[0][1], self.bits[1][1]])
        wide = sum(part.shape[1] // 8 for part in self.parts)
        head = after(self.lhs[0], *earlier)
        outs = pl.pallas_call(
            functools.partial(join_kernel, len(self.lhs), len(self.parts)),
            in_specs=[IN_SMEM] + [IN_VMEM] * (len(self.lhs) + 3 * len(self.parts)),
            out_shape=[self.piece(wide)] * 4,
            scratch_shapes=[pltpu.VMEM((self.rows, 2 * wide), jnp.bfloat16)],
            compiler_params=self.room(),
            cost_estimate=busy(self.time if self.time else self.rows / 256),
            name="join_terms",
        )(jnp.array(order).astype(jnp.int32), head, *self.lhs[1:], *self.parts, *self.came)
        self.mine = [outs[1], outs[3]]
        self.came = [lax.ppermute(outs[2 * half], "rows", PATHS[half][1]) for half in range(2)]
        return outs

    def total(self, *earlier):
        mine = lax.optimization_barrier((*self.mine, *earlier))[:2]
        self.mine = [mine[half] + self.came[half] for half in range(2)]
        self.across = [lax.ppermute(self.mine[half], "rows", PATHS[half][1]) for half in range(2)]
        return self.mine

    def share(self, *earlier):
        mine = lax.optimization_barrier((*self.mine, *earlier))[:2]
        both = [jnp.concatenate([mine[half], self.across[half]]) for half in range(2)]
        self.last = [lax.ppermute(both[half], "rows", PATHS[half][0]) for half in range(2)]
        return both

    def place(self, pieces, kinds, old, *earlier):
        features = sum(part.shape[1] for part in self.parts)
        narrow = min(part.shape[1] // 8 for part in self.parts)
        takes, order = [], []
        for pair, places in enumerate(kinds):
            for half in range(2):
                a, b = self.bits[half]
                for index, (first, second) in enumerate(places):
                    block = 4 * half + 2 * jnp.abs(a - first) + jnp.abs(b - second)
                    for part in range(len(self.parts)):
                        takes.append((2 * pair + half, index * self.rows, part * narrow))
                        order.append(8 * part + block)
        pieces = lax.optimization_barrier((*pieces, *earlier))[: len(pieces)]
        return place(pieces, takes, order, self.sizes, narrow, features, old)

    def place_early(self, *earlier):
        pieces = [*self.mine, *self.across]
        return self.place(pieces, [[(0, 0)], [(0, 1)]], (), *earlier)

    def place_last(self, old, *earlier):
        return self.place(self.last, [[(1, 0), (1, 1)]], old, *earlier)


def sum_everywhere(values, axis):
    size, step = lax.axis_size(axis), 1
    while step < size:
        values = values + lax.ppermute(values, axis, [(i, i ^ step) for i in range(size)])
        step *= 2
    return values


def norm_kernel(
    place, lengths, values, gain, shift, cotangent, normed, inverse, hidden, left, right
):
    wide = values[...].astype(jnp.float32)
    centred = wide - jnp.mean(wide, axis=1, keepdims=True)
    spread = jnp.mean(centred * centred, axis=1, keepdims=True)
    scale = lax.rsqrt(spread + EPSILON)
    units = centred * scale
    normed[...] = units
    inverse[...] = jnp.broadcast_to(scale, inverse.shape)
    low = units * gain[...].astype(jnp.float32) + shift[...].astype(jnp.float32)
    hidden[...] = low.astype(jnp.bfloat16)
    alive = -place[0]
    for piece in range(lengths.shape[1] - 1):
        alive = alive + lengths[0, piece]
    rows = lax.broadcasted_iota(jnp.int32, wide.shape, 0)
    grads = jnp.where(rows < alive, cotangent[...].astype(jnp.float32), 0.0).astype(jnp.bfloat16)
    half = wide.shape[1] // 2
    left[...] = grads[:, 0:half]
    right[...] = grads[:, half:]


def norm(place, lengths, values, gain, shift, cotangent):
    shard, features = values.shape
    part = jax.ShapeDtypeStruct((shard, features // 2), jnp.bfloat16)
    return pl.pallas_call(
        norm_kernel,
        in_specs=[IN_SMEM] * 2 + [pl.BlockSpec()] * 4,
        out_shape=[
            jax.ShapeDtypeStruct((shard, features), jnp.float32),
            jax.ShapeDtypeStruct((shard, 128), jnp.float32),
            jax.ShapeDtypeStruct((shard, features), jnp.bfloat16),
            part,
            part,
        ],
        compiler_params=pltpu.CompilerParams(vmem_limit_bytes=SMALL),
        cost_estimate=busy(2),
        name="norm",
    )(place, lengths, values, gain[None], shift[None], cotangent)


def widen(weight, width):
    return jnp.pad(weight, ((0, 0), (0, width - weight.shape[1]), (0, 0)))


def per_device(
    block_input,
    norm_gain,
    norm_bias,
    qkv_weight,
    qkv_bias,
    out_weight,
    gate_weight,
    up_weight,
    down_weight,
    cotangent,
    doc_lengths,
):
    shard, features = block_input.shape
    group = lax.axis_size("tp")
    tokens = shard * group
    width = qkv_weight.shape[1]
    heads = width // HEAD
    padded = max(width, 128)
    me = lax.axis_index("tp")
    segment, position, live = layout(doc_lengths, tokens)
    first = me * shard
    normed, inverse, normed_low, left_mine, right_mine = norm(
        first[None].astype(jnp.int32), doc_lengths, block_input, norm_gain, norm_bias, cotangent
    )
    hidden_in = lax.all_gather(normed_low, "tp", axis=0, tiled=True)
    if group == 8:
        grad_left = gather(left_mine)
        hidden_in = after(hidden_in, grad_left)
    else:
        grad_left = lax.all_gather(after(left_mine, hidden_in), "tp", axis=0, tiled=True)
    grad_right = lax.all_gather(after(right_mine, hidden_in), "tp", axis=0, tiled=True)
    inverse = inverse[:, 0:1]
    live_mine = lax.dynamic_slice_in_dim(live, first, shard)[:, None]
    input_wide = block_input.astype(jnp.float32)
    gain = norm_gain.astype(jnp.float32)
    tables = turns(position)
    seg_col = jnp.broadcast_to(segment[:, None], (tokens, 128))
    seg_row = jnp.broadcast_to(segment[None, :], (8, tokens))

    projection = widen(qkv_weight, padded).reshape(3 * padded, features)
    shift_lines = widen(qkv_bias[..., None], padded).reshape(1, 3 * padded).astype(jnp.float32)
    out_wide = widen(out_weight[None], padded)[0]
    gate, up, mixed, mixed_t = gated_forward(hidden_in, gate_weight, up_weight)
    query, key, value, context, context_t, logsum = attend_forward(
        after(hidden_in, mixed), projection, shift_lines, tables, seg_col, seg_row, heads
    )
    wide_sum = Sum([mixed_t, context_t], [grad_left, grad_right])
    order = wide_sum.send(0)
    order = wide_sum.send(1, order)
    gate_low, gate_low_t, up_low, up_low_t = gated_backward(
        [grad_left, after(grad_right, order)], down_weight, gate, up
    )
    inner_sum = Sum([gate_low_t, up_low_t], [hidden_in], LONG)
    order = inner_sum.send(0)
    order = wide_sum.join(order)
    lines_low, lines_low_t, bias_grad = attend_backward(
        query,
        key,
        value,
        [grad_left, after(grad_right, order)],
        out_wide,
        logsum,
        tables,
        seg_col,
        seg_row,
        heads,
    )
    bias_grad = bias_grad[0].reshape(3, padded)[:, :width]
    outer_sum = Sum([lines_low_t], [hidden_in], LONG)
    term = merge([gate_low, up_low, lines_low], [gate_weight, up_weight, projection])
    order = wide_sum.total(term)
    order = inner_sum.join(order)
    order = wide_sum.share(order)
    order = outer_sum.send(0, order)
    merged = merge([after(context, order), mixed], [out_wide, down_weight])
    old = wide_sum.place_early(merged)
    down_grad, out_grad = wide_sum.place_last(old)
    order = inner_sum.total(down_grad)
    order = outer_sum.join(order)
    order = inner_sum.share(order)
    order = outer_sum.total(order)
    order = outer_sum.share(order)
    normed_grad = lax.psum_scatter(term, "tp", scatter_dimension=0, tiled=True).astype(jnp.float32)
    sums = jnp.concatenate([jnp.sum(normed_grad * normed, axis=0), jnp.sum(normed_grad, axis=0)])
    merged = lax.psum_scatter(merged, "tp", scatter_dimension=0, tiled=True)
    merged = merged.astype(jnp.float32)
    output = (input_wide + jnp.where(live_mine, merged, 0.0)).astype(jnp.bfloat16)
    scaled = normed_grad * gain
    input_grad = inverse * (
        scaled
        - jnp.mean(scaled, axis=1, keepdims=True)
        - normed * jnp.mean(scaled * normed, axis=1, keepdims=True)
    )
    input_grad = input_grad + cotangent.astype(jnp.float32)
    inner_old = inner_sum.place_early(order, output, input_grad)
    outer_old = outer_sum.place_early(inner_old)
    sums = sum_everywhere(after(sums, outer_old), "tp")
    gate_grad, up_grad = inner_sum.place_last(inner_old, sums)
    sums = sum_everywhere(jnp.concatenate([sums, bias_grad.reshape(-1)]), "rows")
    (qkv_grad,) = outer_sum.place_last(outer_old, gate_grad)
    return (
        output,
        input_grad,
        sums[:features],
        sums[features : 2 * features],
        qkv_grad.reshape(3, padded, features)[:, :width],
        sums[2 * features :].reshape(3, width),
        out_grad[:width],
        gate_grad,
        up_grad,
        down_grad,
    )


def solution(mesh):
    placed = (
        P(("rows", "tp"), None),
        P(),
        P(),
        P(None, "tp", None),
        P(None, "tp"),
        P("tp", None),
        P("tp", None),
        P("tp", None),
        P("tp", None),
        P(("rows", "tp"), None),
        P("rows", None),
    )
    return jax.shard_map(
        per_device,
        mesh=mesh,
        in_specs=placed,
        out_specs=(
            P(("rows", "tp"), None),
            P(("rows", "tp"), None),
            P(),
            P(),
            P(None, "tp", None),
            P(None, "tp"),
            P("tp", None),
            P("tp", None),
            P("tp", None),
            P("tp", None),
        ),
        check_vma=False,
    )
```

```python
import functools
import jax
import jax.numpy as jnp
from jax import lax
from jax.experimental import pallas as pl
from jax.experimental.pallas import tpu as pltpu
from jax.sharding import PartitionSpec as P

HEAD = 64
ROT = 16
MASKED = -1e30
LONG = 1000
EPSILON = 1e-05
ROOM = 13 * 2**20
SMALL = 8 * 2**20
IN_VMEM = pl.BlockSpec(memory_space=pltpu.VMEM)
IN_SMEM = pl.BlockSpec(memory_space=pltpu.SMEM)


def dot_rows(a, b):
    return lax.dot_general(a, b, (((1,), (0,)), ((), ())), preferred_element_type=jnp.float32)


def dot_lanes(a, b):
    return lax.dot_general(a, b, (((1,), (1,)), ((), ())), preferred_element_type=jnp.float32)


def dot_tall(a, b):
    return lax.dot_general(a, b, (((0,), (0,)), ((), ())), preferred_element_type=jnp.float32)


def turn(values, tables, sign):
    half = ROT // 2
    width = values.shape[1]
    tables = [jnp.concatenate([part] * (width // 128), axis=1) for part in tables]
    up = pltpu.roll(values, width - half, 1)
    down = pltpu.roll(values, half, 1)
    return values * tables[0] + sign * (up * tables[1] + down * tables[2])


def of_head(head, shape):
    return lax.broadcasted_iota(jnp.int32, shape, 1) // HEAD == head


def over_blocks(row_len, block, body):
    longest = row_len // 2
    blocks = row_len // block
    if blocks <= 8:
        for index in range(blocks):
            first = index * block
            start = max(0, first + block - (longest + block))
            body(first, start, first + block - start)
    else:
        size = longest + block

        def step(index, carry):
            first = pl.multiple_of(index * block, block)
            start = pl.multiple_of(jnp.maximum(first - longest, 0), block)
            body(first, start, size)
            return carry

        lax.fori_loop(0, blocks, step, 0)


def mask_of(seg_col, seg_row, first, start, block, size):
    rows = first + lax.broadcasted_iota(jnp.int32, (block, size), 0)
    keys = start + lax.broadcasted_iota(jnp.int32, (block, size), 1)
    same = seg_col[pl.ds(first, block), 0:1] == seg_row[0:1, pl.ds(start, size)]
    return jnp.where(same & (keys <= rows), 0.0, MASKED)


def forward_kernel(
    heads,
    hidden_in,
    projection,
    shift,
    tables,
    seg_col,
    seg_row,
    query,
    key,
    value,
    context,
    context_t,
    logsum,
):
    row_len, width = query.shape
    block = 256
    scale = HEAD ** (-0.5)
    for first in range(0, row_len, block):
        here = slice(first, first + block)
        lines = dot_lanes(hidden_in[here, :], projection[...]) + shift[...]
        turning = [tables[part, here, :] for part in range(3)]
        asked = turn(lines[:, 0:width], turning, 1.0).astype(jnp.bfloat16)
        query[here, :] = asked * jnp.bfloat16(scale)
        key[here, :] = turn(lines[:, width : 2 * width], turning, 1.0).astype(jnp.bfloat16)
        value[here, :] = lines[:, 2 * width : 3 * width].astype(jnp.bfloat16)

    def one_block(first, start, size):
        bias = mask_of(seg_col, seg_row, first, start, block, size)
        here = query[pl.ds(first, block), :]
        keys = key[pl.ds(start, size), :]
        values = value[pl.ds(start, size), :]
        total = jnp.zeros((block, width), jnp.float32)
        lane = lax.broadcasted_iota(jnp.int32, (block, 128), 1)
        sums = jnp.zeros((block, 128), jnp.float32)
        for head in range(heads):
            mine = of_head(head, (block, width))
            scores = dot_lanes(jnp.where(mine, here, jnp.bfloat16(0)), keys) + bias
            highest = jnp.max(scores, axis=1, keepdims=True)
            raised = jnp.exp(scores - highest)
            amount = jnp.sum(raised, axis=1, keepdims=True)
            weights = (raised * (1.0 / amount)).astype(jnp.bfloat16)
            total = jnp.where(mine, dot_rows(weights, values), total)
            sums = jnp.where(lane == head, highest + jnp.log(amount), sums)
        context[pl.ds(first, block), :] = total.astype(jnp.bfloat16)
        context_t[:, pl.ds(first, block)] = total.T.astype(jnp.bfloat16)
        logsum[pl.ds(first, block), :] = sums

    over_blocks(row_len, block, one_block)


def attend_forward(hidden_in, projection, shift, tables, seg_col, seg_row, heads):
    row_len, width = hidden_in.shape[0], projection.shape[0] // 3
    low = jax.ShapeDtypeStruct((row_len, width), jnp.bfloat16)
    return pl.pallas_call(
        functools.partial(forward_kernel, heads),
        in_specs=[IN_VMEM] * 6,
        out_shape=(
            low,
            low,
            low,
            low,
            jax.ShapeDtypeStruct((width, row_len), jnp.bfloat16),
            jax.ShapeDtypeStruct((row_len, 128), jnp.float32),
        ),
        compiler_params=pltpu.CompilerParams(vmem_limit_bytes=ROOM + 4096 * row_len),
        cost_estimate=busy(8.5),
        name="attend_forward",
    )(hidden_in, projection, shift, tables, seg_col, seg_row)


def backward_kernel(
    heads,
    query,
    key,
    value,
    grad_left,
    grad_right,
    out_weight,
    logsum,
    tables,
    seg_col,
    seg_row,
    lines_low,
    lines_low_t,
    bias_grad,
    key_grad,
    value_grad,
):
    row_len, width = query.shape
    block = 256
    scale = HEAD ** (-0.5)
    half = grad_left.shape[1]
    key_grad[...] = jnp.zeros_like(key_grad)
    value_grad[...] = jnp.zeros_like(value_grad)
    bias_grad[...] = jnp.zeros_like(bias_grad)

    def put(part, first, grads):
        low = grads.astype(jnp.bfloat16)
        wide = low.astype(jnp.float32)
        columns = slice(part * width, (part + 1) * width)
        lines_low[pl.ds(first, block), columns] = low
        lines_low_t[columns, pl.ds(first, block)] = wide.T.astype(jnp.bfloat16)
        bias_grad[0:1, columns] += jnp.sum(wide, axis=0, keepdims=True)

    def one_block(first, start, size):
        bias = mask_of(seg_col, seg_row, first, start, block, size)
        here = query[pl.ds(first, block), :]
        here_rows = pl.ds(first, block)
        grad_here = dot_lanes(grad_left[here_rows, :], out_weight[:, 0:half])
        grad_here = grad_here + dot_lanes(grad_right[here_rows, :], out_weight[:, half:])
        grad_here = grad_here.astype(jnp.bfloat16)
        keys = key[pl.ds(start, size), :]
        values = value[pl.ds(start, size), :]
        sums = logsum[pl.ds(first, block), :]
        total = jnp.zeros((block, width), jnp.float32)
        for head in range(heads):
            mine = of_head(head, (block, width))
            asked = jnp.where(mine, here, jnp.bfloat16(0))
            pulled = jnp.where(mine, grad_here, jnp.bfloat16(0))
            scores = dot_lanes(asked, keys) + bias
            probs = jnp.exp(scores - sums[:, head : head + 1])
            prob_grad = dot_lanes(pulled, values)
            value_grad[pl.ds(start, size), :] += dot_tall(probs.astype(jnp.bfloat16), pulled)
            inner = jnp.sum(probs * prob_grad, axis=1, keepdims=True)
            score_low = (probs * (prob_grad - inner)).astype(jnp.bfloat16)
            total = jnp.where(mine, dot_rows(score_low, keys), total)
            key_grad[pl.ds(start, size), :] += dot_tall(score_low, asked)
        here_tables = [tables[part, pl.ds(first, block), :] for part in range(3)]
        put(0, first, turn(total * scale, here_tables, -1.0))

    over_blocks(row_len, block, one_block)
    for index in range(row_len // block):
        first = index * block
        here_tables = [tables[part, pl.ds(first, block), :] for part in range(3)]
        put(1, first, turn(key_grad[pl.ds(first, block), :], here_tables, -1.0))
        put(2, first, value_grad[pl.ds(first, block), :])


def attend_backward(
    query, key, value, grads, out_weight, logsum, tables, seg_col, seg_row, heads
):
    row_len, width = query.shape
    return pl.pallas_call(
        functools.partial(backward_kernel, heads),
        in_specs=[IN_VMEM] * 10,
        out_shape=(
            jax.ShapeDtypeStruct((row_len, 3 * width), jnp.bfloat16),
            jax.ShapeDtypeStruct((3 * width, row_len), jnp.bfloat16),
            jax.ShapeDtypeStruct((8, 3 * width), jnp.float32),
        ),
        scratch_shapes=[
            pltpu.VMEM((row_len, width), jnp.float32),
            pltpu.VMEM((row_len, width), jnp.float32),
        ],
        compiler_params=pltpu.CompilerParams(vmem_limit_bytes=ROOM + 4096 * row_len),
        cost_estimate=busy(13.3),
        name="attend_backward",
    )(query, key, value, *grads, out_weight, logsum, tables, seg_col, seg_row)


def layout(doc_lengths, row_len):
    ends = jnp.cumsum(doc_lengths[0])
    starts = ends - doc_lengths[0]
    places = jnp.arange(row_len, dtype=jnp.int32)
    segment = jnp.sum((places[:, None] >= ends[None, :]).astype(jnp.int32), axis=1)
    chosen = segment[:, None] == jnp.arange(ends.shape[0], dtype=jnp.int32)[None, :]
    first = jnp.sum(jnp.where(chosen, starts[None, :], 0), axis=1)
    return segment, places - first, segment < ends.shape[0] - 1


def turns(position):
    half = ROT // 2
    lane = lax.broadcasted_iota(jnp.int32, (position.shape[0], 128), 1) % HEAD
    freq = 10000.0 ** (-((lane % half).astype(jnp.float32) * (2.0 / ROT)))
    angle = position.astype(jnp.float32)[:, None] * freq
    cosine, sine = jnp.cos(angle), jnp.sin(angle)
    return jnp.stack(
        [
            jnp.where(lane < ROT, cosine, 1.0),
            jnp.where(lane < half, -sine, 0.0),
            jnp.where((lane >= half) & (lane < ROT), sine, 0.0),
        ]
    )


def busy(time):
    return pl.CostEstimate(flops=int(time * 1.5 * 10**9), bytes_accessed=0, transcendentals=0)


def blocks_of(tokens):
    return min(512, tokens)


def gated_kernel(hidden_in, gate_weight, up_weight, gate, up, mixed, mixed_t):
    gate_here = dot_lanes(gate_weight[...], hidden_in[...])
    up_here = dot_lanes(up_weight[...], hidden_in[...])
    gate[...] = gate_here
    up[...] = up_here
    total = gate_here * jax.nn.sigmoid(gate_here) * up_here
    mixed_t[...] = total.astype(jnp.bfloat16)
    mixed[...] = total.T.astype(jnp.bfloat16)


def gated_forward(hidden_in, gate_weight, up_weight):
    (tokens, features), units = hidden_in.shape, gate_weight.shape[0]
    block = blocks_of(tokens)
    tall = pl.BlockSpec((units, block), lambda step: (0, step))
    flat = pl.BlockSpec((block, units), lambda step: (step, 0))
    return pl.pallas_call(
        gated_kernel,
        grid=(tokens // block,),
        in_specs=[pl.BlockSpec((block, features), lambda step: (step, 0)), IN_VMEM, IN_VMEM],
        out_specs=[tall, tall, flat, tall],
        out_shape=[
            jax.ShapeDtypeStruct((units, tokens), jnp.float32),
            jax.ShapeDtypeStruct((units, tokens), jnp.float32),
            jax.ShapeDtypeStruct((tokens, units), jnp.bfloat16),
            jax.ShapeDtypeStruct((units, tokens), jnp.bfloat16),
        ],
        compiler_params=pltpu.CompilerParams(vmem_limit_bytes=ROOM),
        cost_estimate=busy(7.5),
        name="gated_forward",
    )(hidden_in, gate_weight, up_weight)


def gated_back_kernel(
    grad_left, grad_right, down_weight, gate, up, gate_low, gate_low_t, up_low, up_low_t
):
    half = grad_left.shape[1]
    mixed_grad = dot_lanes(down_weight[:, 0:half], grad_left[...])
    mixed_grad = mixed_grad + dot_lanes(down_weight[:, half:], grad_right[...])
    gate_here = gate[...]
    sigmoid = jax.nn.sigmoid(gate_here)
    pulled = mixed_grad * sigmoid
    gate_grad = pulled * up[...] * (1.0 + gate_here * (1.0 - sigmoid))
    up_grad = pulled * gate_here
    gate_low_t[...] = gate_grad.astype(jnp.bfloat16)
    up_low_t[...] = up_grad.astype(jnp.bfloat16)
    gate_low[...] = gate_grad.T.astype(jnp.bfloat16)
    up_low[...] = up_grad.T.astype(jnp.bfloat16)


def gated_backward(grads, down_weight, gate, up):
    (tokens, half), units = grads[0].shape, down_weight.shape[0]
    block = blocks_of(tokens)
    tall = pl.BlockSpec((units, block), lambda step: (0, step))
    flat = pl.BlockSpec((block, units), lambda step: (step, 0))
    wide = jax.ShapeDtypeStruct((tokens, units), jnp.bfloat16)
    long = jax.ShapeDtypeStruct((units, tokens), jnp.bfloat16)
    return pl.pallas_call(
        gated_back_kernel,
        grid=(tokens // block,),
        in_specs=[pl.BlockSpec((block, half), lambda step: (step, 0))] * 2 + [IN_VMEM, tall, tall],
        out_specs=[flat, tall, flat, tall],
        out_shape=[wide, long, wide, long],
        compiler_params=pltpu.CompilerParams(vmem_limit_bytes=ROOM),
        cost_estimate=busy(5.4),
        name="gated_backward",
    )(*grads, down_weight, gate, up)


def merge_kernel(count, *refs):
    total = dot_rows(refs[0][...], refs[count][...])
    for index in range(1, count):
        total = total + dot_rows(refs[index][...], refs[count + index][...])
    refs[2 * count][...] = total.astype(jnp.bfloat16)


def merge(lhs, weights):
    tokens, features, count = lhs[0].shape[0], weights[0].shape[1], len(lhs)
    block = min(256, tokens)
    return pl.pallas_call(
        functools.partial(merge_kernel, count),
        grid=(tokens // block,),
        in_specs=[
            *(pl.BlockSpec((block, part.shape[1]), lambda step: (step, 0)) for part in lhs),
            *([IN_VMEM] * count),
        ],
        out_specs=pl.BlockSpec((block, features), lambda step: (step, 0)),
        out_shape=jax.ShapeDtypeStruct((tokens, features), jnp.bfloat16),
        compiler_params=pltpu.CompilerParams(vmem_limit_bytes=SMALL),
        cost_estimate=busy(8),
        name="merge",
    )(*lhs, *weights)


def stacked(lhs, rhs, first, wide, keep):
    row = 0
    block = rhs[:, pl.ds(pl.multiple_of(first, 128), wide)]
    for part in lhs:
        keep(row, part.shape[0], dot_rows(part[...], block))
        row += part.shape[0]


def send_kernel(count, wide, order, *refs):
    lhs, rhs, outs = refs[:count], refs[count], refs[-2:]
    for half, out in enumerate(outs):

        def keep(row, rows, term, out=out):
            out[row : row + rows, :] = term.astype(jnp.bfloat16)

        stacked(lhs, rhs, order[half], wide, keep)


def join_kernel(count, parts, order, *refs):
    lhs, rhs, came = refs[:count], refs[count : count + parts], refs[count + parts : -5]
    outs, total = refs[-5:-1], refs[-1]
    for half in range(2):
        at, bit = 0, order[parts, half]
        for part in range(parts):
            here = came[2 * part + half]
            wide = here.shape[1]
            narrow = wide // 2

            def keep(row, rows, term, here=here, wide=wide):
                there = here[row : row + rows, :].astype(jnp.float32)
                total[row : row + rows, 0:wide] = (term + there).astype(jnp.bfloat16)

            stacked(lhs, rhs[part], order[part, half], wide, keep)
            for out, which in ((outs[2 * half], 1 - bit), (outs[2 * half + 1], bit)):
                columns = pl.ds(pl.multiple_of(which * narrow, narrow), narrow)
                out[:, at : at + narrow] = total[:, columns]
            at += narrow


def place_kernel(takes, olds, order, *refs):
    count = 1 + max(take[0] for take in takes)
    pieces, outs = refs[:count], refs[count + olds :]
    step = pl.program_id(0)
    for index, (which, row, column) in enumerate(takes):
        piece = pieces[which]

        @pl.when(step == index)
        def _(piece=piece, first=row, column=column):
            for out in outs:
                size, narrow = out.shape
                block = piece[first : first + size, column : column + narrow]
                out[...] = block.astype(jnp.float32)
                first += size


def place(pieces, takes, order, sizes, narrow, features, old):
    return pl.pallas_call(
        functools.partial(place_kernel, takes, len(old)),
        grid_spec=pltpu.PrefetchScalarGridSpec(
            num_scalar_prefetch=1,
            grid=(len(takes),),
            in_specs=[IN_VMEM] * len(pieces) + [pl.BlockSpec(memory_space=pl.ANY)] * len(old),
            out_specs=[
                pl.BlockSpec((size, narrow), lambda step, order: (0, order[step]))
                for size in sizes
            ],
        ),
        out_shape=[jax.ShapeDtypeStruct((size, features), jnp.float32) for size in sizes],
        input_output_aliases={1 + len(pieces) + index: index for index in range(len(old))},
        compiler_params=pltpu.CompilerParams(vmem_limit_bytes=SMALL),
        cost_estimate=busy(sum(sizes) * len(takes) * narrow / 300_000),
        name="place",
    )(jnp.stack(order).astype(jnp.int32), *pieces, *old)


def lay_kernel(where, *refs):
    mine, theirs, out, sems = refs[0:6], refs[6:12], refs[12], refs[13]
    for inner in (0, 1):

        @pl.when(where[5] == inner)
        def _(inner=inner):
            taken = (0, 1, 3 - inner, 5 - inner)
            copies = []
            for place, index in enumerate(taken):
                for side, pieces in enumerate((mine, theirs)):
                    core = where[4] if side == 0 else 1 - where[4]
                    target = out.at[where[place], core]
                    copies.append(
                        pltpu.make_async_copy(pieces[index], target, sems.at[place, side])
                    )
            for copy in copies:
                copy.start()
            for copy in copies:
                copy.wait()


def gather(values):
    line = [(2 * i + c, 2 * (i ^ 1) + c) for i in range(4) for c in range(2)]
    middle = [(2 * i + c, 2 * j + c) for i, j in ((0, 0), (1, 2), (2, 1), (3, 3)) for c in range(2)]
    core = [(i, i ^ 1) for i in range(8)]
    me = lax.axis_index("tp")
    chip = me // 2

    def move(pieces, pairs):
        return lax.ppermute(pieces, "tp", pairs)

    near = move(values, line)
    across = move(values, middle)
    far = move(across, line)
    beyond = move(near, middle)
    last = move(beyond, line)
    mine = [values, near, across, far, beyond, last]
    theirs = [move(pieces, core) for pieces in mine]
    low, inner = chip < 2, (chip == 1) | (chip == 2)
    where = [chip, chip ^ 1, 1 + low, 3 * low, me % 2, inner]
    where = jnp.stack([jnp.asarray(entry, jnp.int32) for entry in where])
    shard, features = values.shape
    out = pl.pallas_call(
        lay_kernel,
        in_specs=[IN_SMEM] + [pl.BlockSpec(memory_space=pl.ANY)] * 12,
        out_specs=pl.BlockSpec(memory_space=pl.ANY),
        out_shape=jax.ShapeDtypeStruct((4, 2, shard, features), values.dtype),
        scratch_shapes=[pltpu.SemaphoreType.DMA((4, 2))],
        compiler_params=pltpu.CompilerParams(vmem_limit_bytes=4 * 2**20),
        cost_estimate=busy(2),
        name="lay",
    )(where, *mine, *theirs)
    return out.reshape(8 * shard, features)


NEAR = [(0, 1), (1, 0), (2, 3), (3, 2)]
FAR = [(0, 2), (2, 0), (1, 3), (3, 1)]
PATHS = ((NEAR, FAR), (FAR, NEAR))


def after(value, *others):
    return lax.optimization_barrier((value, others))[0]


class Sum:
    def __init__(self, lhs, parts, time=0):
        row = lax.axis_index("rows")
        near, far = row % 2, row // 2
        self.bits = ((near, far), (far, near))
        self.lhs, self.parts, self.time = lhs, parts, time
        self.rows, self.sizes = sum(part.shape[0] for part in lhs), [part.shape[0] for part in lhs]
        self.came = []

    def first(self, part, half, bit):
        return part.shape[1] // 8 * (4 * half + 2 * bit)

    def piece(self, wide):
        return jax.ShapeDtypeStruct((self.rows, wide), jnp.bfloat16)

    def room(self):
        return pltpu.CompilerParams(vmem_limit_bytes=SMALL + 4096 * self.lhs[0].shape[1])

    def send(self, part, *earlier):
        rhs = self.parts[part]
        order = jnp.stack([self.first(rhs, half, 1 - self.bits[half][0]) for half in range(2)])
        wide = rhs.shape[1] // 4
        head = after(self.lhs[0], *earlier)
        sent = pl.pallas_call(
            functools.partial(send_kernel, len(self.lhs), wide),
            in_specs=[IN_SMEM] + [IN_VMEM] * (len(self.lhs) + 1),
            out_shape=[self.piece(wide)] * 2,
            compiler_params=self.room(),
            cost_estimate=busy(self.rows * wide / 131072),
            name="send_terms",
        )(order.astype(jnp.int32), head, *self.lhs[1:], rhs)
        self.came += [lax.ppermute(sent[half], "rows", PATHS[half][0]) for half in range(2)]
        return sent

    def join(self, *earlier):
        order = [[self.first(part, half, self.bits[half][0]) for half in range(2)] for part in self.parts]
        order.append([self.bits[0][1], self.bits[1][1]])
        wide = sum(part.shape[1] // 8 for part in self.parts)
        head = after(self.lhs[0], *earlier)
        outs = pl.pallas_call(
            functools.partial(join_kernel, len(self.lhs), len(self.parts)),
            in_specs=[IN_SMEM] + [IN_VMEM] * (len(self.lhs) + 3 * len(self.parts)),
            out_shape=[self.piece(wide)] * 4,
            scratch_shapes=[pltpu.VMEM((self.rows, 2 * wide), jnp.bfloat16)],
            compiler_params=self.room(),
            cost_estimate=busy(self.time if self.time else self.rows / 256),
            name="join_terms",
        )(jnp.array(order).astype(jnp.int32), head, *self.lhs[1:], *self.parts, *self.came)
        self.mine = [outs[1], outs[3]]
        self.came = [lax.ppermute(outs[2 * half], "rows", PATHS[half][1]) for half in range(2)]
        return outs

    def total(self, *earlier):
        mine = lax.optimization_barrier((*self.mine, *earlier))[:2]
        self.mine = [mine[half] + self.came[half] for half in range(2)]
        self.across = [lax.ppermute(self.mine[half], "rows", PATHS[half][1]) for half in range(2)]
        return self.mine

    def share(self, *earlier):
        mine = lax.optimization_barrier((*self.mine, *earlier))[:2]
        both = [jnp.concatenate([mine[half], self.across[half]]) for half in range(2)]
        self.last = [lax.ppermute(both[half], "rows", PATHS[half][0]) for half in range(2)]
        return both

    def place(self, pieces, kinds, old, *earlier):
        features = sum(part.shape[1] for part in self.parts)
        narrow = min(part.shape[1] // 8 for part in self.parts)
        takes, order = [], []
        for pair, places in enumerate(kinds):
            for half in range(2):
                a, b = self.bits[half]
                for index, (first, second) in enumerate(places):
                    block = 4 * half + 2 * jnp.abs(a - first) + jnp.abs(b - second)
                    for part in range(len(self.parts)):
                        takes.append((2 * pair + half, index * self.rows, part * narrow))
                        order.append(8 * part + block)
        pieces = lax.optimization_barrier((*pieces, *earlier))[: len(pieces)]
        return place(pieces, takes, order, self.sizes, narrow, features, old)

    def place_early(self, *earlier):
        pieces = [*self.mine, *self.across]
        return self.place(pieces, [[(0, 0)], [(0, 1)]], (), *earlier)

    def place_last(self, old, *earlier):
        return self.place(self.last, [[(1, 0), (1, 1)]], old, *earlier)


def sum_everywhere(values, axis):
    size, step = lax.axis_size(axis), 1
    while step < size:
        values = values + lax.ppermute(values, axis, [(i, i ^ step) for i in range(size)])
        step *= 2
    return values


def norm_kernel(
    place, lengths, values, gain, shift, cotangent, normed, inverse, hidden, left, right
):
    wide = values[...].astype(jnp.float32)
    centred = wide - jnp.mean(wide, axis=1, keepdims=True)
    spread = jnp.mean(centred * centred, axis=1, keepdims=True)
    scale = lax.rsqrt(spread + EPSILON)
    units = centred * scale
    normed[...] = units
    inverse[...] = jnp.broadcast_to(scale, inverse.shape)
    low = units * gain[...].astype(jnp.float32) + shift[...].astype(jnp.float32)
    hidden[...] = low.astype(jnp.bfloat16)
    alive = -place[0]
    for piece in range(lengths.shape[1] - 1):
        alive = alive + lengths[0, piece]
    rows = lax.broadcasted_iota(jnp.int32, wide.shape, 0)
    grads = jnp.where(rows < alive, cotangent[...].astype(jnp.float32), 0.0).astype(jnp.bfloat16)
    half = wide.shape[1] // 2
    left[...] = grads[:, 0:half]
    right[...] = grads[:, half:]


def norm(place, lengths, values, gain, shift, cotangent):
    shard, features = values.shape
    part = jax.ShapeDtypeStruct((shard, features // 2), jnp.bfloat16)
    return pl.pallas_call(
        norm_kernel,
        in_specs=[IN_SMEM] * 2 + [pl.BlockSpec()] * 4,
        out_shape=[
            jax.ShapeDtypeStruct((shard, features), jnp.float32),
            jax.ShapeDtypeStruct((shard, 128), jnp.float32),
            jax.ShapeDtypeStruct((shard, features), jnp.bfloat16),
            part,
            part,
        ],
        compiler_params=pltpu.CompilerParams(vmem_limit_bytes=SMALL),
        cost_estimate=busy(2),
        name="norm",
    )(place, lengths, values, gain[None], shift[None], cotangent)


def widen(weight, width):
    return jnp.pad(weight, ((0, 0), (0, width - weight.shape[1]), (0, 0)))


def per_device(
    block_input,
    norm_gain,
    norm_bias,
    qkv_weight,
    qkv_bias,
    out_weight,
    gate_weight,
    up_weight,
    down_weight,
    cotangent,
    doc_lengths,
):
    shard, features = block_input.shape
    group = lax.axis_size("tp")
    tokens = shard * group
    width = qkv_weight.shape[1]
    heads = width // HEAD
    padded = max(width, 128)
    me = lax.axis_index("tp")
    segment, position, live = layout(doc_lengths, tokens)
    first = me * shard
    normed, inverse, normed_low, left_mine, right_mine = norm(
        first[None].astype(jnp.int32), doc_lengths, block_input, norm_gain, norm_bias, cotangent
    )
    hidden_in = lax.all_gather(normed_low, "tp", axis=0, tiled=True)
    if group == 8:
        grad_left = gather(left_mine)
        hidden_in = after(hidden_in, grad_left)
    else:
        grad_left = lax.all_gather(after(left_mine, hidden_in), "tp", axis=0, tiled=True)
    grad_right = lax.all_gather(after(right_mine, hidden_in), "tp", axis=0, tiled=True)
    inverse = inverse[:, 0:1]
    live_mine = lax.dynamic_slice_in_dim(live, first, shard)[:, None]
    input_wide = block_input.astype(jnp.float32)
    gain = norm_gain.astype(jnp.float32)
    tables = turns(position)
    seg_col = jnp.broadcast_to(segment[:, None], (tokens, 128))
    seg_row = jnp.broadcast_to(segment[None, :], (8, tokens))

    projection = widen(qkv_weight, padded).reshape(3 * padded, features)
    shift_lines = widen(qkv_bias[..., None], padded).reshape(1, 3 * padded).astype(jnp.float32)
    out_wide = widen(out_weight[None], padded)[0]
    gate, up, mixed, mixed_t = gated_forward(hidden_in, gate_weight, up_weight)
    query, key, value, context, context_t, logsum = attend_forward(
        after(hidden_in, mixed), projection, shift_lines, tables, seg_col, seg_row, heads
    )
    wide_sum = Sum([mixed_t, context_t], [grad_left, grad_right])
    order = wide_sum.send(0)
    order = wide_sum.send(1, order)
    gate_low, gate_low_t, up_low, up_low_t = gated_backward(
        [grad_left, after(grad_right, order)], down_weight, gate, up
    )
    inner_sum = Sum([gate_low_t, up_low_t], [hidden_in], LONG)
    order = inner_sum.send(0)
    order = wide_sum.join(order)
    lines_low, lines_low_t, bias_grad = attend_backward(
        query,
        key,
        value,
        [grad_left, after(grad_right, order)],
        out_wide,
        logsum,
        tables,
        seg_col,
        seg_row,
        heads,
    )
    bias_grad = bias_grad[0].reshape(3, padded)[:, :width]
    outer_sum = Sum([lines_low_t], [hidden_in], LONG)
    term = merge([gate_low, up_low, lines_low], [gate_weight, up_weight, projection])
    order = wide_sum.total(term)
    order = inner_sum.join(order)
    order = wide_sum.share(order)
    order = outer_sum.send(0, order)
    merged = merge([after(context, order), mixed], [out_wide, down_weight])
    old = wide_sum.place_early(merged)
    down_grad, out_grad = wide_sum.place_last(old)
    order = inner_sum.total(down_grad)
    order = outer_sum.join(order)
    order = inner_sum.share(order)
    order = outer_sum.total(order)
    order = outer_sum.share(order)
    normed_grad = lax.psum_scatter(term, "tp", scatter_dimension=0, tiled=True).astype(jnp.float32)
    sums = jnp.concatenate([jnp.sum(normed_grad * normed, axis=0), jnp.sum(normed_grad, axis=0)])
    merged = lax.psum_scatter(merged, "tp", scatter_dimension=0, tiled=True)
    merged = merged.astype(jnp.float32)
    output = (input_wide + jnp.where(live_mine, merged, 0.0)).astype(jnp.bfloat16)
    scaled = normed_grad * gain
    input_grad = inverse * (
        scaled
        - jnp.mean(scaled, axis=1, keepdims=True)
        - normed * jnp.mean(scaled * normed, axis=1, keepdims=True)
    )
    input_grad = input_grad + cotangent.astype(jnp.float32)
    inner_old = inner_sum.place_early(order, output, input_grad)
    outer_old = outer_sum.place_early(inner_old)
    sums = sum_everywhere(after(sums, outer_old), "tp")
    gate_grad, up_grad = inner_sum.place_last(inner_old, sums)
    sums = sum_everywhere(jnp.concatenate([sums, bias_grad.reshape(-1)]), "rows")
    (qkv_grad,) = outer_sum.place_last(outer_old, gate_grad)
    return (
        output,
        input_grad,
        sums[:features],
        sums[features : 2 * features],
        qkv_grad.reshape(3, padded, features)[:, :width],
        sums[2 * features :].reshape(3, width),
        out_grad[:width],
        gate_grad,
        up_grad,
        down_grad,
    )


def solution(mesh):
    placed = (
        P(("rows", "tp"), None),
        P(),
        P(),
        P(None, "tp", None),
        P(None, "tp"),
        P("tp", None),
        P("tp", None),
        P("tp", None),
        P("tp", None),
        P(("rows", "tp"), None),
        P("rows", None),
    )
    return jax.shard_map(
        per_device,
        mesh=mesh,
        in_specs=placed,
        out_specs=(
            P(("rows", "tp"), None),
            P(("rows", "tp"), None),
            P(),
            P(),
            P(None, "tp", None),
            P(None, "tp"),
            P("tp", None),
            P("tp", None),
            P("tp", None),
            P("tp", None),
        ),
        check_vma=False,
    )
```

```python
import functools
import jax
import jax.numpy as jnp
from jax import lax
from jax.experimental import pallas as pl
from jax.experimental.pallas import tpu as pltpu
from jax.sharding import PartitionSpec as P

HEAD = 64
ROT = 16
MASKED = -1e30
LONG = 1000
EPSILON = 1e-05
ROOM = 13 * 2**20
SMALL = 8 * 2**20
IN_VMEM = pl.BlockSpec(memory_space=pltpu.VMEM)
IN_SMEM = pl.BlockSpec(memory_space=pltpu.SMEM)


def dot_rows(a, b):
    return lax.dot_general(a, b, (((1,), (0,)), ((), ())), preferred_element_type=jnp.float32)


def dot_lanes(a, b):
    return lax.dot_general(a, b, (((1,), (1,)), ((), ())), preferred_element_type=jnp.float32)


def dot_tall(a, b):
    return lax.dot_general(a, b, (((0,), (0,)), ((), ())), preferred_element_type=jnp.float32)


def turn(values, tables, sign):
    half = ROT // 2
    width = values.shape[1]
    tables = [jnp.concatenate([part] * (width // 128), axis=1) for part in tables]
    up = pltpu.roll(values, width - half, 1)
    down = pltpu.roll(values, half, 1)
    return values * tables[0] + sign * (up * tables[1] + down * tables[2])


def of_head(head, shape):
    return lax.broadcasted_iota(jnp.int32, shape, 1) // HEAD == head


def over_blocks(row_len, block, body):
    longest = row_len // 2
    blocks = row_len // block
    if blocks <= 8:
        for index in range(blocks):
            first = index * block
            start = max(0, first + block - (longest + block))
            body(first, start, first + block - start)
    else:
        size = longest + block

        def step(index, carry):
            first = pl.multiple_of(index * block, block)
            start = pl.multiple_of(jnp.maximum(first - longest, 0), block)
            body(first, start, size)
            return carry

        lax.fori_loop(0, blocks, step, 0)


def mask_of(seg_col, seg_row, first, start, block, size):
    rows = first + lax.broadcasted_iota(jnp.int32, (block, size), 0)
    keys = start + lax.broadcasted_iota(jnp.int32, (block, size), 1)
    same = seg_col[pl.ds(first, block), 0:1] == seg_row[0:1, pl.ds(start, size)]
    return jnp.where(same & (keys <= rows), 0.0, MASKED)


def forward_kernel(
    heads,
    hidden_in,
    projection,
    shift,
    tables,
    seg_col,
    seg_row,
    query,
    key,
    value,
    context,
    context_t,
    logsum,
):
    row_len, width = query.shape
    block = 256
    scale = HEAD ** (-0.5)
    for first in range(0, row_len, block):
        here = slice(first, first + block)
        lines = dot_lanes(hidden_in[here, :], projection[...]) + shift[...]
        turning = [tables[part, here, :] for part in range(3)]
        asked = turn(lines[:, 0:width], turning, 1.0).astype(jnp.bfloat16)
        query[here, :] = asked * jnp.bfloat16(scale)
        key[here, :] = turn(lines[:, width : 2 * width], turning, 1.0).astype(jnp.bfloat16)
        value[here, :] = lines[:, 2 * width : 3 * width].astype(jnp.bfloat16)

    def one_block(first, start, size):
        bias = mask_of(seg_col, seg_row, first, start, block, size)
        here = query[pl.ds(first, block), :]
        keys = key[pl.ds(start, size), :]
        values = value[pl.ds(start, size), :]
        total = jnp.zeros((block, width), jnp.float32)
        lane = lax.broadcasted_iota(jnp.int32, (block, 128), 1)
        sums = jnp.zeros((block, 128), jnp.float32)
        for head in range(heads):
            mine = of_head(head, (block, width))
            scores = dot_lanes(jnp.where(mine, here, jnp.bfloat16(0)), keys) + bias
            highest = jnp.max(scores, axis=1, keepdims=True)
            raised = jnp.exp(scores - highest)
            amount = jnp.sum(raised, axis=1, keepdims=True)
            weights = (raised * (1.0 / amount)).astype(jnp.bfloat16)
            total = jnp.where(mine, dot_rows(weights, values), total)
            sums = jnp.where(lane == head, highest + jnp.log(amount), sums)
        context[pl.ds(first, block), :] = total.astype(jnp.bfloat16)
        context_t[:, pl.ds(first, block)] = total.T.astype(jnp.bfloat16)
        logsum[pl.ds(first, block), :] = sums

    over_blocks(row_len, block, one_block)


def attend_forward(hidden_in, projection, shift, tables, seg_col, seg_row, heads):
    row_len, width = hidden_in.shape[0], projection.shape[0] // 3
    low = jax.ShapeDtypeStruct((row_len, width), jnp.bfloat16)
    return pl.pallas_call(
        functools.partial(forward_kernel, heads),
        in_specs=[IN_VMEM] * 6,
        out_shape=(
            low,
            low,
            low,
            low,
            jax.ShapeDtypeStruct((width, row_len), jnp.bfloat16),
            jax.ShapeDtypeStruct((row_len, 128), jnp.float32),
        ),
        compiler_params=pltpu.CompilerParams(vmem_limit_bytes=ROOM + 4096 * row_len),
        cost_estimate=busy(8.5),
        name="attend_forward",
    )(hidden_in, projection, shift, tables, seg_col, seg_row)


def backward_kernel(
    heads,
    query,
    key,
    value,
    grad_left,
    grad_right,
    out_weight,
    logsum,
    tables,
    seg_col,
    seg_row,
    lines_low,
    lines_low_t,
    bias_grad,
    key_grad,
    value_grad,
):
    row_len, width = query.shape
    block = 256
    scale = HEAD ** (-0.5)
    half = grad_left.shape[1]
    key_grad[...] = jnp.zeros_like(key_grad)
    value_grad[...] = jnp.zeros_like(value_grad)
    bias_grad[...] = jnp.zeros_like(bias_grad)

    def put(part, first, grads):
        low = grads.astype(jnp.bfloat16)
        wide = low.astype(jnp.float32)
        columns = slice(part * width, (part + 1) * width)
        lines_low[pl.ds(first, block), columns] = low
        lines_low_t[columns, pl.ds(first, block)] = wide.T.astype(jnp.bfloat16)
        bias_grad[0:1, columns] += jnp.sum(wide, axis=0, keepdims=True)

    def one_block(first, start, size):
        bias = mask_of(seg_col, seg_row, first, start, block, size)
        here = query[pl.ds(first, block), :]
        here_rows = pl.ds(first, block)
        grad_here = dot_lanes(grad_left[here_rows, :], out_weight[:, 0:half])
        grad_here = grad_here + dot_lanes(grad_right[here_rows, :], out_weight[:, half:])
        grad_here = grad_here.astype(jnp.bfloat16)
        keys = key[pl.ds(start, size), :]
        values = value[pl.ds(start, size), :]
        sums = logsum[pl.ds(first, block), :]
        total = jnp.zeros((block, width), jnp.float32)
        for head in range(heads):
            mine = of_head(head, (block, width))
            asked = jnp.where(mine, here, jnp.bfloat16(0))
            pulled = jnp.where(mine, grad_here, jnp.bfloat16(0))
            scores = dot_lanes(asked, keys) + bias
            probs = jnp.exp(scores - sums[:, head : head + 1])
            prob_grad = dot_lanes(pulled, values)
            value_grad[pl.ds(start, size), :] += dot_tall(probs.astype(jnp.bfloat16), pulled)
            inner = jnp.sum(probs * prob_grad, axis=1, keepdims=True)
            score_low = (probs * (prob_grad - inner)).astype(jnp.bfloat16)
            total = jnp.where(mine, dot_rows(score_low, keys), total)
            key_grad[pl.ds(start, size), :] += dot_tall(score_low, asked)
        here_tables = [tables[part, pl.ds(first, block), :] for part in range(3)]
        put(0, first, turn(total * scale, here_tables, -1.0))

    over_blocks(row_len, block, one_block)
    for index in range(row_len // block):
        first = index * block
        here_tables = [tables[part, pl.ds(first, block), :] for part in range(3)]
        put(1, first, turn(key_grad[pl.ds(first, block), :], here_tables, -1.0))
        put(2, first, value_grad[pl.ds(first, block), :])


def attend_backward(
    query, key, value, grads, out_weight, logsum, tables, seg_col, seg_row, heads
):
    row_len, width = query.shape
    return pl.pallas_call(
        functools.partial(backward_kernel, heads),
        in_specs=[IN_VMEM] * 10,
        out_shape=(
            jax.ShapeDtypeStruct((row_len, 3 * width), jnp.bfloat16),
            jax.ShapeDtypeStruct((3 * width, row_len), jnp.bfloat16),
            jax.ShapeDtypeStruct((8, 3 * width), jnp.float32),
        ),
        scratch_shapes=[
            pltpu.VMEM((row_len, width), jnp.float32),
            pltpu.VMEM((row_len, width), jnp.float32),
        ],
        compiler_params=pltpu.CompilerParams(vmem_limit_bytes=ROOM + 4096 * row_len),
        cost_estimate=busy(13.3),
        name="attend_backward",
    )(query, key, value, *grads, out_weight, logsum, tables, seg_col, seg_row)


def layout(doc_lengths, row_len):
    ends = jnp.cumsum(doc_lengths[0])
    starts = ends - doc_lengths[0]
    places = jnp.arange(row_len, dtype=jnp.int32)
    segment = jnp.sum((places[:, None] >= ends[None, :]).astype(jnp.int32), axis=1)
    chosen = segment[:, None] == jnp.arange(ends.shape[0], dtype=jnp.int32)[None, :]
    first = jnp.sum(jnp.where(chosen, starts[None, :], 0), axis=1)
    return segment, places - first, segment < ends.shape[0] - 1


def turns(position):
    half = ROT // 2
    lane = lax.broadcasted_iota(jnp.int32, (position.shape[0], 128), 1) % HEAD
    freq = 10000.0 ** (-((lane % half).astype(jnp.float32) * (2.0 / ROT)))
    angle = position.astype(jnp.float32)[:, None] * freq
    cosine, sine = jnp.cos(angle), jnp.sin(angle)
    return jnp.stack(
        [
            jnp.where(lane < ROT, cosine, 1.0),
            jnp.where(lane < half, -sine, 0.0),
            jnp.where((lane >= half) & (lane < ROT), sine, 0.0),
        ]
    )


def busy(time):
    return pl.CostEstimate(flops=int(time * 1.5 * 10**9), bytes_accessed=0, transcendentals=0)


def blocks_of(tokens):
    return min(512, tokens)


def gated_kernel(hidden_in, gate_weight, up_weight, gate, up, mixed, mixed_t):
    gate_here = dot_lanes(gate_weight[...], hidden_in[...])
    up_here = dot_lanes(up_weight[...], hidden_in[...])
    gate[...] = gate_here
    up[...] = up_here
    total = gate_here * jax.nn.sigmoid(gate_here) * up_here
    mixed_t[...] = total.astype(jnp.bfloat16)
    mixed[...] = total.T.astype(jnp.bfloat16)


def gated_forward(hidden_in, gate_weight, up_weight):
    (tokens, features), units = hidden_in.shape, gate_weight.shape[0]
    block = blocks_of(tokens)
    tall = pl.BlockSpec((units, block), lambda step: (0, step))
    flat = pl.BlockSpec((block, units), lambda step: (step, 0))
    return pl.pallas_call(
        gated_kernel,
        grid=(tokens // block,),
        in_specs=[pl.BlockSpec((block, features), lambda step: (step, 0)), IN_VMEM, IN_VMEM],
        out_specs=[tall, tall, flat, tall],
        out_shape=[
            jax.ShapeDtypeStruct((units, tokens), jnp.float32),
            jax.ShapeDtypeStruct((units, tokens), jnp.float32),
            jax.ShapeDtypeStruct((tokens, units), jnp.bfloat16),
            jax.ShapeDtypeStruct((units, tokens), jnp.bfloat16),
        ],
        compiler_params=pltpu.CompilerParams(vmem_limit_bytes=ROOM),
        cost_estimate=busy(7.5),
        name="gated_forward",
    )(hidden_in, gate_weight, up_weight)


def gated_back_kernel(
    grad_left, grad_right, down_weight, gate, up, gate_low, gate_low_t, up_low, up_low_t
):
    half = grad_left.shape[1]
    mixed_grad = dot_lanes(down_weight[:, 0:half], grad_left[...])
    mixed_grad = mixed_grad + dot_lanes(down_weight[:, half:], grad_right[...])
    gate_here = gate[...]
    sigmoid = jax.nn.sigmoid(gate_here)
    pulled = mixed_grad * sigmoid
    gate_grad = pulled * up[...] * (1.0 + gate_here * (1.0 - sigmoid))
    up_grad = pulled * gate_here
    gate_low_t[...] = gate_grad.astype(jnp.bfloat16)
    up_low_t[...] = up_grad.astype(jnp.bfloat16)
    gate_low[...] = gate_grad.T.astype(jnp.bfloat16)
    up_low[...] = up_grad.T.astype(jnp.bfloat16)


def gated_backward(grads, down_weight, gate, up):
    (tokens, half), units = grads[0].shape, down_weight.shape[0]
    block = blocks_of(tokens)
    tall = pl.BlockSpec((units, block), lambda step: (0, step))
    flat = pl.BlockSpec((block, units), lambda step: (step, 0))
    wide = jax.ShapeDtypeStruct((tokens, units), jnp.bfloat16)
    long = jax.ShapeDtypeStruct((units, tokens), jnp.bfloat16)
    return pl.pallas_call(
        gated_back_kernel,
        grid=(tokens // block,),
        in_specs=[pl.BlockSpec((block, half), lambda step: (step, 0))] * 2 + [IN_VMEM, tall, tall],
        out_specs=[flat, tall, flat, tall],
        out_shape=[wide, long, wide, long],
        compiler_params=pltpu.CompilerParams(vmem_limit_bytes=ROOM),
        cost_estimate=busy(5.4),
        name="gated_backward",
    )(*grads, down_weight, gate, up)


def merge_kernel(count, *refs):
    total = dot_rows(refs[0][...], refs[count][...])
    for index in range(1, count):
        total = total + dot_rows(refs[index][...], refs[count + index][...])
    refs[2 * count][...] = total.astype(jnp.bfloat16)


def merge(lhs, weights):
    tokens, features, count = lhs[0].shape[0], weights[0].shape[1], len(lhs)
    block = min(256, tokens)
    return pl.pallas_call(
        functools.partial(merge_kernel, count),
        grid=(tokens // block,),
        in_specs=[
            *(pl.BlockSpec((block, part.shape[1]), lambda step: (step, 0)) for part in lhs),
            *([IN_VMEM] * count),
        ],
        out_specs=pl.BlockSpec((block, features), lambda step: (step, 0)),
        out_shape=jax.ShapeDtypeStruct((tokens, features), jnp.bfloat16),
        compiler_params=pltpu.CompilerParams(vmem_limit_bytes=SMALL),
        cost_estimate=busy(8),
        name="merge",
    )(*lhs, *weights)


def stacked(lhs, rhs, first, wide, keep):
    row = 0
    block = rhs[:, pl.ds(pl.multiple_of(first, 128), wide)]
    for part in lhs:
        keep(row, part.shape[0], dot_rows(part[...], block))
        row += part.shape[0]


def send_kernel(count, wide, order, *refs):
    lhs, rhs, outs = refs[:count], refs[count], refs[-2:]
    for half, out in enumerate(outs):

        def keep(row, rows, term, out=out):
            out[row : row + rows, :] = term.astype(jnp.bfloat16)

        stacked(lhs, rhs, order[half], wide, keep)


def join_kernel(count, parts, order, *refs):
    lhs, rhs, came = refs[:count], refs[count : count + parts], refs[count + parts : -5]
    outs, total = refs[-5:-1], refs[-1]
    for half in range(2):
        at, bit = 0, order[parts, half]
        for part in range(parts):
            here = came[2 * part + half]
            wide = here.shape[1]
            narrow = wide // 2

            def keep(row, rows, term, here=here, wide=wide):
                there = here[row : row + rows, :].astype(jnp.float32)
                total[row : row + rows, 0:wide] = (term + there).astype(jnp.bfloat16)

            stacked(lhs, rhs[part], order[part, half], wide, keep)
            for out, which in ((outs[2 * half], 1 - bit), (outs[2 * half + 1], bit)):
                columns = pl.ds(pl.multiple_of(which * narrow, narrow), narrow)
                out[:, at : at + narrow] = total[:, columns]
            at += narrow


def place_kernel(takes, olds, order, *refs):
    count = 1 + max(take[0] for take in takes)
    pieces, outs = refs[:count], refs[count + olds :]
    step = pl.program_id(0)
    for index, (which, row, column) in enumerate(takes):
        piece = pieces[which]

        @pl.when(step == index)
        def _(piece=piece, first=row, column=column):
            for out in outs:
                size, narrow = out.shape
                block = piece[first : first + size, column : column + narrow]
                out[...] = block.astype(jnp.float32)
                first += size


def place(pieces, takes, order, sizes, narrow, features, old):
    return pl.pallas_call(
        functools.partial(place_kernel, takes, len(old)),
        grid_spec=pltpu.PrefetchScalarGridSpec(
            num_scalar_prefetch=1,
            grid=(len(takes),),
            in_specs=[IN_VMEM] * len(pieces) + [pl.BlockSpec(memory_space=pl.ANY)] * len(old),
            out_specs=[
                pl.BlockSpec((size, narrow), lambda step, order: (0, order[step]))
                for size in sizes
            ],
        ),
        out_shape=[jax.ShapeDtypeStruct((size, features), jnp.float32) for size in sizes],
        input_output_aliases={1 + len(pieces) + index: index for index in range(len(old))},
        compiler_params=pltpu.CompilerParams(vmem_limit_bytes=SMALL),
        cost_estimate=busy(sum(sizes) * len(takes) * narrow / 300_000),
        name="place",
    )(jnp.stack(order).astype(jnp.int32), *pieces, *old)


def lay_kernel(where, *refs):
    mine, theirs, out, sems = refs[0:6], refs[6:12], refs[12], refs[13]
    for inner in (0, 1):

        @pl.when(where[5] == inner)
        def _(inner=inner):
            taken = (0, 1, 3 - inner, 5 - inner)
            copies = []
            for place, index in enumerate(taken):
                for side, pieces in enumerate((mine, theirs)):
                    core = where[4] if side == 0 else 1 - where[4]
                    target = out.at[where[place], core]
                    copies.append(
                        pltpu.make_async_copy(pieces[index], target, sems.at[place, side])
                    )
            for copy in copies:
                copy.start()
            for copy in copies:
                copy.wait()


def gather(values, ready):
    line = [(2 * i + c, 2 * (i ^ 1) + c) for i in range(4) for c in range(2)]
    middle = [(2 * i + c, 2 * j + c) for i, j in ((0, 0), (1, 2), (2, 1), (3, 3)) for c in range(2)]
    core = [(i, i ^ 1) for i in range(8)]
    me = lax.axis_index("tp")
    chip = me // 2

    def move(pieces, pairs):
        return lax.ppermute(pieces, "tp", pairs)

    near = move(values, line)
    across = move(values, middle)
    far = move(across, line)
    beyond = move(near, middle)
    beyond = after(beyond, ready)
    last = move(beyond, line)
    mine = [values, near, across, far, beyond, last]
    theirs = [move(pieces, core) for pieces in mine]
    low, inner = chip < 2, (chip == 1) | (chip == 2)
    where = [chip, chip ^ 1, 1 + low, 3 * low, me % 2, inner]
    where = jnp.stack([jnp.asarray(entry, jnp.int32) for entry in where])
    shard, features = values.shape
    out = pl.pallas_call(
        lay_kernel,
        in_specs=[IN_SMEM] + [pl.BlockSpec(memory_space=pl.ANY)] * 12,
        out_specs=pl.BlockSpec(memory_space=pl.ANY),
        out_shape=jax.ShapeDtypeStruct((4, 2, shard, features), values.dtype),
        scratch_shapes=[pltpu.SemaphoreType.DMA((4, 2))],
        compiler_params=pltpu.CompilerParams(vmem_limit_bytes=4 * 2**20),
        cost_estimate=busy(2),
        name="lay",
    )(where, *mine, *theirs)
    return out.reshape(8 * shard, features)


NEAR = [(0, 1), (1, 0), (2, 3), (3, 2)]
FAR = [(0, 2), (2, 0), (1, 3), (3, 1)]
PATHS = ((NEAR, FAR), (FAR, NEAR))


def after(value, *others):
    return lax.optimization_barrier((value, others))[0]


class Sum:
    def __init__(self, lhs, parts, time=0):
        row = lax.axis_index("rows")
        near, far = row % 2, row // 2
        self.bits = ((near, far), (far, near))
        self.lhs, self.parts, self.time = lhs, parts, time
        self.rows, self.sizes = sum(part.shape[0] for part in lhs), [part.shape[0] for part in lhs]
        self.came = []

    def first(self, part, half, bit):
        return part.shape[1] // 8 * (4 * half + 2 * bit)

    def piece(self, wide):
        return jax.ShapeDtypeStruct((self.rows, wide), jnp.bfloat16)

    def room(self):
        return pltpu.CompilerParams(vmem_limit_bytes=SMALL + 4096 * self.lhs[0].shape[1])

    def send(self, part, *earlier):
        rhs = self.parts[part]
        order = jnp.stack([self.first(rhs, half, 1 - self.bits[half][0]) for half in range(2)])
        wide = rhs.shape[1] // 4
        head = after(self.lhs[0], *earlier)
        sent = pl.pallas_call(
            functools.partial(send_kernel, len(self.lhs), wide),
            in_specs=[IN_SMEM] + [IN_VMEM] * (len(self.lhs) + 1),
            out_shape=[self.piece(wide)] * 2,
            compiler_params=self.room(),
            cost_estimate=busy(self.rows * wide / 131072),
            name="send_terms",
        )(order.astype(jnp.int32), head, *self.lhs[1:], rhs)
        self.came += [lax.ppermute(sent[half], "rows", PATHS[half][0]) for half in range(2)]
        return sent

    def join(self, *earlier):
        order = [[self.first(part, half, self.bits[half][0]) for half in range(2)] for part in self.parts]
        order.append([self.bits[0][1], self.bits[1][1]])
        wide = sum(part.shape[1] // 8 for part in self.parts)
        head = after(self.lhs[0], *earlier)
        outs = pl.pallas_call(
            functools.partial(join_kernel, len(self.lhs), len(self.parts)),
            in_specs=[IN_SMEM] + [IN_VMEM] * (len(self.lhs) + 3 * len(self.parts)),
            out_shape=[self.piece(wide)] * 4,
            scratch_shapes=[pltpu.VMEM((self.rows, 2 * wide), jnp.bfloat16)],
            compiler_params=self.room(),
            cost_estimate=busy(self.time if self.time else self.rows / 256),
            name="join_terms",
        )(jnp.array(order).astype(jnp.int32), head, *self.lhs[1:], *self.parts, *self.came)
        self.mine = [outs[1], outs[3]]
        self.came = [lax.ppermute(outs[2 * half], "rows", PATHS[half][1]) for half in range(2)]
        return outs

    def total(self, *earlier):
        mine = lax.optimization_barrier((*self.mine, *earlier))[:2]
        self.mine = [mine[half] + self.came[half] for half in range(2)]
        self.across = [lax.ppermute(self.mine[half], "rows", PATHS[half][1]) for half in range(2)]
        return self.mine

    def share(self, *earlier):
        mine = lax.optimization_barrier((*self.mine, *earlier))[:2]
        both = [jnp.concatenate([mine[half], self.across[half]]) for half in range(2)]
        self.last = [lax.ppermute(both[half], "rows", PATHS[half][0]) for half in range(2)]
        return both

    def place(self, pieces, kinds, old, *earlier):
        features = sum(part.shape[1] for part in self.parts)
        narrow = min(part.shape[1] // 8 for part in self.parts)
        takes, order = [], []
        for pair, places in enumerate(kinds):
            for half in range(2):
                a, b = self.bits[half]
                for index, (first, second) in enumerate(places):
                    block = 4 * half + 2 * jnp.abs(a - first) + jnp.abs(b - second)
                    for part in range(len(self.parts)):
                        takes.append((2 * pair + half, index * self.rows, part * narrow))
                        order.append(8 * part + block)
        pieces = lax.optimization_barrier((*pieces, *earlier))[: len(pieces)]
        return place(pieces, takes, order, self.sizes, narrow, features, old)

    def place_early(self, *earlier):
        pieces = [*self.mine, *self.across]
        return self.place(pieces, [[(0, 0)], [(0, 1)]], (), *earlier)

    def place_last(self, old, *earlier):
        return self.place(self.last, [[(1, 0), (1, 1)]], old, *earlier)


def sum_everywhere(values, axis):
    size, step = lax.axis_size(axis), 1
    while step < size:
        values = values + lax.ppermute(values, axis, [(i, i ^ step) for i in range(size)])
        step *= 2
    return values


def norm_kernel(
    place, lengths, values, gain, shift, cotangent, normed, inverse, hidden, left, right
):
    wide = values[...].astype(jnp.float32)
    centred = wide - jnp.mean(wide, axis=1, keepdims=True)
    spread = jnp.mean(centred * centred, axis=1, keepdims=True)
    scale = lax.rsqrt(spread + EPSILON)
    units = centred * scale
    normed[...] = units
    inverse[...] = jnp.broadcast_to(scale, inverse.shape)
    low = units * gain[...].astype(jnp.float32) + shift[...].astype(jnp.float32)
    hidden[...] = low.astype(jnp.bfloat16)
    alive = -place[0]
    for piece in range(lengths.shape[1] - 1):
        alive = alive + lengths[0, piece]
    rows = lax.broadcasted_iota(jnp.int32, wide.shape, 0)
    grads = jnp.where(rows < alive, cotangent[...].astype(jnp.float32), 0.0).astype(jnp.bfloat16)
    half = wide.shape[1] // 2
    left[...] = grads[:, 0:half]
    right[...] = grads[:, half:]


def norm(place, lengths, values, gain, shift, cotangent):
    shard, features = values.shape
    part = jax.ShapeDtypeStruct((shard, features // 2), jnp.bfloat16)
    return pl.pallas_call(
        norm_kernel,
        in_specs=[IN_SMEM] * 2 + [pl.BlockSpec()] * 4,
        out_shape=[
            jax.ShapeDtypeStruct((shard, features), jnp.float32),
            jax.ShapeDtypeStruct((shard, 128), jnp.float32),
            jax.ShapeDtypeStruct((shard, features), jnp.bfloat16),
            part,
            part,
        ],
        compiler_params=pltpu.CompilerParams(vmem_limit_bytes=SMALL),
        cost_estimate=busy(2),
        name="norm",
    )(place, lengths, values, gain[None], shift[None], cotangent)


def widen(weight, width):
    return jnp.pad(weight, ((0, 0), (0, width - weight.shape[1]), (0, 0)))


def per_device(
    block_input,
    norm_gain,
    norm_bias,
    qkv_weight,
    qkv_bias,
    out_weight,
    gate_weight,
    up_weight,
    down_weight,
    cotangent,
    doc_lengths,
):
    shard, features = block_input.shape
    group = lax.axis_size("tp")
    tokens = shard * group
    width = qkv_weight.shape[1]
    heads = width // HEAD
    padded = max(width, 128)
    me = lax.axis_index("tp")
    segment, position, live = layout(doc_lengths, tokens)
    first = me * shard
    normed, inverse, normed_low, left_mine, right_mine = norm(
        first[None].astype(jnp.int32), doc_lengths, block_input, norm_gain, norm_bias, cotangent
    )
    tables = turns(position)
    seg_col = jnp.broadcast_to(segment[:, None], (tokens, 128))
    seg_row = jnp.broadcast_to(segment[None, :], (8, tokens))
    hidden_in = lax.all_gather(normed_low, "tp", axis=0, tiled=True)
    if group == 8:
        grad_left = gather(left_mine, position)
        hidden_in = after(hidden_in, grad_left)
    else:
        grad_left = lax.all_gather(after(left_mine, hidden_in), "tp", axis=0, tiled=True)
    grad_right = lax.all_gather(after(right_mine, hidden_in), "tp", axis=0, tiled=True)
    inverse = inverse[:, 0:1]
    live_mine = lax.dynamic_slice_in_dim(live, first, shard)[:, None]
    input_wide = block_input.astype(jnp.float32)
    gain = norm_gain.astype(jnp.float32)
    projection = widen(qkv_weight, padded).reshape(3 * padded, features)
    shift_lines = widen(qkv_bias[..., None], padded).reshape(1, 3 * padded).astype(jnp.float32)
    out_wide = widen(out_weight[None], padded)[0]
    gate, up, mixed, mixed_t = gated_forward(hidden_in, gate_weight, up_weight)
    query, key, value, context, context_t, logsum = attend_forward(
        after(hidden_in, mixed), projection, shift_lines, tables, seg_col, seg_row, heads
    )
    wide_sum = Sum([mixed_t, context_t], [grad_left, grad_right])
    order = wide_sum.send(0)
    order = wide_sum.send(1, order)
    gate_low, gate_low_t, up_low, up_low_t = gated_backward(
        [grad_left, after(grad_right, order)], down_weight, gate, up
    )
    inner_sum = Sum([gate_low_t, up_low_t], [hidden_in], LONG)
    order = inner_sum.send(0)
    order = wide_sum.join(order)
    lines_low, lines_low_t, bias_grad = attend_backward(
        query,
        key,
        value,
        [grad_left, after(grad_right, order)],
        out_wide,
        logsum,
        tables,
        seg_col,
        seg_row,
        heads,
    )
    bias_grad = bias_grad[0].reshape(3, padded)[:, :width]
    outer_sum = Sum([lines_low_t], [hidden_in], LONG)
    term = merge([gate_low, up_low, lines_low], [gate_weight, up_weight, projection])
    order = wide_sum.total(term)
    order = inner_sum.join(order)
    order = wide_sum.share(order)
    order = outer_sum.send(0, order)
    merged = merge([after(context, order), mixed], [out_wide, down_weight])
    old = wide_sum.place_early(merged)
    down_grad, out_grad = wide_sum.place_last(old)
    order = inner_sum.total(down_grad)
    order = outer_sum.join(order)
    order = inner_sum.share(order)
    order = outer_sum.total(order)
    order = outer_sum.share(order)
    normed_grad = lax.psum_scatter(term, "tp", scatter_dimension=0, tiled=True).astype(jnp.float32)
    sums = jnp.concatenate([jnp.sum(normed_grad * normed, axis=0), jnp.sum(normed_grad, axis=0)])
    merged = lax.psum_scatter(merged, "tp", scatter_dimension=0, tiled=True)
    merged = merged.astype(jnp.float32)
    output = (input_wide + jnp.where(live_mine, merged, 0.0)).astype(jnp.bfloat16)
    scaled = normed_grad * gain
    input_grad = inverse * (
        scaled
        - jnp.mean(scaled, axis=1, keepdims=True)
        - normed * jnp.mean(scaled * normed, axis=1, keepdims=True)
    )
    input_grad = input_grad + cotangent.astype(jnp.float32)
    inner_old = inner_sum.place_early(order, output, input_grad)
    outer_old = outer_sum.place_early(inner_old)
    sums = sum_everywhere(after(sums, outer_old), "tp")
    gate_grad, up_grad = inner_sum.place_last(inner_old, sums)
    sums = sum_everywhere(jnp.concatenate([sums, bias_grad.reshape(-1)]), "rows")
    (qkv_grad,) = outer_sum.place_last(outer_old, gate_grad)
    return (
        output,
        input_grad,
        sums[:features],
        sums[features : 2 * features],
        qkv_grad.reshape(3, padded, features)[:, :width],
        sums[2 * features :].reshape(3, width),
        out_grad[:width],
        gate_grad,
        up_grad,
        down_grad,
    )


def solution(mesh):
    placed = (
        P(("rows", "tp"), None),
        P(),
        P(),
        P(None, "tp", None),
        P(None, "tp"),
        P("tp", None),
        P("tp", None),
        P("tp", None),
        P("tp", None),
        P(("rows", "tp"), None),
        P("rows", None),
    )
    return jax.shard_map(
        per_device,
        mesh=mesh,
        in_specs=placed,
        out_specs=(
            P(("rows", "tp"), None),
            P(("rows", "tp"), None),
            P(),
            P(),
            P(None, "tp", None),
            P(None, "tp"),
            P("tp", None),
            P("tp", None),
            P("tp", None),
            P("tp", None),
        ),
        check_vma=False,
    )
```
